32 devices in a mesh: row: 4 (over y, x), col: 8 (over z, core).
Axes of the slice: x: 2, y: 2, z: 4, core: 2. Of those that a mesh axis runs over, the one named last changes fastest.
Arguments:
- inputs: float32 [8, 1024, 2048], P('col', 'row'), may hold values from -6 to 6
- cotangent: float32 [8, 1024, 2048], P('col', 'row'), may hold values from -6 to 6
- image_starts: int32 [8, 2], P('col'), may hold values from 0 to 768, as said below
- owners: int32 [16], replicated, may hold values from 0 to 7, as said below
- query_master: float32 [4096, 3, 2048], P('col', None, 'row'), may hold values from -0.125 to 0.125
- query_first: float32 [4096, 3, 2048], P('col', None, 'row')
- query_second: float32 [4096, 3, 2048], P('col', None, 'row'), may hold values from 8192 to 32768
- output_master: float32 [4096, 2048], P('col', 'row'), may hold values from -1 to 1
- output_first: float32 [4096, 2048], P('col', 'row')
- output_second: float32 [4096, 2048], P('col', 'row'), may hold values from 128 to 512
- gate_master: float32 [4096, 2, 5632], P('col', None, 'row'), may hold values from -0.125 to 0.125
- gate_first: float32 [4096, 2, 5632], P('col', None, 'row')
- gate_second: float32 [4096, 2, 5632], P('col', None, 'row'), may hold values from 1024 to 4096
- down_master: float32 [4096, 5632], P('col', 'row'), may hold values from -0.078125 to 0.078125
- down_first: float32 [4096, 5632], P('col', 'row')
- down_second: float32 [4096, 5632], P('col', 'row'), may hold values from 2048 to 8192
- vector_master: float32 [4096, 7], P('col'), may hold values from -0.5 to 1.4
- vector_first: float32 [4096, 7], P('col')
- vector_second: float32 [4096, 7], P('col'), may hold values from 8192 to 32768
Outputs:
- layer_out: float32 [8, 1024, 2048], P('col', 'row')
- input_grad: float32 [8, 1024, 2048], P('col', 'row')
- query_master_new: float32 [4096, 3, 2048], P('col', None, 'row')
- query_first_new: float32 [4096, 3, 2048], P('col', None, 'row')
- query_second_new: float32 [4096, 3, 2048], P('col', None, 'row')
- output_master_new: float32 [4096, 2048], P('col', 'row')
- output_first_new: float32 [4096, 2048], P('col', 'row')
- output_second_new: float32 [4096, 2048], P('col', 'row')
- gate_master_new: float32 [4096, 2, 5632], P('col', None, 'row')
- gate_first_new: float32 [4096, 2, 5632], P('col', None, 'row')
- gate_second_new: float32 [4096, 2, 5632], P('col', None, 'row')
- down_master_new: float32 [4096, 5632], P('col', 'row')
- down_first_new: float32 [4096, 5632], P('col', 'row')
- down_second_new: float32 [4096, 5632], P('col', 'row')
- vector_master_new: float32 [4096, 7], P('col')
- vector_first_new: float32 [4096, 7], P('col')
- vector_second_new: float32 [4096, 7], P('col')
The draws below stay inside these ranges and needn't reach their ends.
Inputs may be any that keep to these rules, and one draw needn't show every extreme that they name: `image_starts`: in each sequence the 2 image blocks of 256 positions do not intersect; block k lies within positions k * 512 to (k + 1) * 512 - 1. `owners`: each index of col owns 1 to 4 blocks, and one owns exactly 4.
All inputs are finite; a program needn't handle non-finite values.
Results may differ from the reference program's by a relative error of at most 0.023.
Values may be sent and summed in bfloat16 or wider, within the bound.
No kernel may reach another device: no remote copies, remote signals or barrier semaphores. Data moves between devices by JAX's collectives and lax.ppermute only.
A program may use at most 256 MiB of HBM per device.

```python
import math
import jax
import jax.numpy as jnp
from jax import lax

D = 2048
HEADS = 32
HEAD_DIM = 64
FF = 5632
ROT = 16
SEQ = 1024
IMG = 256
NIMG = 2
BLK_COL = 2
STEP = 5
CAP = 4
SEQS = 8
TOKENS = 8192
NBLK = 16
DB = 128
SLOTS = 32
SLOT_ROWS = 4096


def first_moment(seed_key, shape_of, square):
    return math.sqrt(square) * jnp.clip(jax.random.normal(seed_key, shape_of, jnp.float32), -3.0, 3.0)


def second_moment(seed_key, shape_of, square):
    return square * jnp.exp(jax.random.uniform(seed_key, shape_of, jnp.float32, 0.0, math.log(4.0)))


def draw_image_starts(key, part):
    key = jax.random.fold_in(key, 1)
    region = SEQ // NIMG
    offsets = jax.random.randint(key, (SEQS, NIMG), 0, region - IMG + 1)
    starts = jnp.arange(NIMG, dtype=jnp.int32)[None, :] * region + offsets
    chosen = jax.random.randint(jax.random.fold_in(key, 2), (), 0, SEQS)
    is_chosen = jnp.arange(SEQS, dtype=jnp.int32)[:, None] == chosen
    first_column = jnp.arange(NIMG, dtype=jnp.int32)[None, :] == 0
    last_column = jnp.arange(NIMG, dtype=jnp.int32)[None, :] == NIMG - 1
    starts = jnp.where(is_chosen & first_column, 0, starts)
    starts = jnp.where(is_chosen & last_column, SEQ - IMG, starts)
    return starts.astype(jnp.int32)


def draw_owners(key, part):
    key = jax.random.fold_in(key, 2)
    device_order = jax.random.permutation(key, SEQS)
    bumps = jnp.array([BLK_COL, 1 - BLK_COL, -1, 1, -1], jnp.int32)
    counts = BLK_COL + jnp.zeros((SEQS,), jnp.int32).at[device_order[:5]].set(bumps)
    grouped = jnp.repeat(jnp.arange(SEQS, dtype=jnp.int32), counts, total_repeat_length=NBLK)
    mixing = jax.random.permutation(jax.random.fold_in(key, 7), NBLK)
    return grouped[mixing].astype(jnp.int32)


def draw_vector_master(key, part):
    key = jax.random.fold_in(key, 3)
    gains = jax.random.uniform(key, (SLOT_ROWS, 7), jnp.float32, 0.6, 1.4)
    shifts = jax.random.uniform(jax.random.fold_in(key, 1), (SLOT_ROWS, 7), jnp.float32, -0.5, 0.5)
    columns = jnp.arange(7, dtype=jnp.int32)
    is_gain = (columns == 0) | (columns == 2)
    return jnp.where(is_gain[None, :], gains, shifts)


def draw_query_first(key, part):
    key = jax.random.fold_in(key, 11)
    return first_moment(key, (SLOT_ROWS, 3, D), 1.0 * TOKENS)


def draw_query_second(key, part):
    key = jax.random.fold_in(key, 12)
    return second_moment(key, (SLOT_ROWS, 3, D), 1.0 * TOKENS)


def draw_output_first(key, part):
    key = jax.random.fold_in(key, 13)
    return first_moment(key, (SLOT_ROWS, D), 16.0 * TOKENS / SEQ)


def draw_output_second(key, part):
    key = jax.random.fold_in(key, 14)
    return second_moment(key, (SLOT_ROWS, D), 16.0 * TOKENS / SEQ)


def draw_gate_first(key, part):
    key = jax.random.fold_in(key, 15)
    return first_moment(key, (SLOT_ROWS, 2, FF), TOKENS / 8.0)


def draw_gate_second(key, part):
    key = jax.random.fold_in(key, 16)
    return second_moment(key, (SLOT_ROWS, 2, FF), TOKENS / 8.0)


def draw_down_first(key, part):
    key = jax.random.fold_in(key, 17)
    return first_moment(key, (SLOT_ROWS, FF), TOKENS / 4.0)


def draw_down_second(key, part):
    key = jax.random.fold_in(key, 18)
    return second_moment(key, (SLOT_ROWS, FF), TOKENS / 4.0)


def draw_vector_first(key, part):
    key = jax.random.fold_in(key, 19)
    return first_moment(key, (SLOT_ROWS, 7), 1.0 * TOKENS)


def draw_vector_second(key, part):
    key = jax.random.fold_in(key, 20)
    return second_moment(key, (SLOT_ROWS, 7), 1.0 * TOKENS)


def levels(rng, dims, pieces, low, top_value):
    factor_of, own = 1.0, jax.random.fold_in(rng, 6)
    for dim, parts in pieces:
        draws = jnp.exp(jax.random.uniform(jax.random.fold_in(own, dim), (parts,), jnp.float32, low / len(pieces), top_value / len(pieces)))
        factor_of = factor_of * jnp.repeat(draws, dims[dim] // parts).reshape([-1 if axis == dim else 1 for axis in range(len(dims))])
    return factor_of


def bell_draw(key, dims, scale, bound, split=(), held_as=jnp.bfloat16):
    values = scale * jax.random.normal(key, dims, jnp.float32)
    if split:
        values = values * levels(key, dims, split, -0.22, 0.18)
    return jnp.clip(values, -bound, bound).astype(held_as)


def setup_inputs(seed: int = 0) -> dict:
    splits = jax.random.split(jax.random.key(seed), 20)
    inputs = bell_draw(splits[0], (SEQS, SEQ, D), 1.0, 6.0, ((0, 8), (1, 4)), jnp.float32)
    cotangent = bell_draw(splits[1], (SEQS, SEQ, D), 1.0, 6.0, ((0, 8), (1, 4)), jnp.float32)
    image_starts = draw_image_starts(jax.random.fold_in(splits[19], 71), 0)
    owners = draw_owners(jax.random.fold_in(splits[19], 71), 0)
    query_master = bell_draw(splits[4], (SLOT_ROWS, 3, D), D ** -0.5, 0.125, ((0, 8), (2, 4)), jnp.float32)
    query_first = draw_query_first(jax.random.fold_in(splits[19], 71), 0)
    query_second = draw_query_second(jax.random.fold_in(splits[19], 71), 0)
    output_master = bell_draw(splits[7], (SLOT_ROWS, D), (D * 16 // SEQ) ** -0.5, 1.0, ((0, 8), (1, 4)), jnp.float32)
    output_first = draw_output_first(jax.random.fold_in(splits[19], 71), 0)
    output_second = draw_output_second(jax.random.fold_in(splits[19], 71), 0)
    gate_master = bell_draw(splits[10], (SLOT_ROWS, 2, FF), D ** -0.5, 0.125, ((0, 8), (2, 4)), jnp.float32)
    gate_first = draw_gate_first(jax.random.fold_in(splits[19], 71), 0)
    gate_second = draw_gate_second(jax.random.fold_in(splits[19], 71), 0)
    down_master = bell_draw(splits[13], (SLOT_ROWS, FF), FF ** -0.5, 0.078125, ((0, 8), (1, 4)), jnp.float32)
    down_first = draw_down_first(jax.random.fold_in(splits[19], 71), 0)
    down_second = draw_down_second(jax.random.fold_in(splits[19], 71), 0)
    vector_master = draw_vector_master(jax.random.fold_in(splits[19], 71), 0)
    vector_first = draw_vector_first(jax.random.fold_in(splits[19], 71), 0)
    vector_second = draw_vector_second(jax.random.fold_in(splits[19], 71), 0)
    return {"inputs": inputs, "cotangent": cotangent, "image_starts": image_starts, "owners": owners, "query_master": query_master, "query_first": query_first, "query_second": query_second, "output_master": output_master, "output_first": output_first, "output_second": output_second, "gate_master": gate_master, "gate_first": gate_first, "gate_second": gate_second, "down_master": down_master, "down_first": down_first, "down_second": down_second, "vector_master": vector_master, "vector_first": vector_first, "vector_second": vector_second}


NORM_EPSILON = 1e-05
ADAM_EPSILON = 1e-08
MOMENT_DECAY = 0.5
WEIGHT_DECAY = 0.1
ROTARY_BASE = 10000.0
MASKED_SCORE = -1e+30

@jax.custom_vjp
def low(v):
    return lax.optimization_barrier(v.astype(jnp.bfloat16)).astype(jnp.float32)

@jax.custom_vjp
def low_back(v):
    return v

def low_keep(v):
    return (low(v), None)

def low_pass(kept, grad):
    return (grad,)

def back_keep(v):
    return (v, None)

def back_low(kept, grad):
    return (low(grad),)
low.defvjp(low_keep, low_pass)
low_back.defvjp(back_keep, back_low)

def owner_slots(owners):
    block_count = owners.shape[0]
    block_order = jnp.arange(block_count, dtype=jnp.int32)
    before = (owners[:, None] == owners[None, :]) & (block_order[None, :] < block_order[:, None])
    return (owners * CAP + lax.optimization_barrier(jnp.sum(before.astype(jnp.int32), axis=1))).astype(jnp.int32)

def slot_sources(slot_of, slot_count):
    matches = slot_of[None, :] == jnp.arange(slot_count, dtype=jnp.int32)[:, None]
    filled = jnp.any(matches, axis=1)
    numbers = jnp.arange(slot_of.shape[0], dtype=jnp.int32)
    source = lax.optimization_barrier(jnp.sum(jnp.where(matches, numbers[None, :], 0), axis=1)).astype(jnp.int32)
    return (source, filled)

def unpack(master, slot_of):
    shaped = master.reshape((SLOTS, DB) + master.shape[1:])
    return jnp.take(shaped, slot_of, axis=0).reshape((D,) + master.shape[1:])

def pack(gradient, source, filled):
    shaped = gradient.reshape((NBLK, DB) + gradient.shape[1:])
    picked = jnp.take(shaped, source, axis=0)
    slot_mask = filled.reshape((SLOTS,) + (1,) * (picked.ndim - 1))
    return jnp.where(slot_mask, picked, jnp.zeros_like(picked)).reshape((SLOT_ROWS,) + gradient.shape[1:])

def normalize(values):
    center = lax.optimization_barrier(jnp.mean(values, axis=-1, keepdims=True))
    spread = lax.optimization_barrier(jnp.mean(values * values, axis=-1, keepdims=True)) - center * center
    return (values - center) * lax.rsqrt(spread + NORM_EPSILON)

def rotary_tables():
    half_rot = ROT // 2
    frequency = ROTARY_BASE ** (-2.0 * jnp.arange(half_rot, dtype=jnp.float32) / ROT)
    angles = jnp.arange(SEQ, dtype=jnp.float32)[:, None] * frequency[None, :]
    return (jnp.cos(angles), jnp.sin(angles))

def rotate(values, cosine_table, sine_table):
    half_rot = ROT // 2
    first_half = values[..., :half_rot]
    second_half = values[..., half_rot:ROT]
    cosine_part = cosine_table[:, None, :]
    sine_part = sine_table[:, None, :]
    return jnp.concatenate([first_half * cosine_part - second_half * sine_part, second_half * cosine_part + first_half * sine_part, values[..., ROT:]], axis=-1)

def block_ids(starts):
    positions = jnp.arange(SEQ, dtype=jnp.int32)
    inside = (positions[None, :] >= starts[:, None]) & (positions[None, :] < starts[:, None] + IMG)
    numbers = jnp.arange(1, starts.shape[0] + 1, dtype=jnp.int32)
    return lax.optimization_barrier(jnp.sum(jnp.where(inside, numbers[:, None], 0), axis=0)).astype(jnp.int32)

def attention(queries, key_rows, value_rows, labels):
    positions = jnp.arange(SEQ, dtype=jnp.int32)
    block_size = min(512, SEQ)
    score_scale = 1.0 / math.sqrt(HEAD_DIM)

    def one_block(block_index):
        first_row = block_index * block_size
        query_rows = lax.dynamic_slice_in_dim(queries, first_row, block_size, 0)
        row_pos = first_row + jnp.arange(block_size, dtype=jnp.int32)
        row_label = lax.dynamic_slice_in_dim(labels, first_row, block_size, 0)
        scores = low_back(jnp.einsum('qhe,khe->hqk', query_rows, key_rows, precision=lax.Precision.HIGHEST) * score_scale)
        allowed = (positions[None, :] <= row_pos[:, None]) | (row_label[:, None] == labels[None, :]) & (row_label[:, None] > 0)
        scores = jnp.where(allowed[None], scores, MASKED_SCORE)
        weights = jax.nn.softmax(scores, axis=-1)
        return jnp.einsum('hqk,khe->qhe', low(weights), value_rows, precision=lax.Precision.HIGHEST)
    block_outs = lax.map(jax.checkpoint(one_block), jnp.arange(SEQ // block_size, dtype=jnp.int32))
    return block_outs.reshape(SEQ, HEADS, HEAD_DIM)

def layer(sequence, starts, weights, cosine_table, sine_table):
    w_query, w_output, w_gate, w_down, vectors = weights
    labels = block_ids(starts)
    normed_one = low(normalize(sequence) * vectors[:, 0] + vectors[:, 1])
    mixed_proj = low_back(jnp.einsum('td,djh->tjh', normed_one, w_query, precision=lax.Precision.HIGHEST) + vectors[:, 4:7].T[None])
    queries = low(rotate(mixed_proj[:, 0].reshape(SEQ, HEADS, HEAD_DIM), cosine_table, sine_table))
    key_rows = low(rotate(mixed_proj[:, 1].reshape(SEQ, HEADS, HEAD_DIM), cosine_table, sine_table))
    value_rows = low(mixed_proj[:, 2].reshape(SEQ, HEADS, HEAD_DIM))
    attended = low_back(low(attention(queries, key_rows, value_rows, labels).reshape(SEQ, D)))
    branch = low_back(jnp.einsum('th,dh->td', attended, w_output, precision=lax.Precision.HIGHEST))
    middle = sequence + branch
    normed_two = low(normalize(middle) * vectors[:, 2] + vectors[:, 3])
    gate_up = low_back(jnp.einsum('td,djf->tjf', normed_two, w_gate, precision=lax.Precision.HIGHEST))
    hidden = low(jax.nn.silu(gate_up[:, 0]) * gate_up[:, 1])
    return middle + low_back(jnp.einsum('tf,df->td', hidden, w_down, precision=lax.Precision.HIGHEST))

def adam_step(master, first_state, second_state, gradient, keep_rows, rate):
    new_first = MOMENT_DECAY * first_state + (1.0 - MOMENT_DECAY) * gradient
    new_second = MOMENT_DECAY * second_state + (1.0 - MOMENT_DECAY) * gradient * gradient
    correction = 1.0 - MOMENT_DECAY ** STEP
    direction = new_first / correction / (jnp.sqrt(new_second / correction) + ADAM_EPSILON)
    new_master = master - rate * (direction + WEIGHT_DECAY * master)
    keep_mask = keep_rows.reshape(keep_rows.shape + (1,) * (master.ndim - 1))
    return (jnp.where(keep_mask, new_master, master), jnp.where(keep_mask, new_first, first_state), jnp.where(keep_mask, new_second, second_state))

def step_rates():
    return (2.0 / math.sqrt(D), 2.0 / math.sqrt(D * 16 // SEQ), 2.0 / math.sqrt(D), 2.0 / math.sqrt(FF), 0.5)

def reference(inputs, cotangent, image_starts, owners, query_master, query_first, query_second, output_master, output_first, output_second, gate_master, gate_first, gate_second, down_master, down_first, down_second, vector_master, vector_first, vector_second):
    slot_of = owner_slots(owners)
    source, filled = slot_sources(slot_of, SLOTS)
    masters = (query_master, output_master, gate_master, down_master, vector_master)
    unpacked = tuple((unpack(master, slot_of) for master in masters))
    cosine_table, sine_table = rotary_tables()

    def forward(layer_inputs, weights):
        rounded = tuple((low(weight) for weight in weights))

        def one_sequence(running, paired):
            return (running, jax.checkpoint(layer)(paired[0], paired[1], rounded, cosine_table, sine_table))
        unused, outputs = lax.scan(one_sequence, jnp.zeros((), jnp.float32), (layer_inputs, image_starts))
        return outputs
    layer_out, pullback = jax.vjp(forward, inputs, unpacked)
    input_grad, weight_grads = pullback(cotangent)
    keep_rows = jnp.repeat(filled, DB)
    firsts = (query_first, output_first, gate_first, down_first, vector_first)
    seconds = (query_second, output_second, gate_second, down_second, vector_second)
    rates = step_rates()
    updated = []
    for kind_index in range(5):
        packed = pack(weight_grads[kind_index], source, filled)
        updated.append(adam_step(masters[kind_index], firsts[kind_index], seconds[kind_index], packed, keep_rows, rates[kind_index]))
    return (layer_out, input_grad, updated[0][0], updated[0][1], updated[0][2], updated[1][0], updated[1][1], updated[1][2], updated[2][0], updated[2][1], updated[2][2], updated[3][0], updated[3][1], updated[3][2], updated[4][0], updated[4][1], updated[4][2])
```

```python
import math

import jax
import jax.numpy as jnp
import numpy as np
from jax import lax
from jax.experimental import pallas as pl
from jax.experimental.layout import Layout, with_layout_constraint
from jax.experimental.pallas import tpu as pltpu
from jax.sharding import PartitionSpec as P

D = 2048
HEAD_DIM = 64
FF = 5632
ROT = 16
SEQ = 1024
IMG = 256
STEP = 5
CAP = 4

LANES = 128
MIB = 1 << 20

NORM_EPSILON = 1e-05
ADAM_EPSILON = 1e-08
MOMENT_DECAY = 0.5
WEIGHT_DECAY = 0.1
ROTARY_BASE = 10000.0
MASKED_SCORE = -1e30


def owner_slots(owners):
    block_count = owners.shape[0]
    block_order = jnp.arange(block_count, dtype=jnp.int32)
    before = (owners[:, None] == owners[None, :]) & (block_order[None, :] < block_order[:, None])
    return owners * CAP + jnp.sum(before.astype(jnp.int32), axis=1)


def slot_sources(slot_of, slot_count):
    matches = slot_of[None, :] == jnp.arange(slot_count, dtype=jnp.int32)[:, None]
    filled = jnp.any(matches, axis=1)
    numbers = jnp.arange(slot_of.shape[0], dtype=jnp.int32)
    source = jnp.sum(jnp.where(matches, numbers[None, :], 0), axis=1)
    return (source, filled)


def unpack(gathered, slot_of, block_rows):
    shaped = gathered.reshape((-1, block_rows) + gathered.shape[1:])
    return jnp.take(shaped, slot_of, axis=0).reshape((-1,) + gathered.shape[1:])


def own_blocks(gradient, own_source, block_rows):
    shaped = gradient.reshape((-1, block_rows) + gradient.shape[1:])
    return jnp.take(shaped, own_source, axis=0).reshape((-1,) + gradient.shape[1:])


def normalize(values):
    center = jnp.mean(values, axis=-1, keepdims=True)
    spread = jnp.mean(values * values, axis=-1, keepdims=True) - center * center
    inverse = lax.rsqrt(spread + NORM_EPSILON)
    return ((values - center) * inverse, inverse)


def norm_back(upstream, plain_rows, inverse, gain_row):
    scaled = upstream * gain_row
    return inverse * (
        scaled
        - jnp.mean(scaled, axis=-1, keepdims=True)
        - plain_rows * jnp.mean(scaled * plain_rows, axis=-1, keepdims=True)
    )


def rotary_tables(seq_len):
    half_rot = ROT // 2
    frequency = ROTARY_BASE ** (-2.0 * jnp.arange(half_rot, dtype=jnp.float32) / ROT)
    angles = jnp.arange(seq_len, dtype=jnp.float32)[:, None] * frequency[None, :]
    return (jnp.cos(angles), jnp.sin(angles))


def rotate(values, cosine_table, sine_table):
    half_rot = ROT // 2
    first_half = values[..., :half_rot]
    second_half = values[..., half_rot:ROT]
    cosine_part = cosine_table[:, None, :]
    sine_part = sine_table[:, None, :]
    return jnp.concatenate(
        [
            first_half * cosine_part - second_half * sine_part,
            second_half * cosine_part + first_half * sine_part,
            values[..., ROT:],
        ],
        axis=-1,
    )


def rotate_back(values, cosine_table, sine_table):
    half_rot = ROT // 2
    first_half = values[..., :half_rot]
    second_half = values[..., half_rot:ROT]
    cosine_part = cosine_table[:, None, :]
    sine_part = sine_table[:, None, :]
    return jnp.concatenate(
        [
            first_half * cosine_part + second_half * sine_part,
            second_half * cosine_part - first_half * sine_part,
            values[..., ROT:],
        ],
        axis=-1,
    )


def block_ids(starts, seq_len):
    positions = jnp.arange(seq_len, dtype=jnp.int32)
    inside = (positions[None, :] >= starts[:, None]) & (positions[None, :] < starts[:, None] + IMG)
    numbers = jnp.arange(1, starts.shape[0] + 1, dtype=jnp.int32)
    return jnp.sum(jnp.where(inside, numbers[:, None], 0), axis=0)


def adam_step(master, first_state, second_state, gradient, keep_rows, rate):
    new_first = MOMENT_DECAY * first_state + (1.0 - MOMENT_DECAY) * gradient
    new_second = MOMENT_DECAY * second_state + (1.0 - MOMENT_DECAY) * gradient * gradient
    correction = 1.0 - MOMENT_DECAY**STEP
    direction = new_first / correction / (jnp.sqrt(new_second / correction) + ADAM_EPSILON)
    new_master = master - rate * (direction + WEIGHT_DECAY * master)
    keep_mask = keep_rows.reshape(keep_rows.shape + (1,) * (master.ndim - 1))
    return (
        jnp.where(keep_mask, new_master, master),
        jnp.where(keep_mask, new_first, first_state),
        jnp.where(keep_mask, new_second, second_state),
    )


def step_rates():
    return (
        2.0 / math.sqrt(D),
        2.0 / math.sqrt(D * 16 // SEQ),
        2.0 / math.sqrt(D),
        2.0 / math.sqrt(FF),
        0.5,
    )


def local(
    inputs,
    cotangent,
    image_starts,
    owners,
    query_master,
    query_first,
    query_second,
    output_master,
    output_first,
    output_second,
    gate_master,
    gate_first,
    gate_second,
    down_master,
    down_first,
    down_second,
    vector_master,
    vector_first,
    vector_second,
):
    columns = lax.axis_size("col")
    col_index = lax.axis_index("col")
    row_index = lax.axis_index("row")
    block_rows = D // owners.shape[0]
    slot_of = owner_slots(owners)
    source, filled = slot_sources(slot_of, CAP * columns)
    shared = (
        lax.all_gather(query_master.astype(jnp.bfloat16), "col", axis=0, tiled=True),
        lax.all_gather(output_master.astype(jnp.bfloat16), "col", axis=0, tiled=True),
        lax.all_gather(gate_master.astype(jnp.bfloat16), "col", axis=0, tiled=True),
        lax.all_gather(down_master.astype(jnp.bfloat16), "col", axis=0, tiled=True),
        lax.all_gather(vector_master.astype(jnp.bfloat16), "col", axis=0, tiled=True),
    )
    w_query = unpack(shared[0], slot_of, block_rows)
    w_output = unpack(shared[1], slot_of, block_rows)
    w_gate = unpack(shared[2], slot_of, block_rows)
    w_down = unpack(shared[3], slot_of, block_rows)
    vectors = unpack(shared[4], slot_of, block_rows).astype(jnp.float32)
    local_in = inputs[0]
    width = local_in.shape[1]
    head_cols = w_query.shape[2]
    local_heads = head_cols // HEAD_DIM
    score_scale = 1.0 / math.sqrt(HEAD_DIM)
    qkv_bias = lax.dynamic_slice_in_dim(vectors[:, 4:7], row_index * head_cols, head_cols, 0).T
    plain_one, inverse_one = normalize(local_in)
    normed_one = (plain_one * vectors[:, 0] + vectors[:, 1]).astype(jnp.bfloat16)
    rows_one = lax.all_gather(normed_one, "row", axis=0, tiled=True)
    seq_len = rows_one.shape[0]
    mixed_proj = (
        jnp.einsum("td,djh->tjh", rows_one, w_query, preferred_element_type=jnp.float32)
        + qkv_bias[None]
    )
    cosine_table, sine_table = rotary_tables(seq_len)
    queries = rotate(
        mixed_proj[:, 0].reshape(seq_len, local_heads, HEAD_DIM), cosine_table, sine_table
    ).astype(jnp.bfloat16)
    key_rows = rotate(
        mixed_proj[:, 1].reshape(seq_len, local_heads, HEAD_DIM), cosine_table, sine_table
    ).astype(jnp.bfloat16)
    value_rows = mixed_proj[:, 2].reshape(seq_len, local_heads, HEAD_DIM).astype(jnp.bfloat16)
    labels = block_ids(image_starts[0], seq_len)
    block_size = min(512, seq_len)
    block_count = seq_len // block_size
    positions = jnp.arange(seq_len, dtype=jnp.int32)

    def scores_at(first_row):
        row_pos = first_row + jnp.arange(block_size, dtype=jnp.int32)
        row_label = lax.dynamic_slice_in_dim(labels, first_row, block_size, 0)
        allowed = (positions[None, :] <= row_pos[:, None]) | (
            row_label[:, None] == labels[None, :]
        ) & (row_label[:, None] > 0)
        query_rows = lax.dynamic_slice_in_dim(queries, first_row, block_size, 0)
        raw_scores = (
            jnp.einsum("qhe,khe->hqk", query_rows, key_rows, preferred_element_type=jnp.float32)
            * score_scale
        )
        return (jnp.where(allowed[None], raw_scores, MASKED_SCORE), query_rows)

    def forward_block(block_index):
        scores, query_rows = scores_at(block_index * block_size)
        row_peak = jnp.max(scores, axis=-1, keepdims=True)
        powers = jnp.exp(scores - row_peak)
        row_total = jnp.sum(powers, axis=-1, keepdims=True)
        weights = (powers / row_total).astype(jnp.bfloat16)
        output = jnp.einsum("hqk,khe->qhe", weights, value_rows, preferred_element_type=jnp.float32)
        return (output, (row_peak + jnp.log(row_total))[..., 0])

    output_blocks, log_totals = lax.map(forward_block, jnp.arange(block_count, dtype=jnp.int32))
    attended = output_blocks.reshape(seq_len, head_cols).astype(jnp.bfloat16)
    picked_rows = attended
    middle = local_in + lax.psum_scatter(
        jnp.einsum("th,dh->td", picked_rows, w_output, preferred_element_type=jnp.float32),
        "row",
        scatter_dimension=0,
        tiled=True,
    )
    plain_two, inverse_two = normalize(middle)
    normed_two = (plain_two * vectors[:, 2] + vectors[:, 3]).astype(jnp.bfloat16)
    rows_two = lax.all_gather(normed_two, "row", axis=0, tiled=True)
    gate_up = jnp.einsum("td,djf->tjf", rows_two, w_gate, preferred_element_type=jnp.float32)
    gate_part = gate_up[:, 0]
    up_part = gate_up[:, 1]
    gate_sigmoid = jax.nn.sigmoid(gate_part)
    activated = gate_part * gate_sigmoid
    hidden = (activated * up_part).astype(jnp.bfloat16)
    picked_rows = hidden
    layer_out = middle + lax.psum_scatter(
        jnp.einsum("tf,df->td", picked_rows, w_down, preferred_element_type=jnp.float32).astype(
            jnp.bfloat16
        ),
        "row",
        scatter_dimension=0,
        tiled=True,
    ).astype(jnp.float32)
    upstream = cotangent[0]
    rows_grad = lax.all_gather(upstream.astype(jnp.bfloat16), "row", axis=0, tiled=True)
    hidden_grad = jnp.einsum("td,df->tf", rows_grad, w_down, preferred_element_type=jnp.float32)
    down_grad = jnp.einsum("tf,td->df", hidden, rows_grad, preferred_element_type=jnp.float32)
    gate_grad = hidden_grad * up_part * gate_sigmoid * (1.0 + gate_part * (1.0 - gate_sigmoid))
    up_grad = hidden_grad * activated
    gate_up_grad = jnp.stack([gate_grad, up_grad], axis=1).astype(jnp.bfloat16)
    gate_weight_grad = jnp.einsum(
        "td,tjf->djf", rows_two, gate_up_grad, preferred_element_type=jnp.float32
    )
    picked_rows = gate_up_grad
    normed_two_grad = lax.psum_scatter(
        jnp.einsum("tjf,djf->td", picked_rows, w_gate, preferred_element_type=jnp.float32),
        "row",
        scatter_dimension=0,
        tiled=True,
    )
    middle_grad = upstream + norm_back(normed_two_grad, plain_two, inverse_two, vectors[:, 2])
    rows_mid = lax.all_gather(middle_grad.astype(jnp.bfloat16), "row", axis=0, tiled=True)
    attended_grad = jnp.einsum(
        "td,dh->th", rows_mid, w_output, preferred_element_type=jnp.float32
    ).astype(jnp.bfloat16)
    output_grad = jnp.einsum("th,td->dh", attended, rows_mid, preferred_element_type=jnp.float32)
    head_grad = attended_grad.reshape(seq_len, local_heads, HEAD_DIM)

    def backward_block(running, block_index):
        key_total, value_total = running
        first_row = block_index * block_size
        scores, query_rows = scores_at(first_row)
        probabilities = jnp.exp(scores - log_totals[block_index][..., None])
        row_grad = lax.dynamic_slice_in_dim(head_grad, first_row, block_size, 0)
        prob_grad = jnp.einsum(
            "qhe,khe->hqk", row_grad, value_rows, preferred_element_type=jnp.float32
        )
        inner = jnp.sum(prob_grad * probabilities, axis=-1, keepdims=True)
        score_grad = (probabilities * (prob_grad - inner)).astype(jnp.bfloat16)
        query_grad = (
            jnp.einsum("hqk,khe->qhe", score_grad, key_rows, preferred_element_type=jnp.float32)
            * score_scale
        )
        key_total = (
            key_total
            + jnp.einsum("hqk,qhe->khe", score_grad, query_rows, preferred_element_type=jnp.float32)
            * score_scale
        )
        value_total = value_total + jnp.einsum(
            "hqk,qhe->khe",
            probabilities.astype(jnp.bfloat16),
            row_grad,
            preferred_element_type=jnp.float32,
        )
        return ((key_total, value_total), query_grad)

    empty_heads = jnp.zeros((seq_len, local_heads, HEAD_DIM), jnp.float32)
    (key_grad, value_grad), query_blocks = lax.scan(
        backward_block, (empty_heads, empty_heads), jnp.arange(block_count, dtype=jnp.int32)
    )
    query_grad = query_blocks.reshape(seq_len, local_heads, HEAD_DIM)
    mixed_grad = jnp.stack(
        [
            rotate_back(query_grad, cosine_table, sine_table).reshape(seq_len, head_cols),
            rotate_back(key_grad, cosine_table, sine_table).reshape(seq_len, head_cols),
            value_grad.reshape(seq_len, head_cols),
        ],
        axis=1,
    ).astype(jnp.bfloat16)
    bias_grad = jnp.sum(mixed_grad, axis=0, dtype=jnp.float32)
    query_weight_grad = jnp.einsum(
        "td,tjh->djh", rows_one, mixed_grad, preferred_element_type=jnp.float32
    )
    picked_rows = mixed_grad
    normed_one_grad = lax.psum_scatter(
        jnp.einsum("tjh,djh->td", picked_rows, w_query, preferred_element_type=jnp.float32).astype(
            jnp.bfloat16
        ),
        "row",
        scatter_dimension=0,
        tiled=True,
    ).astype(jnp.float32)
    input_grad = middle_grad + norm_back(normed_one_grad, plain_one, inverse_one, vectors[:, 0])
    norm_grads = jnp.stack(
        [
            jnp.sum(normed_one_grad * plain_one, axis=0),
            jnp.sum(normed_one_grad, axis=0),
            jnp.sum(normed_two_grad * plain_two, axis=0),
            jnp.sum(normed_two_grad, axis=0),
        ],
        axis=1,
    )
    placed = lax.dynamic_update_slice_in_dim(
        jnp.zeros((width, 3), jnp.float32), bias_grad.T, row_index * head_cols, 0
    )
    vector_grad = lax.psum(
        jnp.concatenate([norm_grads, placed], axis=1).astype(jnp.bfloat16), "row"
    )
    own_filled = lax.dynamic_slice_in_dim(filled, col_index * CAP, CAP, 0)
    own_source = lax.dynamic_slice_in_dim(source, col_index * CAP, CAP, 0)
    summed = (
        lax.psum(query_weight_grad.astype(jnp.bfloat16), "col").astype(jnp.float32),
        lax.psum(output_grad.astype(jnp.bfloat16), "col").astype(jnp.float32),
        lax.psum(gate_weight_grad.astype(jnp.bfloat16), "col").astype(jnp.float32),
        lax.psum(down_grad.astype(jnp.bfloat16), "col").astype(jnp.float32),
        lax.psum(vector_grad, "col").astype(jnp.float32),
    )
    owned_grads = tuple((own_blocks(whole_grad, own_source, block_rows) for whole_grad in summed))
    keep_rows = jnp.repeat(own_filled, block_rows)
    masters = (query_master, output_master, gate_master, down_master, vector_master)
    firsts = (query_first, output_first, gate_first, down_first, vector_first)
    seconds = (query_second, output_second, gate_second, down_second, vector_second)
    rates = step_rates()
    updated = [
        adam_step(
            masters[kind_index],
            firsts[kind_index],
            seconds[kind_index],
            owned_grads[kind_index],
            keep_rows,
            rates[kind_index],
        )
        for kind_index in range(5)
    ]
    return (
        layer_out[None],
        input_grad[None],
        updated[0][0],
        updated[0][1],
        updated[0][2],
        updated[1][0],
        updated[1][1],
        updated[1][2],
        updated[2][0],
        updated[2][1],
        updated[2][2],
        updated[3][0],
        updated[3][1],
        updated[3][2],
        updated[4][0],
        updated[4][1],
        updated[4][2],
    )


BF16 = jnp.bfloat16
F32 = jnp.float32


def smem():
    return pl.BlockSpec(memory_space=pltpu.SMEM)


def params(mib=32):
    return pltpu.CompilerParams(vmem_limit_bytes=mib * MIB)


def cost(flops, nbytes, powers=0):
    return pl.CostEstimate(flops=int(flops), bytes_accessed=int(nbytes), transcendentals=int(powers))


def lane_block(number):
    return pl.ds(pl.multiple_of(number * LANES, LANES), LANES)


def after(value, *others):
    return lax.optimization_barrier((value, *others))[0]


def pack_query(slabs):
    kinds, rows, width = slabs.shape
    block = rows // CAP

    def kernel(in_ref, out_ref):
        for kind in range(kinds):
            out_ref[0, :, kind * width : (kind + 1) * width] = in_ref[kind].astype(BF16)

    return pl.pallas_call(
        kernel,
        grid=(CAP,),
        in_specs=[pl.BlockSpec((kinds, block, width), lambda s: (0, s, 0))],
        out_specs=pl.BlockSpec((1, block, kinds * width), lambda s: (s, 0, 0)),
        out_shape=jax.ShapeDtypeStruct((CAP, block, kinds * width), BF16),
        compiler_params=params(),
        cost_estimate=cost(0, 6 * slabs.size),
        name="pack_query",
    )(slabs)


def pack_flat(name, master):
    rows, width = master.shape
    block = rows // CAP

    def kernel(in_ref, out_ref):
        out_ref[0] = in_ref[...].astype(BF16)

    return pl.pallas_call(
        kernel,
        grid=(CAP,),
        in_specs=[pl.BlockSpec((block, width), lambda s: (s, 0))],
        out_specs=pl.BlockSpec((1, block, width), lambda s: (s, 0, 0)),
        out_shape=jax.ShapeDtypeStruct((CAP, block, width), BF16),
        compiler_params=params(),
        cost_estimate=cost(0, 6 * rows * width),
        name=name,
    )(master)


def gate_lines(values):
    rows, kinds, width = values.shape
    split = with_layout_constraint(
        values.reshape(rows, kinds, width // LANES, LANES), Layout(major_to_minor=(0, 2, 1, 3))
    )
    return jnp.transpose(split, (0, 2, 1, 3)).reshape(rows * kinds * width // LANES, LANES)


def gate_unlines(lines, shape):
    rows, kinds, width = shape
    split = jnp.transpose(lines.reshape(rows, width // LANES, kinds, LANES), (0, 2, 1, 3))
    return with_layout_constraint(split, Layout(major_to_minor=(0, 2, 1, 3))).reshape(shape)


def pack_gate(lines, rows):
    block = rows // CAP
    tiles = lines.shape[0] // rows

    def kernel(in_ref, out_ref):
        for tile in range(tiles):
            out_ref[0, :, tile * LANES : (tile + 1) * LANES] = in_ref[
                pl.ds(tile, block, stride=tiles), :
            ].astype(BF16)

    return pl.pallas_call(
        kernel,
        grid=(CAP,),
        in_specs=[pl.BlockSpec((block * tiles, LANES), lambda s: (s, 0))],
        out_specs=pl.BlockSpec((1, block, tiles * LANES), lambda s: (s, 0, 0)),
        out_shape=jax.ShapeDtypeStruct((CAP, block, tiles * LANES), BF16),
        compiler_params=params(),
        cost_estimate=cost(0, 6 * lines.size),
        name="pack_gate",
    )(lines)


def pick_blocks(codes, first, count, sources):
    shape = sources[0].shape[1:]

    def kernel(code_ref, *refs):
        ins, out, sems = refs[: len(sources)], refs[-2], refs[-1]
        for place in range(count):
            code = code_ref[first + place]
            index = jnp.bitwise_and(code, 15)
            origin = lax.shift_right_logical(code, 4)
            for number, source in enumerate(ins):

                @pl.when(origin == number)
                def start(source=source, index=index, place=place):
                    pltpu.make_async_copy(source.at[index], out.at[place], sems.at[place]).start()

        for place in range(count):
            pltpu.make_async_copy(ins[0].at[0], out.at[place], sems.at[place]).wait()

    moved = count * shape[0] * shape[1]
    return pl.pallas_call(
        kernel,
        in_specs=[smem()] + [pl.BlockSpec(memory_space=pl.ANY)] * len(sources),
        out_specs=pl.BlockSpec(memory_space=pltpu.VMEM),
        out_shape=jax.ShapeDtypeStruct((count, *shape), BF16),
        scratch_shapes=[pltpu.SemaphoreType.DMA((count,))],
        compiler_params=params(16),
        cost_estimate=cost(0, 4 * moved),
        name="pick_blocks",
    )(codes, *sources)


def row_blocks(height, width, first=0):
    return pl.BlockSpec((height, width), lambda i: (i + first, 0))


def whole(height, width):
    return pl.BlockSpec((height, width), lambda i: (0, 0))


NORM_ROWS = 64


def statistics(values):
    center = jnp.mean(values, axis=-1, keepdims=True)
    spread = jnp.mean(values * values, axis=-1, keepdims=True) - center * center
    return center, lax.rsqrt(spread + NORM_EPSILON)


def order_grad(order, cotangent):
    rows, width = cotangent.shape

    def kernel(order_ref, in_ref, out_ref):
        for place in range(width // LANES):
            out_ref[:, place * LANES : (place + 1) * LANES] = in_ref[
                :, lane_block(order_ref[place])
            ].astype(BF16)

    return pl.pallas_call(
        kernel,
        grid=(rows // NORM_ROWS,),
        in_specs=[smem(), row_blocks(NORM_ROWS, width)],
        out_specs=row_blocks(NORM_ROWS, width),
        out_shape=jax.ShapeDtypeStruct((rows, width), BF16),
        compiler_params=params(16),
        cost_estimate=cost(0, 6 * rows * width),
        name="order_grad",
    )(order, cotangent)


def norm_one(order, inputs):
    rows, width = inputs.shape

    def kernel(order_ref, in_ref, out_ref):
        center, inverse = statistics(in_ref[...])
        for place in range(width // LANES):
            span = slice(place * LANES, (place + 1) * LANES)
            plain = (in_ref[:, lane_block(order_ref[place])] - center) * inverse
            out_ref[:, span] = plain.astype(BF16)

    return pl.pallas_call(
        kernel,
        grid=(rows // NORM_ROWS,),
        in_specs=[smem(), row_blocks(NORM_ROWS, width)],
        out_specs=row_blocks(NORM_ROWS, width),
        out_shape=jax.ShapeDtypeStruct((rows, width), BF16),
        compiler_params=params(16),
        cost_estimate=cost(0, 6 * rows * width),
        name="norm_one",
    )(order, inputs)


def scale_rows(plain, vectors):
    rows, width = plain.shape
    tile = 256

    def kernel(in_ref, vec_ref, out_ref):
        out_ref[...] = (in_ref[...].astype(F32) * vec_ref[0:1, :] + vec_ref[1:2, :]).astype(BF16)

    return pl.pallas_call(
        kernel,
        grid=(rows // tile,),
        in_specs=[row_blocks(tile, width), whole(8, width)],
        out_specs=row_blocks(tile, width),
        out_shape=jax.ShapeDtypeStruct((rows, width), BF16),
        compiler_params=params(16),
        cost_estimate=cost(0, 4 * rows * width),
        name="scale_rows",
    )(plain, vectors)


def norm_two(order, inputs, partial, vectors):
    rows, width = inputs.shape
    own, from_x, from_y = partial

    def kernel(order_ref, in_ref, own_ref, x_ref, y_ref, vec_ref, mid_ref, out_ref):
        for place in range(width // LANES):
            span = slice(place * LANES, (place + 1) * LANES)
            mid_ref[:, span] = (
                in_ref[:, lane_block(order_ref[place])]
                + own_ref[:, span].astype(F32)
                + x_ref[:, span].astype(F32)
                + y_ref[:, span].astype(F32)
            )
        middle = mid_ref[...]
        center, inverse = statistics(middle)
        plain = (middle - center) * inverse
        out_ref[...] = (plain * vec_ref[2:3, :] + vec_ref[3:4, :]).astype(BF16)

    spec = row_blocks(NORM_ROWS, width)
    return pl.pallas_call(
        kernel,
        grid=(rows // NORM_ROWS,),
        in_specs=[smem(), spec, spec, spec, spec, whole(8, width)],
        out_specs=[spec, spec],
        out_shape=[
            jax.ShapeDtypeStruct((rows, width), F32),
            jax.ShapeDtypeStruct((rows, width), BF16),
        ],
        compiler_params=params(16),
        cost_estimate=cost(0, 16 * rows * width),
        name="norm_two",
    )(order, inputs, own, from_x, from_y, vectors)


def finish_out(order, middle, partial):
    rows, width = middle.shape
    own, from_x, from_y = partial

    def kernel(order_ref, mid_ref, own_ref, x_ref, y_ref, out_ref):
        for place in range(width // LANES):
            span = slice(place * LANES, (place + 1) * LANES)
            out_ref[:, lane_block(order_ref[place])] = (
                mid_ref[:, span]
                + own_ref[:, span].astype(F32)
                + x_ref[:, span].astype(F32)
                + y_ref[:, span].astype(F32)
            )

    spec = row_blocks(NORM_ROWS, width)
    return pl.pallas_call(
        kernel,
        grid=(rows // NORM_ROWS,),
        in_specs=[smem(), spec, spec, spec, spec],
        out_specs=spec,
        out_shape=jax.ShapeDtypeStruct((rows, width), F32),
        compiler_params=params(16),
        cost_estimate=cost(0, 14 * rows * width),
        name="finish_out",
    )(order, middle, own, from_x, from_y)


def norm_pull(upstream, plain, inverse, gain):
    scaled = upstream * gain
    return inverse * (
        scaled
        - jnp.mean(scaled, axis=-1, keepdims=True)
        - plain * jnp.mean(scaled * plain, axis=-1, keepdims=True)
    )


def add_sums(sum_ref, upstream, plain):
    @pl.when(pl.program_id(0) == 0)
    def clear():
        sum_ref[...] = jnp.zeros_like(sum_ref)

    sum_ref[0:1, :] += jnp.sum(upstream * plain, axis=0, keepdims=True)
    sum_ref[1:2, :] += jnp.sum(upstream, axis=0, keepdims=True)


def norm_two_back(order, cotangent, middle, partial, vectors):
    rows, width = middle.shape
    own, from_x, from_y = partial

    def kernel(
        order_ref, cot_ref, mid_ref, own_ref, x_ref, y_ref, vec_ref, grad_ref, low_ref, sum_ref
    ):
        middle_rows = mid_ref[...]
        center, inverse = statistics(middle_rows)
        plain = (middle_rows - center) * inverse
        upstream = own_ref[...].astype(F32) + x_ref[...].astype(F32) + y_ref[...].astype(F32)
        add_sums(sum_ref, upstream, plain)
        grad_ref[...] = norm_pull(upstream, plain, inverse, vec_ref[2:3, :])
        for place in range(width // LANES):
            span = slice(place * LANES, (place + 1) * LANES)
            total = grad_ref[:, span] + cot_ref[:, lane_block(order_ref[place])]
            grad_ref[:, span] = total
            low_ref[:, span] = total.astype(BF16)

    spec = row_blocks(NORM_ROWS, width)
    return pl.pallas_call(
        kernel,
        grid=(rows // NORM_ROWS,),
        in_specs=[smem(), spec, spec, spec, spec, spec, whole(8, width)],
        out_specs=[spec, spec, whole(8, width)],
        out_shape=[
            jax.ShapeDtypeStruct((rows, width), F32),
            jax.ShapeDtypeStruct((rows, width), BF16),
            jax.ShapeDtypeStruct((8, width), F32),
        ],
        compiler_params=params(16),
        cost_estimate=cost(0, 20 * rows * width),
        name="norm_two_back",
    )(order, cotangent, middle, own, from_x, from_y, vectors)


def norm_one_back(order, inputs, middle_grad, partial, vectors):
    rows, width = inputs.shape
    own, from_x, from_y = partial

    def kernel(
        order_ref,
        in_ref,
        mid_ref,
        own_ref,
        x_ref,
        y_ref,
        vec_ref,
        out_ref,
        sum_ref,
        plain_ref,
        pull_ref,
    ):
        center, inverse = statistics(in_ref[...])
        for place in range(width // LANES):
            span = slice(place * LANES, (place + 1) * LANES)
            plain_ref[:, span] = (in_ref[:, lane_block(order_ref[place])] - center) * inverse
        plain = plain_ref[...]
        upstream = own_ref[...].astype(F32) + x_ref[...].astype(F32) + y_ref[...].astype(F32)
        add_sums(sum_ref, upstream, plain)
        pull_ref[...] = norm_pull(upstream, plain, inverse, vec_ref[0:1, :])
        for place in range(width // LANES):
            span = slice(place * LANES, (place + 1) * LANES)
            out_ref[:, lane_block(order_ref[place])] = mid_ref[:, span] + pull_ref[:, span]

    spec = row_blocks(NORM_ROWS, width)
    return pl.pallas_call(
        kernel,
        grid=(rows // NORM_ROWS,),
        in_specs=[smem(), spec, spec, spec, spec, spec, whole(8, width)],
        out_specs=[spec, whole(8, width)],
        out_shape=[
            jax.ShapeDtypeStruct((rows, width), F32),
            jax.ShapeDtypeStruct((8, width), F32),
        ],
        scratch_shapes=[pltpu.VMEM((NORM_ROWS, width), F32), pltpu.VMEM((NORM_ROWS, width), F32)],
        compiler_params=params(16),
        cost_estimate=cost(0, 18 * rows * width),
        name="norm_one_back",
    )(order, inputs, middle_grad, own, from_x, from_y, vectors)


def spread_vectors(sorted_slots, head_slots, gathered):
    places = sorted_slots.shape[0]
    heads = head_slots.shape[0]

    def kernel(sorted_ref, head_ref, in_ref, vec_ref, bias_ref):
        for place in range(places):
            vec_ref[:, place * LANES : (place + 1) * LANES] = in_ref[sorted_ref[place]].astype(F32)
        for place in range(heads):
            bias_ref[:, place * LANES : (place + 1) * LANES] = in_ref[head_ref[place]].astype(F32)

    return pl.pallas_call(
        kernel,
        in_specs=[smem(), smem(), pl.BlockSpec(memory_space=pltpu.VMEM)],
        out_shape=[
            jax.ShapeDtypeStruct((16, places * LANES), F32),
            jax.ShapeDtypeStruct((16, heads * LANES), F32),
        ],
        compiler_params=params(16),
        name="spread_vectors",
    )(sorted_slots, head_slots, gathered)


def place_vector_grads(head_places, sums_one, sums_two, bias_sums):
    heads = head_places.shape[0]

    def kernel(head_ref, one_ref, two_ref, bias_ref, out_ref):
        out_ref[0:2, :] = one_ref[0:2, :]
        out_ref[2:4, :] = two_ref[0:2, :]
        out_ref[4:8, :] = jnp.zeros((4, out_ref.shape[1]), F32)
        for place in range(heads):
            for kind in range(3):
                first = (kind * heads + place) * LANES
                out_ref[4 + kind : 5 + kind, lane_block(head_ref[place])] = bias_ref[
                    0:1, first : first + LANES
                ]

    return pl.pallas_call(
        kernel,
        in_specs=[smem()] + [pl.BlockSpec(memory_space=pltpu.VMEM)] * 3,
        out_shape=jax.ShapeDtypeStruct(sums_one.shape, F32),
        compiler_params=params(16),
        name="place_vector_grads",
    )(head_places, sums_one, sums_two, bias_sums)


def adam_vector(keep, home_places, states, gradient, rate):
    kinds, rows = states[0].shape
    block = rows // CAP

    def kernel(keep_ref, home_ref, m_ref, f_ref, s_ref, g_ref, mo_ref, fo_ref, so_ref):
        for slot in range(CAP):
            span = slice(slot * block, (slot + 1) * block)
            grad = g_ref[:, lane_block(home_ref[slot])][:kinds]
            mo_ref[:, span], fo_ref[:, span], so_ref[:, span] = adam_update(
                m_ref[:, span], f_ref[:, span], s_ref[:, span], grad, keep_ref[slot] > 0, rate
            )

    return pl.pallas_call(
        kernel,
        in_specs=[smem(), smem()] + [pl.BlockSpec(memory_space=pltpu.VMEM)] * 4,
        out_shape=[jax.ShapeDtypeStruct(states[0].shape, F32)] * 3,
        compiler_params=params(16),
        name="adam_vector",
    )(keep, home_places, *states, gradient)


def lane_tables(seq_len):
    half = ROT // 2
    frequency = (ROTARY_BASE ** (-2.0 * np.arange(half, dtype=np.float32) / ROT)).astype(np.float32)
    angles = np.arange(seq_len, dtype=np.float32)[:, None] * frequency[None, :]
    cosine = np.cos(angles).astype(np.float32)
    sine = np.sin(angles).astype(np.float32)
    rest = HEAD_DIM - ROT
    ones = np.ones((seq_len, rest), np.float32)
    none = np.zeros((seq_len, rest), np.float32)
    blank = np.zeros((seq_len, half), np.float32)
    keep = np.concatenate([cosine, cosine, ones], axis=1)
    lower = np.concatenate([-sine, blank, none], axis=1)
    upper = np.concatenate([blank, sine, none], axis=1)
    return tuple(jnp.asarray(np.concatenate([table, table], axis=1)) for table in (keep, lower, upper))


def turn(values, keep, lower, upper):
    half = ROT // 2
    return (
        values * keep
        + pltpu.roll(values, LANES - half, 1) * lower
        + pltpu.roll(values, half, 1) * upper
    )


def head_mask(rows, head):
    lanes = lax.broadcasted_iota(jnp.int32, (rows, LANES), 1)
    return (lanes // HEAD_DIM) == head


def dot_nt(left, right):
    return lax.dot_general(left, right, (((1,), (1,)), ((), ())), preferred_element_type=F32)


def dot_nn(left, right):
    return lax.dot_general(left, right, (((1,), (0,)), ((), ())), preferred_element_type=F32)


def fill_masks(starts_ref, mask_ref, region):
    for part in range(2):
        keys = part * region + lax.broadcasted_iota(jnp.int32, (region, region), 0)
        queries = part * region + lax.broadcasted_iota(jnp.int32, (region, region), 1)
        visible = keys <= queries
        for image in range(starts_ref.shape[1]):
            first = starts_ref[0, image]
            visible = visible | (
                (keys >= first)
                & (keys < first + IMG)
                & (queries >= first)
                & (queries < first + IMG)
            )
        mask_ref[part] = jnp.where(visible, 0.0, MASKED_SCORE)


def tile_scores(key_rows, query_tile, mask_ref, part, first, tile, region):
    scores = dot_nt(key_rows, query_tile)
    mask = mask_ref[part, :, first : first + tile]
    if part == 0:
        return scores + mask
    return jnp.concatenate([scores[:region], scores[region:] + mask], axis=0)


def attend(row, starts, mixed, bias, tables):
    seq_len = mixed.shape[0]
    width = mixed.shape[1] // 3
    pairs = width // LANES
    tile = seq_len // 4
    region = seq_len // 2
    scale = 1.0 / math.sqrt(HEAD_DIM)

    def kernel(
        row_ref,
        starts_ref,
        q_ref,
        k_ref,
        v_ref,
        qb_ref,
        kb_ref,
        vb_ref,
        keep_ref,
        lower_ref,
        upper_ref,
        out_ref,
        qo_ref,
        ko_ref,
        vo_ref,
        log_ref,
        mask_ref,
    ):
        @pl.when(pl.program_id(0) == 0)
        def masks():
            fill_masks(starts_ref, mask_ref, region)

        for number in range(4):
            place = slice(number * tile, (number + 1) * tile)
            origin = pl.ds(pl.multiple_of(jnp.bitwise_xor(row_ref[0], number) * tile, tile), tile)
            turns = (keep_ref[place, :], lower_ref[place, :], upper_ref[place, :])
            turned = turn(q_ref[origin, :] + qb_ref[4:5, :], *turns)
            qo_ref[place, :] = (turned.astype(BF16).astype(F32) * scale).astype(BF16)
            ko_ref[place, :] = turn(k_ref[origin, :] + kb_ref[5:6, :], *turns).astype(BF16)
            vo_ref[place, :] = (v_ref[origin, :] + vb_ref[6:7, :]).astype(BF16)
        value_columns = jnp.transpose(vo_ref[...])
        for number in range(4):
            part = number // 2
            seen = region * (part + 1)
            first = (number % 2) * tile
            outs = []
            for head in range(2):
                query_tile = jnp.where(
                    head_mask(tile, head),
                    qo_ref[number * tile : (number + 1) * tile, :],
                    jnp.zeros((), BF16),
                )
                scores = tile_scores(
                    ko_ref[:seen, :], query_tile, mask_ref, part, first, tile, region
                )
                peak = jnp.max(scores, axis=0, keepdims=True)
                powers = jnp.exp(scores - peak)
                total = jnp.sum(powers, axis=0, keepdims=True)
                log_ref[0, head : head + 1, number * tile : (number + 1) * tile] = peak + jnp.log(
                    total
                )
                mixed_values = dot_nn(
                    value_columns[head * HEAD_DIM : (head + 1) * HEAD_DIM, :seen],
                    powers.astype(BF16),
                )
                outs.append(mixed_values / total)
            place = pl.ds(pl.multiple_of(jnp.bitwise_xor(row_ref[0], number) * tile, tile), tile)
            out_ref[place, :] = jnp.transpose(jnp.concatenate(outs, axis=0)).astype(BF16)

    def columns(kind):
        return pl.BlockSpec((seq_len, LANES), lambda h: (0, kind * pairs + h))

    bias_block = pl.BlockSpec((8, LANES), lambda h: (0, h))
    table = pl.BlockSpec((seq_len, LANES), lambda h: (0, 0))
    low = jax.ShapeDtypeStruct((seq_len, width), BF16)
    return pl.pallas_call(
        kernel,
        grid=(pairs,),
        in_specs=[smem(), smem()]
        + [columns(0), columns(1), columns(2)]
        + [bias_block] * 3
        + [table] * 3,
        out_specs=[columns(0)] * 4 + [pl.BlockSpec((1, 8, seq_len), lambda h: (h, 0, 0))],
        out_shape=[low] * 4 + [jax.ShapeDtypeStruct((pairs, 8, seq_len), F32)],
        scratch_shapes=[pltpu.VMEM((2, region, region), F32)],
        compiler_params=params(40),
        cost_estimate=cost(
            3 * seq_len * seq_len * width * 4, 20 * seq_len * width, seq_len * seq_len * 2 * pairs
        ),
        name="attend",
    )(row, starts, mixed, mixed, mixed, bias, bias, bias, *tables)


def attend_back(row, starts, queries, keys, values, logs, outputs, grads, tables):
    seq_len, width = queries.shape
    pairs = width // LANES
    tile = seq_len // 4
    region = seq_len // 2
    scale = 1.0 / math.sqrt(HEAD_DIM)

    def kernel(
        row_ref,
        starts_ref,
        q_ref,
        k_ref,
        v_ref,
        log_ref,
        o_ref,
        g_ref,
        keep_ref,
        lower_ref,
        upper_ref,
        out_ref,
        sum_ref,
        mask_ref,
        dq_ref,
        dk_ref,
        dv_ref,
        low_ref,
        bias_ref,
    ):
        @pl.when((pl.program_id(0) == 0) & (pl.program_id(1) == 0))
        def masks():
            fill_masks(starts_ref, mask_ref, region)

        @pl.when(pl.program_id(1) == 0)
        def work():
            dk_ref[...] = jnp.zeros_like(dk_ref)
            dv_ref[...] = jnp.zeros_like(dv_ref)
            key_columns = jnp.transpose(k_ref[...])
            for number in range(4):
                part = number // 2
                seen = region * (part + 1)
                first = (number % 2) * tile
                span = slice(number * tile, (number + 1) * tile)
                origin = pl.ds(
                    pl.multiple_of(jnp.bitwise_xor(row_ref[0], number) * tile, tile), tile
                )
                grad_tile = g_ref[origin, :]
                products = jnp.transpose(grad_tile.astype(F32) * o_ref[origin, :].astype(F32))
                query_grads = []
                for head in range(2):
                    mine = head_mask(tile, head)
                    query_tile = jnp.where(mine, q_ref[span, :], jnp.zeros((), BF16))
                    head_grad = jnp.where(mine, grad_tile, jnp.zeros((), BF16))
                    inner = jnp.sum(
                        products[head * HEAD_DIM : (head + 1) * HEAD_DIM], axis=0, keepdims=True
                    )
                    scores = tile_scores(
                        k_ref[:seen, :], query_tile, mask_ref, part, first, tile, region
                    )
                    weights = jnp.exp(scores - log_ref[0, head : head + 1, span])
                    pulls = dot_nt(v_ref[:seen, :], head_grad)
                    score_grad = (weights * (pulls - inner)).astype(BF16)
                    dv_ref[:seen, :] += dot_nn(weights.astype(BF16), head_grad)
                    dk_ref[:seen, :] += dot_nn(score_grad, query_tile)
                    query_grads.append(
                        dot_nn(
                            key_columns[head * HEAD_DIM : (head + 1) * HEAD_DIM, :seen], score_grad
                        )
                    )
                dq_ref[span, :] = jnp.transpose(jnp.concatenate(query_grads, axis=0)) * scale
            bias_ref[...] = jnp.zeros_like(bias_ref)
            for number in range(4):
                span = slice(number * tile, (number + 1) * tile)
                origin = pl.ds(
                    pl.multiple_of(jnp.bitwise_xor(row_ref[0], number) * tile, tile), tile
                )
                turns = (keep_ref[span, :], -lower_ref[span, :], -upper_ref[span, :])
                parts = (
                    turn(dq_ref[span, :], *turns),
                    turn(dk_ref[span, :], *turns),
                    dv_ref[span, :],
                )
                for kind in range(3):
                    low = parts[kind].astype(BF16)
                    low_ref[kind, origin, :] = low
                    bias_ref[kind, 0:1, :] += jnp.sum(low.astype(F32), axis=0, keepdims=True)

        out_ref[...] = low_ref[pl.program_id(1)]
        sum_ref[...] = bias_ref[pl.program_id(1)]

    columns = pl.BlockSpec((seq_len, LANES), lambda h, j: (0, h))
    table = pl.BlockSpec((seq_len, LANES), lambda h, j: (0, 0))
    return pl.pallas_call(
        kernel,
        grid=(pairs, 3),
        in_specs=[smem(), smem()]
        + [columns] * 3
        + [pl.BlockSpec((1, 8, seq_len), lambda h, j: (h, 0, 0))]
        + [columns] * 2
        + [table] * 3,
        out_specs=[
            pl.BlockSpec((seq_len, LANES), lambda h, j: (0, j * pairs + h)),
            pl.BlockSpec((8, LANES), lambda h, j: (0, j * pairs + h)),
        ],
        out_shape=[
            jax.ShapeDtypeStruct((seq_len, 3 * width), BF16),
            jax.ShapeDtypeStruct((8, 3 * width), F32),
        ],
        scratch_shapes=[
            pltpu.VMEM((2, region, region), F32),
            pltpu.VMEM((seq_len, LANES), F32),
            pltpu.VMEM((seq_len, LANES), F32),
            pltpu.VMEM((seq_len, LANES), F32),
            pltpu.VMEM((3, seq_len, LANES), BF16),
            pltpu.VMEM((3, 8, LANES), F32),
        ],
        compiler_params=params(48),
        cost_estimate=cost(
            8 * seq_len * seq_len * width * 4, 20 * seq_len * width, seq_len * seq_len * 2 * pairs
        ),
        name="attend_back",
    )(row, starts, queries, keys, values, logs, outputs, grads, *tables)


def gate_up(rows_two, w_gate):
    tokens, width = rows_two.shape
    tiles = w_gate.shape[1] // (2 * LANES)

    def kernel(in_ref, w_ref, gate_ref, up_ref, hidden_ref):
        both = dot_nn(in_ref[...], w_ref[...])
        gate, up = both[:, :LANES], both[:, LANES:]
        gate_ref[...] = gate.astype(BF16)
        up_ref[...] = up.astype(BF16)
        hidden_ref[...] = (gate * jax.nn.sigmoid(gate) * up).astype(BF16)

    out = pl.BlockSpec((tokens, LANES), lambda i: (0, i))
    return pl.pallas_call(
        kernel,
        grid=(tiles,),
        in_specs=[whole(tokens, width), pl.BlockSpec((width, 2 * LANES), lambda i: (0, i))],
        out_specs=[out] * 3,
        out_shape=[jax.ShapeDtypeStruct((tokens, tiles * LANES), BF16)] * 3,
        compiler_params=params(40),
        cost_estimate=cost(
            2 * tokens * w_gate.size,
            2 * (rows_two.size + w_gate.size) + 6 * tokens * tiles * LANES,
            tokens * tiles * LANES,
        ),
        name="gate_up",
    )(rows_two, w_gate)


def gate_up_back(rows_grad, w_down, gate, up):
    tokens, width = rows_grad.shape
    hidden = w_down.shape[1]
    tile = 256

    def kernel(in_ref, w_ref, gate_ref, up_ref, out_ref):
        pulled = dot_nn(in_ref[...], w_ref[...])
        for number in range(hidden // LANES):
            span = slice(number * LANES, (number + 1) * LANES)
            grad = pulled[:, span]
            gate_part = gate_ref[:, span].astype(F32)
            up_part = up_ref[:, span].astype(F32)
            squash = jax.nn.sigmoid(gate_part)
            first = 2 * number * LANES
            out_ref[:, first : first + LANES] = (
                grad * up_part * squash * (1.0 + gate_part * (1.0 - squash))
            ).astype(BF16)
            out_ref[:, first + LANES : first + 2 * LANES] = (grad * gate_part * squash).astype(BF16)

    return pl.pallas_call(
        kernel,
        grid=(tokens // tile,),
        in_specs=[
            row_blocks(tile, width),
            whole(width, hidden),
            row_blocks(tile, hidden),
            row_blocks(tile, hidden),
        ],
        out_specs=row_blocks(tile, 2 * hidden),
        out_shape=jax.ShapeDtypeStruct((tokens, 2 * hidden), BF16),
        compiler_params=params(40),
        cost_estimate=cost(
            2 * tokens * w_down.size,
            2 * (rows_grad.size + w_down.size) + 8 * tokens * hidden,
            tokens * hidden,
        ),
        name="gate_up_back",
    )(rows_grad, w_down, gate, up)


def adam_update(master, first, second, gradient, keep, rate):
    correction = 1.0 - MOMENT_DECAY**STEP
    new_first = MOMENT_DECAY * first + (1.0 - MOMENT_DECAY) * gradient
    new_second = MOMENT_DECAY * second + (1.0 - MOMENT_DECAY) * gradient * gradient
    direction = new_first / correction / (jnp.sqrt(new_second / correction) + ADAM_EPSILON)
    new_master = master - rate * (direction + WEIGHT_DECAY * master)
    return (
        jnp.where(keep, new_master, master),
        jnp.where(keep, new_first, first),
        jnp.where(keep, new_second, second),
    )


def adam_call(name, keep, states, gradient, rate, grid, state_spec, grad_spec, pieces):
    def kernel(keep_ref, m_ref, f_ref, s_ref, g_ref, mo_ref, fo_ref, so_ref):
        live = keep_ref[pl.program_id(0)] > 0
        for state_at, grad_at in pieces:
            results = adam_update(
                m_ref[state_at],
                f_ref[state_at],
                s_ref[state_at],
                g_ref[grad_at].astype(F32),
                live,
                rate,
            )
            mo_ref[state_at], fo_ref[state_at], so_ref[state_at] = results

    return pl.pallas_call(
        kernel,
        grid=grid,
        in_specs=[smem()] + [state_spec] * 3 + [grad_spec],
        out_specs=[state_spec] * 3,
        out_shape=[jax.ShapeDtypeStruct(states[0].shape, F32)] * 3,
        compiler_params=params(40),
        cost_estimate=cost(12 * states[0].size, 26 * states[0].size, states[0].size),
        name=name,
    )(keep, *states, gradient)


def adam_query(keep, states, gradient, rate):
    kinds, rows, width = states[0].shape
    block = rows // CAP
    return adam_call(
        "adam_query",
        keep,
        states,
        gradient,
        rate,
        (CAP, kinds),
        pl.BlockSpec((1, block, width), lambda s, j: (j, s, 0)),
        pl.BlockSpec((1, block, width), lambda s, j: (s, 0, j)),
        [((0,), (0,))],
    )


def adam_flat(name, keep, states, gradient, rate):
    rows, width = states[0].shape
    block = rows // CAP
    return adam_call(
        name,
        keep,
        states,
        gradient,
        rate,
        (CAP,),
        pl.BlockSpec((block, width), lambda s: (s, 0)),
        pl.BlockSpec((1, block, width), lambda s: (s, 0, 0)),
        [((slice(None), slice(None)), (0,))],
    )


def adam_gate(keep, states, gradient, rate):
    block, width = gradient.shape[1:]
    tiles = width // LANES
    part = block // 2
    pieces = [
        (
            (pl.ds(tile, part, stride=tiles), slice(None)),
            (0, slice(None), slice(tile * LANES, (tile + 1) * LANES)),
        )
        for tile in range(tiles)
    ]
    return adam_call(
        "adam_gate",
        keep,
        states,
        gradient,
        rate,
        (CAP, 2),
        pl.BlockSpec((part * tiles, LANES), lambda s, i: (2 * s + i, 0)),
        pl.BlockSpec((1, part, width), lambda s, i: (s, i, 0)),
        pieces,
    )


def matmul(left, right, left_dim, right_dim, dtype):
    return lax.dot_general(
        left, right, (((left_dim,), (right_dim,)), ((), ())), preferred_element_type=F32
    ).astype(dtype)


def flips(axis, reach):
    return [(index, index ^ reach) for index in range(lax.axis_size(axis))]


def x_pairs():
    return flips("row", 1)


def y_pairs():
    return flips("row", 2)


def share_rows(own):
    half = own.shape[0] // 2
    by_x = lax.ppermute(own, "row", x_pairs())
    by_y = lax.ppermute(own, "row", y_pairs())
    top = lax.ppermute(by_x[:half], "row", y_pairs())
    bottom = lax.ppermute(by_y[half:], "row", x_pairs())
    return jnp.concatenate([own, by_x, by_y, top, bottom], axis=0), by_x, by_y


def scatter_rows(sums):
    rows = sums.shape[0] // 4
    half = rows // 2
    top = lax.ppermute(sums[3 * rows : 3 * rows + half], "row", y_pairs())
    bottom = lax.ppermute(sums[3 * rows + half :], "row", x_pairs())
    to_x = jnp.concatenate([sums[rows : rows + half] + top, sums[rows + half : 2 * rows]], axis=0)
    to_y = jnp.concatenate(
        [sums[2 * rows : 2 * rows + half], sums[2 * rows + half : 3 * rows] + bottom], axis=0
    )
    return (
        (sums, lax.ppermute(to_x, "row", x_pairs()), lax.ppermute(to_y, "row", y_pairs())),
        to_x,
        to_y,
    )


def chip_moves(columns, moves):
    chips = columns // 2
    return [
        (2 * chip + core, 2 * (chip + moves[core]) + core)
        for chip in range(chips)
        for core in range(2)
        if 0 <= chip + moves[core] < chips
    ]


def swap_cores(values, columns):
    return lax.ppermute(values, "col", [(index, index ^ 1) for index in range(columns)])


def both_cores(values, columns):
    return values, swap_cores(values, columns)


def local_line(
    inputs,
    cotangent,
    image_starts,
    owners,
    query_master,
    query_first,
    query_second,
    output_master,
    output_first,
    output_second,
    gate_master,
    gate_first,
    gate_second,
    down_master,
    down_first,
    down_second,
    vector_master,
    vector_first,
    vector_second,
):
    columns = lax.axis_size("col")
    col_index = lax.axis_index("col")
    row_index = lax.axis_index("row")
    blocks = owners.shape[0]
    block_rows = D // blocks
    chip, core = col_index // 2, col_index % 2

    slot_of = owner_slots(owners)
    numbers = jnp.arange(blocks, dtype=jnp.int32)
    place_of = jnp.sum((slot_of[None, :] < slot_of[:, None]).astype(jnp.int32), axis=1)
    at_place = place_of[None, :] == numbers[:, None]
    order = jnp.sum(jnp.where(at_place, numbers[None, :], 0), axis=1)
    sorted_slots = jnp.sum(jnp.where(at_place, slot_of[None, :], 0), axis=1)
    head_blocks = query_master.shape[2] // LANES
    head_slots = lax.dynamic_slice_in_dim(slot_of, row_index * head_blocks, head_blocks, 0)
    head_places = lax.dynamic_slice_in_dim(place_of, row_index * head_blocks, head_blocks, 0)

    def owned_below(index):
        return jnp.sum((owners < index).astype(jnp.int32))

    chip_first = owned_below(2 * chip)
    chip_middle = owned_below(2 * chip + 1)
    chip_end = owned_below(2 * chip + 2)
    own_first = owned_below(col_index)
    own_count = owned_below(col_index + 1) - own_first
    chip_numbers = jnp.arange(columns // 2, dtype=jnp.int32)
    below = jnp.sum((owners[None, :] < 2 * chip_numbers[:, None]).astype(jnp.int32), axis=1)
    uneven = jnp.max(jnp.abs(below - 4 * chip_numbers)) > 2

    def chip_code(place):
        owner_core = (place >= chip_middle).astype(jnp.int32)
        rank = place - jnp.where(owner_core > 0, chip_middle, chip_first)
        code = jnp.where(owner_core == core, 0, 16) + rank
        return jnp.where((place >= chip_first) & (place < chip_end), code, 0)

    pair = jnp.arange(2, dtype=jnp.int32)
    toward = jnp.where(core == 0, 1, -1)
    kept_place = 4 * chip + 2 * core + pair
    near_code = 32 + pair
    far_code = 48 + pair
    keep_codes = jnp.where(
        kept_place < chip_first,
        jnp.where(core == 0, near_code, far_code),
        jnp.where(
            kept_place >= chip_end,
            jnp.where(core == 0, far_code, near_code),
            chip_code(kept_place),
        ),
    )
    four = jnp.arange(CAP, dtype=jnp.int32)
    live = (four < own_count).astype(jnp.int32)
    home_places = own_first + jnp.minimum(four, own_count - 1)
    home_side = home_places // 4 - chip
    home_core = (home_places % 4) // 2
    near_side = jnp.where(home_core == 0, 1, -1)
    home_source = jnp.where(home_side == 0, 0, jnp.where(home_side == near_side, 1, 4))
    home_other = jnp.where(home_source == 4, 5, home_source + 2)
    codes = jnp.concatenate(
        [
            chip_code(4 * (chip + toward) + 2 * core + pair),
            chip_code(4 * (chip - toward) + 2 * core + pair),
            keep_codes,
            16 * jnp.where(home_core == core, home_source, home_other) + home_places % 2,
        ]
    )

    inward = chip_moves(columns, (1, -1))
    outward = chip_moves(columns, (-1, 1))

    def spread_out(own, send_codes, keep_codes):
        partner = swap_cores(own, columns)
        sent = pick_blocks(send_codes, 0, 2, [own, partner])
        near = lax.ppermute(sent, "col", inward)

        def farther():
            far = lax.ppermute(pick_blocks(codes, 2, 2, [own, partner]), "col", outward)
            return pick_blocks(keep_codes, 4, 2, [own, partner, near, far])

        kept = lax.cond(
            uneven, farther, lambda: pick_blocks(keep_codes, 4, 2, [own, partner, near])
        )
        return sent, kept.reshape(2 * block_rows, own.shape[2])

    def gather(part):
        return lax.all_gather(part, "col", axis=0, tiled=True)

    def sum_up(gradient):
        own = lax.psum_scatter(gradient, "col", scatter_dimension=0, tiled=True)
        return own.reshape(2, block_rows, own.shape[1])

    def send_home(own):
        near = lax.ppermute(own, "col", outward)
        held = [own, near, swap_cores(own, columns), swap_cores(near, columns)]

        def farther():
            far = lax.ppermute(own, "col", inward)
            return pick_blocks(codes, 6, CAP, held + [far, swap_cores(far, columns)])

        return lax.cond(uneven, farther, lambda: pick_blocks(codes, 6, CAP, held))

    local_in = inputs[0]
    upstream = cotangent[0]
    row = row_index.reshape(1)
    tables = lane_tables(inputs.shape[1] * 4)
    rates = step_rates()

    query_slabs = [
        jnp.transpose(part, (1, 0, 2)) for part in (query_master, query_first, query_second)
    ]
    plain_one = norm_one(order, local_in)
    rows_plain, *plain_parts = share_rows(plain_one)
    sent_query, query_part = spread_out(
        pack_query(query_slabs[0]), after(codes, plain_one), after(codes, *plain_parts)
    )
    w_query = gather(query_part)
    vector_rows = jnp.pad(vector_master.T, ((0, 9), (0, 0))).astype(BF16)
    vector_blocks = jnp.transpose(vector_rows.reshape(16, CAP, block_rows), (1, 0, 2))
    vectors, bias = spread_vectors(
        sorted_slots, head_slots, gather(after(vector_blocks, query_part))
    )
    unused, output_part = spread_out(
        pack_flat("pack_output", output_master),
        after(codes, rows_plain, vectors),
        after(codes, query_part),
    )
    w_output = gather(output_part)
    rows_grad = share_rows(order_grad(after(order, rows_plain), upstream))[0]
    rows_one = scale_rows(rows_plain, vectors)
    mixed = matmul(rows_one, w_query, 1, 0, F32)
    gate_states = [gate_lines(part) for part in (gate_master, gate_first, gate_second)]
    unused, gate_part = spread_out(
        pack_gate(gate_states[0], gate_master.shape[0]),
        after(codes, rows_one, output_part),
        after(codes, mixed),
    )
    w_gate = gather(gate_part)
    attended, queries, keys, values, logs = attend(
        after(row, gate_part), image_starts, mixed, bias, tables
    )
    unused, down_part = spread_out(
        pack_flat("pack_down", down_master), after(codes, gate_part), after(codes, attended)
    )
    w_down = gather(down_part)
    middle, normed_two = norm_two(
        order,
        local_in,
        scatter_rows(matmul(attended, w_output, 1, 1, BF16))[0],
        after(vectors, down_part, rows_grad),
    )
    rows_two = share_rows(normed_two)[0]
    gate, up, hidden = gate_up(rows_two, w_gate)

    down_sums = matmul(rows_grad, hidden, 0, 0, BF16)
    down_own = sum_up(down_sums)
    gate_up_grad = gate_up_back(rows_grad, w_down, after(gate, down_sums), up)
    pulled_two = matmul(gate_up_grad, w_gate, 1, 1, BF16)
    gate_sums = matmul(rows_two, after(gate_up_grad, pulled_two), 0, 0, BF16)
    gate_own = sum_up(gate_sums)
    out_sums = matmul(after(hidden, gate_sums), w_down, 1, 1, BF16)
    middle_grad, low_middle, sums_two = norm_two_back(
        order, upstream, middle, scatter_rows(pulled_two)[0], after(vectors, gate_sums, out_sums)
    )
    rows_mid = share_rows(low_middle)[0]
    new_down = adam_flat(
        "adam_down",
        live,
        (down_master, down_first, down_second),
        send_home(after(down_own, low_middle)),
        rates[3],
    )
    attended_grad = matmul(after(rows_mid, new_down[0]), w_output, 1, 0, BF16)
    output_sums = matmul(rows_mid, after(attended, attended_grad), 0, 0, BF16)
    output_own = sum_up(output_sums)
    out_partial, *out_parts = scatter_rows(after(out_sums, attended_grad))
    mixed_grad, bias_sums = attend_back(
        after(row, output_sums, *out_parts),
        image_starts,
        queries,
        keys,
        values,
        logs,
        attended,
        attended_grad,
        tables,
    )
    layer_out = finish_out(order, middle, out_partial)
    pulled_one = matmul(after(mixed_grad, layer_out), w_query, 1, 1, BF16)
    query_sums = matmul(rows_one, after(mixed_grad, pulled_one), 0, 0, BF16)
    query_own = sum_up(query_sums)
    input_grad, sums_one = norm_one_back(
        order,
        local_in,
        middle_grad,
        scatter_rows(pulled_one)[0],
        after(vectors, query_sums),
    )
    new_gate = [
        gate_unlines(part, gate_master.shape)
        for part in adam_gate(
            live, gate_states, send_home(after(gate_own, query_sums)), rates[2]
        )
    ]
    vector_sums = place_vector_grads(
        after(head_places, new_gate[0]), sums_one, sums_two, bias_sums
    )
    for axis, reach in (("row", 1), ("row", 2), ("col", 1), ("col", 2), ("col", 4)):
        vector_sums = vector_sums + lax.ppermute(vector_sums, axis, flips(axis, reach))
    new_output = adam_flat(
        "adam_output",
        live,
        (output_master, output_first, output_second),
        send_home(after(output_own, new_gate[0])),
        rates[1],
    )
    new_vector = [
        part.T
        for part in adam_vector(
            live,
            home_places,
            [part.T for part in (vector_master, vector_first, vector_second)],
            vector_sums,
            rates[4],
        )
    ]
    query_own = after(query_own, new_output[0], new_vector[0], input_grad)
    new_query = [
        jnp.transpose(part, (1, 0, 2))
        for part in adam_query(live, query_slabs, send_home(query_own), rates[0])
    ]
    return (
        layer_out[None],
        input_grad[None],
        *new_query,
        *new_output,
        *new_gate,
        *new_down,
        *new_vector,
    )


def solution(mesh):
    one_hop_line = mesh.shape["row"] == 4 and mesh.shape["col"] == 8
    return jax.shard_map(
        local_line if one_hop_line else local,
        mesh=mesh,
        in_specs=(
            P("col", "row", None),
            P("col", "row", None),
            P("col", None),
            P(),
            P("col", None, "row"),
            P("col", None, "row"),
            P("col", None, "row"),
            P("col", "row"),
            P("col", "row"),
            P("col", "row"),
            P("col", None, "row"),
            P("col", None, "row"),
            P("col", None, "row"),
            P("col", "row"),
            P("col", "row"),
            P("col", "row"),
            P("col", None),
            P("col", None),
            P("col", None),
        ),
        out_specs=(
            P("col", "row", None),
            P("col", "row", None),
            P("col", None, "row"),
            P("col", None, "row"),
            P("col", None, "row"),
            P("col", "row"),
            P("col", "row"),
            P("col", "row"),
            P("col", None, "row"),
            P("col", None, "row"),
            P("col", None, "row"),
            P("col", "row"),
            P("col", "row"),
            P("col", "row"),
            P("col", None),
            P("col", None),
            P("col", None),
        ),
        check_vma=False,
    )
```

```python
import math

import jax
import jax.numpy as jnp
import numpy as np
from jax import lax
from jax.experimental import pallas as pl
from jax.experimental.layout import Layout, with_layout_constraint
from jax.experimental.pallas import tpu as pltpu
from jax.sharding import PartitionSpec as P

D = 2048
HEAD_DIM = 64
FF = 5632
ROT = 16
SEQ = 1024
IMG = 256
STEP = 5
CAP = 4

LANES = 128
MIB = 1 << 20

NORM_EPSILON = 1e-05
ADAM_EPSILON = 1e-08
MOMENT_DECAY = 0.5
WEIGHT_DECAY = 0.1
ROTARY_BASE = 10000.0
MASKED_SCORE = -1e30


def owner_slots(owners):
    block_count = owners.shape[0]
    block_order = jnp.arange(block_count, dtype=jnp.int32)
    before = (owners[:, None] == owners[None, :]) & (block_order[None, :] < block_order[:, None])
    return owners * CAP + jnp.sum(before.astype(jnp.int32), axis=1)


def slot_sources(slot_of, slot_count):
    matches = slot_of[None, :] == jnp.arange(slot_count, dtype=jnp.int32)[:, None]
    filled = jnp.any(matches, axis=1)
    numbers = jnp.arange(slot_of.shape[0], dtype=jnp.int32)
    source = jnp.sum(jnp.where(matches, numbers[None, :], 0), axis=1)
    return (source, filled)


def unpack(gathered, slot_of, block_rows):
    shaped = gathered.reshape((-1, block_rows) + gathered.shape[1:])
    return jnp.take(shaped, slot_of, axis=0).reshape((-1,) + gathered.shape[1:])


def own_blocks(gradient, own_source, block_rows):
    shaped = gradient.reshape((-1, block_rows) + gradient.shape[1:])
    return jnp.take(shaped, own_source, axis=0).reshape((-1,) + gradient.shape[1:])


def normalize(values):
    center = jnp.mean(values, axis=-1, keepdims=True)
    spread = jnp.mean(values * values, axis=-1, keepdims=True) - center * center
    inverse = lax.rsqrt(spread + NORM_EPSILON)
    return ((values - center) * inverse, inverse)


def norm_back(upstream, plain_rows, inverse, gain_row):
    scaled = upstream * gain_row
    return inverse * (
        scaled
        - jnp.mean(scaled, axis=-1, keepdims=True)
        - plain_rows * jnp.mean(scaled * plain_rows, axis=-1, keepdims=True)
    )


def rotary_tables(seq_len):
    half_rot = ROT // 2
    frequency = ROTARY_BASE ** (-2.0 * jnp.arange(half_rot, dtype=jnp.float32) / ROT)
    angles = jnp.arange(seq_len, dtype=jnp.float32)[:, None] * frequency[None, :]
    return (jnp.cos(angles), jnp.sin(angles))


def rotate(values, cosine_table, sine_table):
    half_rot = ROT // 2
    first_half = values[..., :half_rot]
    second_half = values[..., half_rot:ROT]
    cosine_part = cosine_table[:, None, :]
    sine_part = sine_table[:, None, :]
    return jnp.concatenate(
        [
            first_half * cosine_part - second_half * sine_part,
            second_half * cosine_part + first_half * sine_part,
            values[..., ROT:],
        ],
        axis=-1,
    )


def rotate_back(values, cosine_table, sine_table):
    half_rot = ROT // 2
    first_half = values[..., :half_rot]
    second_half = values[..., half_rot:ROT]
    cosine_part = cosine_table[:, None, :]
    sine_part = sine_table[:, None, :]
    return jnp.concatenate(
        [
            first_half * cosine_part + second_half * sine_part,
            second_half * cosine_part - first_half * sine_part,
            values[..., ROT:],
        ],
        axis=-1,
    )


def block_ids(starts, seq_len):
    positions = jnp.arange(seq_len, dtype=jnp.int32)
    inside = (positions[None, :] >= starts[:, None]) & (positions[None, :] < starts[:, None] + IMG)
    numbers = jnp.arange(1, starts.shape[0] + 1, dtype=jnp.int32)
    return jnp.sum(jnp.where(inside, numbers[:, None], 0), axis=0)


def adam_step(master, first_state, second_state, gradient, keep_rows, rate):
    new_first = MOMENT_DECAY * first_state + (1.0 - MOMENT_DECAY) * gradient
    new_second = MOMENT_DECAY * second_state + (1.0 - MOMENT_DECAY) * gradient * gradient
    correction = 1.0 - MOMENT_DECAY**STEP
    direction = new_first / correction / (jnp.sqrt(new_second / correction) + ADAM_EPSILON)
    new_master = master - rate * (direction + WEIGHT_DECAY * master)
    keep_mask = keep_rows.reshape(keep_rows.shape + (1,) * (master.ndim - 1))
    return (
        jnp.where(keep_mask, new_master, master),
        jnp.where(keep_mask, new_first, first_state),
        jnp.where(keep_mask, new_second, second_state),
    )


def step_rates():
    return (
        2.0 / math.sqrt(D),
        2.0 / math.sqrt(D * 16 // SEQ),
        2.0 / math.sqrt(D),
        2.0 / math.sqrt(FF),
        0.5,
    )


def local(
    inputs,
    cotangent,
    image_starts,
    owners,
    query_master,
    query_first,
    query_second,
    output_master,
    output_first,
    output_second,
    gate_master,
    gate_first,
    gate_second,
    down_master,
    down_first,
    down_second,
    vector_master,
    vector_first,
    vector_second,
):
    columns = lax.axis_size("col")
    col_index = lax.axis_index("col")
    row_index = lax.axis_index("row")
    block_rows = D // owners.shape[0]
    slot_of = owner_slots(owners)
    source, filled = slot_sources(slot_of, CAP * columns)
    shared = (
        lax.all_gather(query_master.astype(jnp.bfloat16), "col", axis=0, tiled=True),
        lax.all_gather(output_master.astype(jnp.bfloat16), "col", axis=0, tiled=True),
        lax.all_gather(gate_master.astype(jnp.bfloat16), "col", axis=0, tiled=True),
        lax.all_gather(down_master.astype(jnp.bfloat16), "col", axis=0, tiled=True),
        lax.all_gather(vector_master.astype(jnp.bfloat16), "col", axis=0, tiled=True),
    )
    w_query = unpack(shared[0], slot_of, block_rows)
    w_output = unpack(shared[1], slot_of, block_rows)
    w_gate = unpack(shared[2], slot_of, block_rows)
    w_down = unpack(shared[3], slot_of, block_rows)
    vectors = unpack(shared[4], slot_of, block_rows).astype(jnp.float32)
    local_in = inputs[0]
    width = local_in.shape[1]
    head_cols = w_query.shape[2]
    local_heads = head_cols // HEAD_DIM
    score_scale = 1.0 / math.sqrt(HEAD_DIM)
    qkv_bias = lax.dynamic_slice_in_dim(vectors[:, 4:7], row_index * head_cols, head_cols, 0).T
    plain_one, inverse_one = normalize(local_in)
    normed_one = (plain_one * vectors[:, 0] + vectors[:, 1]).astype(jnp.bfloat16)
    rows_one = lax.all_gather(normed_one, "row", axis=0, tiled=True)
    seq_len = rows_one.shape[0]
    mixed_proj = (
        jnp.einsum("td,djh->tjh", rows_one, w_query, preferred_element_type=jnp.float32)
        + qkv_bias[None]
    )
    cosine_table, sine_table = rotary_tables(seq_len)
    queries = rotate(
        mixed_proj[:, 0].reshape(seq_len, local_heads, HEAD_DIM), cosine_table, sine_table
    ).astype(jnp.bfloat16)
    key_rows = rotate(
        mixed_proj[:, 1].reshape(seq_len, local_heads, HEAD_DIM), cosine_table, sine_table
    ).astype(jnp.bfloat16)
    value_rows = mixed_proj[:, 2].reshape(seq_len, local_heads, HEAD_DIM).astype(jnp.bfloat16)
    labels = block_ids(image_starts[0], seq_len)
    block_size = min(512, seq_len)
    block_count = seq_len // block_size
    positions = jnp.arange(seq_len, dtype=jnp.int32)

    def scores_at(first_row):
        row_pos = first_row + jnp.arange(block_size, dtype=jnp.int32)
        row_label = lax.dynamic_slice_in_dim(labels, first_row, block_size, 0)
        allowed = (positions[None, :] <= row_pos[:, None]) | (
            row_label[:, None] == labels[None, :]
        ) & (row_label[:, None] > 0)
        query_rows = lax.dynamic_slice_in_dim(queries, first_row, block_size, 0)
        raw_scores = (
            jnp.einsum("qhe,khe->hqk", query_rows, key_rows, preferred_element_type=jnp.float32)
            * score_scale
        )
        return (jnp.where(allowed[None], raw_scores, MASKED_SCORE), query_rows)

    def forward_block(block_index):
        scores, query_rows = scores_at(block_index * block_size)
        row_peak = jnp.max(scores, axis=-1, keepdims=True)
        powers = jnp.exp(scores - row_peak)
        row_total = jnp.sum(powers, axis=-1, keepdims=True)
        weights = (powers / row_total).astype(jnp.bfloat16)
        output = jnp.einsum("hqk,khe->qhe", weights, value_rows, preferred_element_type=jnp.float32)
        return (output, (row_peak + jnp.log(row_total))[..., 0])

    output_blocks, log_totals = lax.map(forward_block, jnp.arange(block_count, dtype=jnp.int32))
    attended = output_blocks.reshape(seq_len, head_cols).astype(jnp.bfloat16)
    picked_rows = attended
    middle = local_in + lax.psum_scatter(
        jnp.einsum("th,dh->td", picked_rows, w_output, preferred_element_type=jnp.float32),
        "row",
        scatter_dimension=0,
        tiled=True,
    )
    plain_two, inverse_two = normalize(middle)
    normed_two = (plain_two * vectors[:, 2] + vectors[:, 3]).astype(jnp.bfloat16)
    rows_two = lax.all_gather(normed_two, "row", axis=0, tiled=True)
    gate_up = jnp.einsum("td,djf->tjf", rows_two, w_gate, preferred_element_type=jnp.float32)
    gate_part = gate_up[:, 0]
    up_part = gate_up[:, 1]
    gate_sigmoid = jax.nn.sigmoid(gate_part)
    activated = gate_part * gate_sigmoid
    hidden = (activated * up_part).astype(jnp.bfloat16)
    picked_rows = hidden
    layer_out = middle + lax.psum_scatter(
        jnp.einsum("tf,df->td", picked_rows, w_down, preferred_element_type=jnp.float32).astype(
            jnp.bfloat16
        ),
        "row",
        scatter_dimension=0,
        tiled=True,
    ).astype(jnp.float32)
    upstream = cotangent[0]
    rows_grad = lax.all_gather(upstream.astype(jnp.bfloat16), "row", axis=0, tiled=True)
    hidden_grad = jnp.einsum("td,df->tf", rows_grad, w_down, preferred_element_type=jnp.float32)
    down_grad = jnp.einsum("tf,td->df", hidden, rows_grad, preferred_element_type=jnp.float32)
    gate_grad = hidden_grad * up_part * gate_sigmoid * (1.0 + gate_part * (1.0 - gate_sigmoid))
    up_grad = hidden_grad * activated
    gate_up_grad = jnp.stack([gate_grad, up_grad], axis=1).astype(jnp.bfloat16)
    gate_weight_grad = jnp.einsum(
        "td,tjf->djf", rows_two, gate_up_grad, preferred_element_type=jnp.float32
    )
    picked_rows = gate_up_grad
    normed_two_grad = lax.psum_scatter(
        jnp.einsum("tjf,djf->td", picked_rows, w_gate, preferred_element_type=jnp.float32),
        "row",
        scatter_dimension=0,
        tiled=True,
    )
    middle_grad = upstream + norm_back(normed_two_grad, plain_two, inverse_two, vectors[:, 2])
    rows_mid = lax.all_gather(middle_grad.astype(jnp.bfloat16), "row", axis=0, tiled=True)
    attended_grad = jnp.einsum(
        "td,dh->th", rows_mid, w_output, preferred_element_type=jnp.float32
    ).astype(jnp.bfloat16)
    output_grad = jnp.einsum("th,td->dh", attended, rows_mid, preferred_element_type=jnp.float32)
    head_grad = attended_grad.reshape(seq_len, local_heads, HEAD_DIM)

    def backward_block(running, block_index):
        key_total, value_total = running
        first_row = block_index * block_size
        scores, query_rows = scores_at(first_row)
        probabilities = jnp.exp(scores - log_totals[block_index][..., None])
        row_grad = lax.dynamic_slice_in_dim(head_grad, first_row, block_size, 0)
        prob_grad = jnp.einsum(
            "qhe,khe->hqk", row_grad, value_rows, preferred_element_type=jnp.float32
        )
        inner = jnp.sum(prob_grad * probabilities, axis=-1, keepdims=True)
        score_grad = (probabilities * (prob_grad - inner)).astype(jnp.bfloat16)
        query_grad = (
            jnp.einsum("hqk,khe->qhe", score_grad, key_rows, preferred_element_type=jnp.float32)
            * score_scale
        )
        key_total = (
            key_total
            + jnp.einsum("hqk,qhe->khe", score_grad, query_rows, preferred_element_type=jnp.float32)
            * score_scale
        )
        value_total = value_total + jnp.einsum(
            "hqk,qhe->khe",
            probabilities.astype(jnp.bfloat16),
            row_grad,
            preferred_element_type=jnp.float32,
        )
        return ((key_total, value_total), query_grad)

    empty_heads = jnp.zeros((seq_len, local_heads, HEAD_DIM), jnp.float32)
    (key_grad, value_grad), query_blocks = lax.scan(
        backward_block, (empty_heads, empty_heads), jnp.arange(block_count, dtype=jnp.int32)
    )
    query_grad = query_blocks.reshape(seq_len, local_heads, HEAD_DIM)
    mixed_grad = jnp.stack(
        [
            rotate_back(query_grad, cosine_table, sine_table).reshape(seq_len, head_cols),
            rotate_back(key_grad, cosine_table, sine_table).reshape(seq_len, head_cols),
            value_grad.reshape(seq_len, head_cols),
        ],
        axis=1,
    ).astype(jnp.bfloat16)
    bias_grad = jnp.sum(mixed_grad, axis=0, dtype=jnp.float32)
    query_weight_grad = jnp.einsum(
        "td,tjh->djh", rows_one, mixed_grad, preferred_element_type=jnp.float32
    )
    picked_rows = mixed_grad
    normed_one_grad = lax.psum_scatter(
        jnp.einsum("tjh,djh->td", picked_rows, w_query, preferred_element_type=jnp.float32).astype(
            jnp.bfloat16
        ),
        "row",
        scatter_dimension=0,
        tiled=True,
    ).astype(jnp.float32)
    input_grad = middle_grad + norm_back(normed_one_grad, plain_one, inverse_one, vectors[:, 0])
    norm_grads = jnp.stack(
        [
            jnp.sum(normed_one_grad * plain_one, axis=0),
            jnp.sum(normed_one_grad, axis=0),
            jnp.sum(normed_two_grad * plain_two, axis=0),
            jnp.sum(normed_two_grad, axis=0),
        ],
        axis=1,
    )
    placed = lax.dynamic_update_slice_in_dim(
        jnp.zeros((width, 3), jnp.float32), bias_grad.T, row_index * head_cols, 0
    )
    vector_grad = lax.psum(
        jnp.concatenate([norm_grads, placed], axis=1).astype(jnp.bfloat16), "row"
    )
    own_filled = lax.dynamic_slice_in_dim(filled, col_index * CAP, CAP, 0)
    own_source = lax.dynamic_slice_in_dim(source, col_index * CAP, CAP, 0)
    summed = (
        lax.psum(query_weight_grad.astype(jnp.bfloat16), "col").astype(jnp.float32),
        lax.psum(output_grad.astype(jnp.bfloat16), "col").astype(jnp.float32),
        lax.psum(gate_weight_grad.astype(jnp.bfloat16), "col").astype(jnp.float32),
        lax.psum(down_grad.astype(jnp.bfloat16), "col").astype(jnp.float32),
        lax.psum(vector_grad, "col").astype(jnp.float32),
    )
    owned_grads = tuple((own_blocks(whole_grad, own_source, block_rows) for whole_grad in summed))
    keep_rows = jnp.repeat(own_filled, block_rows)
    masters = (query_master, output_master, gate_master, down_master, vector_master)
    firsts = (query_first, output_first, gate_first, down_first, vector_first)
    seconds = (query_second, output_second, gate_second, down_second, vector_second)
    rates = step_rates()
    updated = [
        adam_step(
            masters[kind_index],
            firsts[kind_index],
            seconds[kind_index],
            owned_grads[kind_index],
            keep_rows,
            rates[kind_index],
        )
        for kind_index in range(5)
    ]
    return (
        layer_out[None],
        input_grad[None],
        updated[0][0],
        updated[0][1],
        updated[0][2],
        updated[1][0],
        updated[1][1],
        updated[1][2],
        updated[2][0],
        updated[2][1],
        updated[2][2],
        updated[3][0],
        updated[3][1],
        updated[3][2],
        updated[4][0],
        updated[4][1],
        updated[4][2],
    )


BF16 = jnp.bfloat16
F32 = jnp.float32


def smem():
    return pl.BlockSpec(memory_space=pltpu.SMEM)


def params(mib=16):
    return pltpu.CompilerParams(vmem_limit_bytes=mib * MIB)


def cost(flops, nbytes, powers=0):
    return pl.CostEstimate(flops=int(flops), bytes_accessed=int(nbytes), transcendentals=int(powers))


def lane_block(number):
    return pl.ds(pl.multiple_of(number * LANES, LANES), LANES)


def after(value, *others):
    return lax.optimization_barrier((value, *others))[0]


PICKS, LIVE, PLACES, UNEVEN, TABLE = 0, 10, 14, 18, 32


def plan_blocks(owners, places, columns, head_blocks):
    blocks = owners.shape[0]
    half = blocks // (columns // 2)

    def kernel(owner_ref, at_ref, table_ref, order_ref, sorted_ref, head_slot_ref, head_ref):
        held = [owner_ref[block] for block in range(blocks)]
        col, row = at_ref[0], at_ref[1]
        chip = lax.shift_right_logical(col, 1)
        core = jnp.bitwise_and(col, 1)

        def total(flags):
            return sum(flag.astype(jnp.int32) for flag in flags)

        def below(index):
            return total(owner < index for owner in held)

        for block in range(blocks):
            rank = total(held[other] == held[block] for other in range(block)) + jnp.int32(0)
            place = below(held[block]) + rank
            slot = held[block] * CAP + rank
            order_ref[place] = jnp.int32(block)
            sorted_ref[place] = slot
            head = block - row * head_blocks

            @pl.when((head >= 0) & (head < head_blocks))
            def mine(head=head, slot=slot, place=place):
                head_slot_ref[head] = slot
                head_ref[head] = place

        first = below(2 * chip)
        middle = below(2 * chip + 1)
        end = below(2 * chip + 2)
        own_first = below(col)
        own_count = below(col + 1) - own_first

        def chip_code(place):
            second = place >= middle
            rank = place - jnp.where(second, middle, first)
            code = jnp.where(second.astype(jnp.int32) == core, 0, 16) + rank
            return jnp.where((place >= first) & (place < end), code, 0)

        toward = 1 - 2 * core
        for index in range(2):
            offset = 2 * core + index
            table_ref[index] = chip_code(half * (chip + toward) + offset)
            table_ref[2 + index] = chip_code(half * (chip - toward) + offset)
            kept = half * chip + offset
            near, far = 32 + index, 48 + index
            table_ref[4 + index] = jnp.where(
                kept < first,
                jnp.where(core == 0, near, far),
                jnp.where(kept >= end, jnp.where(core == 0, far, near), chip_code(kept)),
            )
        for rank in range(CAP):
            live = rank < own_count
            place = own_first + jnp.minimum(rank, own_count - 1)
            there = lax.shift_right_logical(place, 2)
            side = there - chip
            other = lax.shift_right_logical(place - half * there, 1)
            near_side = 1 - 2 * other
            same = other == core
            source = jnp.where(
                side == 0,
                jnp.where(same, 0, 2),
                jnp.where(side == near_side, jnp.where(same, 1, 3), jnp.where(same, 4, 5)),
            )
            table_ref[6 + rank] = 16 * source + jnp.bitwise_and(place, 1)
            table_ref[LIVE + rank] = live.astype(jnp.int32)
            table_ref[PLACES + rank] = place
        widest = jnp.int32(0)
        for number in range(1, columns // 2):
            widest = jnp.maximum(widest, jnp.abs(below(2 * number) - half * number))
        table_ref[UNEVEN] = (widest > 2).astype(jnp.int32)
        for index in range(UNEVEN + 1, TABLE):
            table_ref[index] = jnp.int32(0)

    def ints(size):
        return jax.ShapeDtypeStruct((size,), jnp.int32)

    return pl.pallas_call(
        kernel,
        in_specs=[smem(), smem()],
        out_specs=[smem()] * 5,
        out_shape=[ints(TABLE), ints(blocks), ints(blocks), ints(head_blocks), ints(head_blocks)],
        compiler_params=params(),
        name="plan_blocks",
    )(owners, places)


def pack_attention(slabs, output):
    kinds, rows, width = slabs.shape
    block = rows // CAP
    total = kinds * width + output.shape[1]

    def kernel(in_ref, output_ref, out_ref):
        for kind in range(kinds):
            out_ref[0, :, kind * width : (kind + 1) * width] = in_ref[kind].astype(BF16)
        out_ref[0, :, kinds * width :] = output_ref[...].astype(BF16)

    return pl.pallas_call(
        kernel,
        grid=(CAP,),
        in_specs=[
            pl.BlockSpec((kinds, block, width), lambda s: (0, s, 0)),
            pl.BlockSpec((block, output.shape[1]), lambda s: (s, 0)),
        ],
        out_specs=pl.BlockSpec((1, block, total), lambda s: (s, 0, 0)),
        out_shape=jax.ShapeDtypeStruct((CAP, block, total), BF16),
        compiler_params=params(58),
        cost_estimate=cost(0, 6 * rows * total),
        name="pack_attention",
    )(slabs, output)


def after(value, *others):
    return lax.optimization_barrier((value, *others))[0]


def gate_lines(values):
    rows, kinds, width = values.shape
    split = with_layout_constraint(
        values.reshape(rows, kinds, width // LANES, LANES), Layout(major_to_minor=(0, 2, 1, 3))
    )
    return jnp.transpose(split, (0, 2, 1, 3)).reshape(rows * kinds * width // LANES, LANES)


def gate_unlines(lines, shape):
    rows, kinds, width = shape
    split = jnp.transpose(lines.reshape(rows, width // LANES, kinds, LANES), (0, 2, 1, 3))
    return with_layout_constraint(split, Layout(major_to_minor=(0, 2, 1, 3))).reshape(shape)


def pack_flat(name, master):
    rows, width = master.shape
    block = rows // CAP

    def kernel(in_ref, out_ref):
        out_ref[0] = in_ref[...].astype(BF16)

    return pl.pallas_call(
        kernel,
        grid=(CAP,),
        in_specs=[pl.BlockSpec((block, width), lambda s: (s, 0))],
        out_specs=pl.BlockSpec((1, block, width), lambda s: (s, 0, 0)),
        out_shape=jax.ShapeDtypeStruct((CAP, block, width), BF16),
        compiler_params=params(),
        cost_estimate=cost(0, 6 * rows * width),
        name=name,
    )(master)


def pack_gate(lines, rows):
    block = rows // CAP
    tiles = lines.shape[0] // rows

    def kernel(in_ref, out_ref):
        for tile in range(tiles):
            out_ref[0, :, tile * LANES : (tile + 1) * LANES] = in_ref[
                pl.ds(tile, block, stride=tiles), :
            ].astype(BF16)

    return pl.pallas_call(
        kernel,
        grid=(CAP,),
        in_specs=[pl.BlockSpec((block * tiles, LANES), lambda s: (s, 0))],
        out_specs=pl.BlockSpec((1, block, tiles * LANES), lambda s: (s, 0, 0)),
        out_shape=jax.ShapeDtypeStruct((CAP, block, tiles * LANES), BF16),
        compiler_params=params(58),
        cost_estimate=cost(0, 6 * lines.size),
        name="pack_gate",
    )(lines)


def pick_blocks(codes, first, count, sources):
    shape = sources[0].shape[1:]

    def kernel(code_ref, *refs):
        ins, out, sems = refs[: len(sources)], refs[-2], refs[-1]
        for place in range(count):
            code = code_ref[first + place]
            index = jnp.bitwise_and(code, 15)
            origin = lax.shift_right_logical(code, 4)
            for number, source in enumerate(ins):

                @pl.when(origin == number)
                def start(source=source, index=index, place=place):
                    pltpu.make_async_copy(source.at[index], out.at[place], sems.at[place]).start()

        for place in range(count):
            pltpu.make_async_copy(ins[0].at[0], out.at[place], sems.at[place]).wait()

    moved = count * shape[0] * shape[1]
    return pl.pallas_call(
        kernel,
        in_specs=[smem()] + [pl.BlockSpec(memory_space=pl.ANY)] * len(sources),
        out_specs=pl.BlockSpec(memory_space=pltpu.VMEM),
        out_shape=jax.ShapeDtypeStruct((count, *shape), BF16),
        scratch_shapes=[pltpu.SemaphoreType.DMA((count,))],
        compiler_params=params(),
        cost_estimate=cost(0, 4 * moved),
        name="pick_blocks",
    )(codes, *sources)


def row_blocks(height, width, first=0):
    return pl.BlockSpec((height, width), lambda i: (i + first, 0))


def whole(height, width):
    return pl.BlockSpec((height, width), lambda i: (0, 0))


NORM_ROWS = 64


def statistics(values):
    center = jnp.mean(values, axis=-1, keepdims=True)
    spread = jnp.mean(values * values, axis=-1, keepdims=True) - center * center
    return center, lax.rsqrt(spread + NORM_EPSILON)


def order_grad(order, cotangent):
    rows, width = cotangent.shape

    def kernel(order_ref, in_ref, out_ref):
        for place in range(width // LANES):
            out_ref[:, place * LANES : (place + 1) * LANES] = in_ref[
                :, lane_block(order_ref[place])
            ].astype(BF16)

    return pl.pallas_call(
        kernel,
        grid=(rows // NORM_ROWS,),
        in_specs=[smem(), row_blocks(NORM_ROWS, width)],
        out_specs=row_blocks(NORM_ROWS, width),
        out_shape=jax.ShapeDtypeStruct((rows, width), BF16),
        compiler_params=params(),
        cost_estimate=cost(0, 6 * rows * width),
        name="order_grad",
    )(order, cotangent)


def norm_one(order, inputs):
    rows, width = inputs.shape

    def kernel(order_ref, in_ref, out_ref):
        center, inverse = statistics(in_ref[...])
        for place in range(width // LANES):
            span = slice(place * LANES, (place + 1) * LANES)
            plain = (in_ref[:, lane_block(order_ref[place])] - center) * inverse
            out_ref[:, span] = plain.astype(BF16)

    return pl.pallas_call(
        kernel,
        grid=(rows // NORM_ROWS,),
        in_specs=[smem(), row_blocks(NORM_ROWS, width)],
        out_specs=row_blocks(NORM_ROWS, width),
        out_shape=jax.ShapeDtypeStruct((rows, width), BF16),
        compiler_params=params(),
        cost_estimate=cost(0, 6 * rows * width),
        name="norm_one",
    )(order, inputs)


def scale_rows(plain, vectors):
    rows, width = plain.shape
    tile = 256

    def kernel(in_ref, vec_ref, out_ref):
        out_ref[...] = (in_ref[...].astype(F32) * vec_ref[0:1, :] + vec_ref[1:2, :]).astype(BF16)

    return pl.pallas_call(
        kernel,
        grid=(rows // tile,),
        in_specs=[row_blocks(tile, width), whole(8, width)],
        out_specs=row_blocks(tile, width),
        out_shape=jax.ShapeDtypeStruct((rows, width), BF16),
        compiler_params=params(),
        cost_estimate=cost(0, 4 * rows * width),
        name="scale_rows",
    )(plain, vectors)


def norm_two(order, inputs, partial, vectors):
    rows, width = inputs.shape
    own, from_x, from_y = partial

    def kernel(order_ref, in_ref, own_ref, x_ref, y_ref, vec_ref, mid_ref, out_ref):
        for place in range(width // LANES):
            span = slice(place * LANES, (place + 1) * LANES)
            mid_ref[:, span] = (
                in_ref[:, lane_block(order_ref[place])]
                + own_ref[:, span].astype(F32)
                + x_ref[:, span].astype(F32)
                + y_ref[:, span].astype(F32)
            )
        middle = mid_ref[...]
        center, inverse = statistics(middle)
        plain = (middle - center) * inverse
        out_ref[...] = (plain * vec_ref[2:3, :] + vec_ref[3:4, :]).astype(BF16)

    spec = row_blocks(NORM_ROWS, width)
    return pl.pallas_call(
        kernel,
        grid=(rows // NORM_ROWS,),
        in_specs=[smem(), spec, spec, spec, spec, whole(8, width)],
        out_specs=[spec, spec],
        out_shape=[
            jax.ShapeDtypeStruct((rows, width), F32),
            jax.ShapeDtypeStruct((rows, width), BF16),
        ],
        compiler_params=params(),
        cost_estimate=cost(0, 16 * rows * width),
        name="norm_two",
    )(order, inputs, own, from_x, from_y, vectors)


def finish_out(order, middle, partial):
    rows, width = middle.shape
    own, from_x, from_y = partial

    def kernel(order_ref, mid_ref, own_ref, x_ref, y_ref, out_ref):
        for place in range(width // LANES):
            span = slice(place * LANES, (place + 1) * LANES)
            out_ref[:, lane_block(order_ref[place])] = (
                mid_ref[:, span]
                + own_ref[:, span].astype(F32)
                + x_ref[:, span].astype(F32)
                + y_ref[:, span].astype(F32)
            )

    spec = row_blocks(NORM_ROWS, width)
    return pl.pallas_call(
        kernel,
        grid=(rows // NORM_ROWS,),
        in_specs=[smem(), spec, spec, spec, spec],
        out_specs=spec,
        out_shape=jax.ShapeDtypeStruct((rows, width), F32),
        compiler_params=params(),
        cost_estimate=cost(0, 14 * rows * width),
        name="finish_out",
    )(order, middle, own, from_x, from_y)


def norm_pull(upstream, plain, inverse, gain):
    scaled = upstream * gain
    return inverse * (
        scaled
        - jnp.mean(scaled, axis=-1, keepdims=True)
        - plain * jnp.mean(scaled * plain, axis=-1, keepdims=True)
    )


def add_sums(sum_ref, upstream, plain):
    @pl.when(pl.program_id(0) == 0)
    def clear():
        sum_ref[...] = jnp.zeros_like(sum_ref)

    sum_ref[0:1, :] += jnp.sum(upstream * plain, axis=0, keepdims=True)
    sum_ref[1:2, :] += jnp.sum(upstream, axis=0, keepdims=True)


def norm_two_back(order, cotangent, middle, partial, vectors):
    rows, width = middle.shape
    own, from_x, from_y = partial

    def kernel(
        order_ref, cot_ref, mid_ref, own_ref, x_ref, y_ref, vec_ref, grad_ref, low_ref, sum_ref
    ):
        middle_rows = mid_ref[...]
        center, inverse = statistics(middle_rows)
        plain = (middle_rows - center) * inverse
        upstream = own_ref[...].astype(F32) + x_ref[...].astype(F32) + y_ref[...].astype(F32)
        add_sums(sum_ref, upstream, plain)
        grad_ref[...] = norm_pull(upstream, plain, inverse, vec_ref[2:3, :])
        for place in range(width // LANES):
            span = slice(place * LANES, (place + 1) * LANES)
            total = grad_ref[:, span] + cot_ref[:, lane_block(order_ref[place])]
            grad_ref[:, span] = total
            low_ref[:, span] = total.astype(BF16)

    spec = row_blocks(NORM_ROWS, width)
    return pl.pallas_call(
        kernel,
        grid=(rows // NORM_ROWS,),
        in_specs=[smem(), spec, spec, spec, spec, spec, whole(8, width)],
        out_specs=[spec, spec, whole(8, width)],
        out_shape=[
            jax.ShapeDtypeStruct((rows, width), F32),
            jax.ShapeDtypeStruct((rows, width), BF16),
            jax.ShapeDtypeStruct((8, width), F32),
        ],
        compiler_params=params(),
        cost_estimate=cost(0, 20 * rows * width),
        name="norm_two_back",
    )(order, cotangent, middle, own, from_x, from_y, vectors)


def norm_one_back(order, inputs, middle_grad, partial, vectors):
    rows, width = inputs.shape
    own, from_x, from_y = partial

    def kernel(
        order_ref,
        in_ref,
        mid_ref,
        own_ref,
        x_ref,
        y_ref,
        vec_ref,
        out_ref,
        sum_ref,
        plain_ref,
        pull_ref,
    ):
        center, inverse = statistics(in_ref[...])
        for place in range(width // LANES):
            span = slice(place * LANES, (place + 1) * LANES)
            plain_ref[:, span] = (in_ref[:, lane_block(order_ref[place])] - center) * inverse
        plain = plain_ref[...]
        upstream = own_ref[...].astype(F32) + x_ref[...].astype(F32) + y_ref[...].astype(F32)
        add_sums(sum_ref, upstream, plain)
        pull_ref[...] = norm_pull(upstream, plain, inverse, vec_ref[0:1, :])
        for place in range(width // LANES):
            span = slice(place * LANES, (place + 1) * LANES)
            out_ref[:, lane_block(order_ref[place])] = mid_ref[:, span] + pull_ref[:, span]

    spec = row_blocks(NORM_ROWS, width)
    return pl.pallas_call(
        kernel,
        grid=(rows // NORM_ROWS,),
        in_specs=[smem(), spec, spec, spec, spec, spec, whole(8, width)],
        out_specs=[spec, whole(8, width)],
        out_shape=[
            jax.ShapeDtypeStruct((rows, width), F32),
            jax.ShapeDtypeStruct((8, width), F32),
        ],
        scratch_shapes=[pltpu.VMEM((NORM_ROWS, width), F32), pltpu.VMEM((NORM_ROWS, width), F32)],
        compiler_params=params(),
        cost_estimate=cost(0, 18 * rows * width),
        name="norm_one_back",
    )(order, inputs, middle_grad, own, from_x, from_y, vectors)


def spread_vectors(sorted_slots, head_slots, gathered):
    places = sorted_slots.shape[0]
    heads = head_slots.shape[0]

    def kernel(sorted_ref, head_ref, in_ref, vec_ref, bias_ref):
        for place in range(places):
            vec_ref[:, place * LANES : (place + 1) * LANES] = in_ref[sorted_ref[place]].astype(F32)
        for place in range(heads):
            bias_ref[:, place * LANES : (place + 1) * LANES] = in_ref[head_ref[place]].astype(F32)

    return pl.pallas_call(
        kernel,
        in_specs=[smem(), smem(), pl.BlockSpec(memory_space=pltpu.VMEM)],
        out_shape=[
            jax.ShapeDtypeStruct((16, places * LANES), F32),
            jax.ShapeDtypeStruct((16, heads * LANES), F32),
        ],
        compiler_params=params(),
        name="spread_vectors",
    )(sorted_slots, head_slots, gathered)


def place_vector_grads(head_places, sums_one, sums_two, bias_sums):
    heads = head_places.shape[0]

    def kernel(head_ref, one_ref, two_ref, bias_ref, out_ref):
        out_ref[0:2, :] = one_ref[0:2, :]
        out_ref[2:4, :] = two_ref[0:2, :]
        out_ref[4:8, :] = jnp.zeros((4, out_ref.shape[1]), F32)
        for place in range(heads):
            for kind in range(3):
                first = (kind * heads + place) * LANES
                out_ref[4 + kind : 5 + kind, lane_block(head_ref[place])] = bias_ref[
                    0:1, first : first + LANES
                ]

    return pl.pallas_call(
        kernel,
        in_specs=[smem()] + [pl.BlockSpec(memory_space=pltpu.VMEM)] * 3,
        out_shape=jax.ShapeDtypeStruct(sums_one.shape, F32),
        compiler_params=params(),
        name="place_vector_grads",
    )(head_places, sums_one, sums_two, bias_sums)


def adam_vector(keep, states, gradient, rate):
    kinds, rows = states[0].shape
    block = rows // CAP

    def kernel(keep_ref, m_ref, f_ref, s_ref, g_ref, mo_ref, fo_ref, so_ref):
        for slot in range(CAP):
            span = slice(slot * block, (slot + 1) * block)
            grad = g_ref[:, lane_block(keep_ref[PLACES + slot])][:kinds]
            mo_ref[:, span], fo_ref[:, span], so_ref[:, span] = adam_update(
                m_ref[:, span], f_ref[:, span], s_ref[:, span], grad, keep_ref[LIVE + slot] > 0, rate
            )

    return pl.pallas_call(
        kernel,
        in_specs=[smem()] + [pl.BlockSpec(memory_space=pltpu.VMEM)] * 4,
        out_shape=[jax.ShapeDtypeStruct(states[0].shape, F32)] * 3,
        compiler_params=params(),
        name="adam_vector",
    )(keep, *states, gradient)


def lane_tables(seq_len):
    half = ROT // 2
    frequency = (ROTARY_BASE ** (-2.0 * np.arange(half, dtype=np.float32) / ROT)).astype(np.float32)
    angles = np.arange(seq_len, dtype=np.float32)[:, None] * frequency[None, :]
    cosine = np.cos(angles).astype(np.float32)
    sine = np.sin(angles).astype(np.float32)
    rest = HEAD_DIM - ROT
    ones = np.ones((seq_len, rest), np.float32)
    none = np.zeros((seq_len, rest), np.float32)
    blank = np.zeros((seq_len, half), np.float32)
    keep = np.concatenate([cosine, cosine, ones], axis=1)
    lower = np.concatenate([-sine, blank, none], axis=1)
    upper = np.concatenate([blank, sine, none], axis=1)
    return tuple(jnp.asarray(np.concatenate([table, table], axis=1)) for table in (keep, lower, upper))


def turn(values, keep, lower, upper):
    half = ROT // 2
    return (
        values * keep
        + pltpu.roll(values, LANES - half, 1) * lower
        + pltpu.roll(values, half, 1) * upper
    )


def head_mask(rows, head):
    lanes = lax.broadcasted_iota(jnp.int32, (rows, LANES), 1)
    return (lanes // HEAD_DIM) == head


def dot_nt(left, right):
    return lax.dot_general(left, right, (((1,), (1,)), ((), ())), preferred_element_type=F32)


def dot_nn(left, right):
    return lax.dot_general(left, right, (((1,), (0,)), ((), ())), preferred_element_type=F32)


def fill_masks(starts_ref, mask_ref, region):
    for part in range(2):
        keys = part * region + lax.broadcasted_iota(jnp.int32, (region, region), 0)
        queries = part * region + lax.broadcasted_iota(jnp.int32, (region, region), 1)
        visible = keys <= queries
        for image in range(starts_ref.shape[1]):
            first = starts_ref[0, image]
            visible = visible | (
                (keys >= first)
                & (keys < first + IMG)
                & (queries >= first)
                & (queries < first + IMG)
            )
        mask_ref[part] = jnp.where(visible, 0.0, MASKED_SCORE)


def tile_scores(key_rows, query_tile, mask_ref, part, first, tile, region):
    scores = dot_nt(key_rows, query_tile)
    mask = mask_ref[part, :, first : first + tile]
    if part == 0:
        return scores + mask
    return jnp.concatenate([scores[:region], scores[region:] + mask], axis=0)


def attend(row, starts, mixed, bias, tables):
    seq_len = mixed.shape[0]
    width = mixed.shape[1] // 3
    pairs = width // LANES
    tile = seq_len // 4
    region = seq_len // 2
    scale = 1.0 / math.sqrt(HEAD_DIM)

    def kernel(
        row_ref,
        starts_ref,
        q_ref,
        k_ref,
        v_ref,
        qb_ref,
        kb_ref,
        vb_ref,
        keep_ref,
        lower_ref,
        upper_ref,
        out_ref,
        qo_ref,
        ko_ref,
        vo_ref,
        log_ref,
        mask_ref,
    ):
        @pl.when(pl.program_id(0) == 0)
        def masks():
            fill_masks(starts_ref, mask_ref, region)

        for number in range(4):
            place = slice(number * tile, (number + 1) * tile)
            origin = pl.ds(pl.multiple_of(jnp.bitwise_xor(row_ref[0], number) * tile, tile), tile)
            turns = (keep_ref[place, :], lower_ref[place, :], upper_ref[place, :])
            turned = turn(q_ref[origin, :] + qb_ref[4:5, :], *turns)
            qo_ref[place, :] = (turned.astype(BF16).astype(F32) * scale).astype(BF16)
            ko_ref[place, :] = turn(k_ref[origin, :] + kb_ref[5:6, :], *turns).astype(BF16)
            vo_ref[place, :] = (v_ref[origin, :] + vb_ref[6:7, :]).astype(BF16)
        value_columns = jnp.transpose(vo_ref[...])
        for number in range(4):
            part = number // 2
            seen = region * (part + 1)
            first = (number % 2) * tile
            outs = []
            for head in range(2):
                query_tile = jnp.where(
                    head_mask(tile, head),
                    qo_ref[number * tile : (number + 1) * tile, :],
                    jnp.zeros((), BF16),
                )
                scores = tile_scores(
                    ko_ref[:seen, :], query_tile, mask_ref, part, first, tile, region
                )
                peak = jnp.max(scores, axis=0, keepdims=True)
                powers = jnp.exp(scores - peak)
                total = jnp.sum(powers, axis=0, keepdims=True)
                log_ref[0, head : head + 1, number * tile : (number + 1) * tile] = peak + jnp.log(
                    total
                )
                mixed_values = dot_nn(
                    value_columns[head * HEAD_DIM : (head + 1) * HEAD_DIM, :seen],
                    powers.astype(BF16),
                )
                outs.append(mixed_values / total)
            place = pl.ds(pl.multiple_of(jnp.bitwise_xor(row_ref[0], number) * tile, tile), tile)
            out_ref[place, :] = jnp.transpose(jnp.concatenate(outs, axis=0)).astype(BF16)

    def columns(kind):
        return pl.BlockSpec((seq_len, LANES), lambda h: (0, kind * pairs + h))

    bias_block = pl.BlockSpec((8, LANES), lambda h: (0, h))
    table = pl.BlockSpec((seq_len, LANES), lambda h: (0, 0))
    low = jax.ShapeDtypeStruct((seq_len, width), BF16)
    return pl.pallas_call(
        kernel,
        grid=(pairs,),
        in_specs=[smem(), smem()]
        + [columns(0), columns(1), columns(2)]
        + [bias_block] * 3
        + [table] * 3,
        out_specs=[columns(0)] * 4 + [pl.BlockSpec((1, 8, seq_len), lambda h: (h, 0, 0))],
        out_shape=[low] * 4 + [jax.ShapeDtypeStruct((pairs, 8, seq_len), F32)],
        scratch_shapes=[pltpu.VMEM((2, region, region), F32)],
        compiler_params=params(40),
        cost_estimate=cost(
            3 * seq_len * seq_len * width * 4, 20 * seq_len * width, seq_len * seq_len * 2 * pairs
        ),
        name="attend",
    )(row, starts, mixed, mixed, mixed, bias, bias, bias, *tables)


def attend_back(row, starts, queries, keys, values, logs, outputs, grads, tables):
    seq_len, width = queries.shape
    pairs = width // LANES
    tile = seq_len // 4
    region = seq_len // 2
    scale = 1.0 / math.sqrt(HEAD_DIM)

    def kernel(
        row_ref,
        starts_ref,
        q_ref,
        k_ref,
        v_ref,
        log_ref,
        o_ref,
        g_ref,
        keep_ref,
        lower_ref,
        upper_ref,
        out_ref,
        sum_ref,
        mask_ref,
        dq_ref,
        dk_ref,
        dv_ref,
        low_ref,
        bias_ref,
    ):
        @pl.when((pl.program_id(0) == 0) & (pl.program_id(1) == 0))
        def masks():
            fill_masks(starts_ref, mask_ref, region)

        @pl.when(pl.program_id(1) == 0)
        def work():
            dk_ref[...] = jnp.zeros_like(dk_ref)
            dv_ref[...] = jnp.zeros_like(dv_ref)
            key_columns = jnp.transpose(k_ref[...])
            for number in range(4):
                part = number // 2
                seen = region * (part + 1)
                first = (number % 2) * tile
                span = slice(number * tile, (number + 1) * tile)
                origin = pl.ds(
                    pl.multiple_of(jnp.bitwise_xor(row_ref[0], number) * tile, tile), tile
                )
                grad_tile = g_ref[origin, :]
                products = jnp.transpose(grad_tile.astype(F32) * o_ref[origin, :].astype(F32))
                query_grads = []
                for head in range(2):
                    mine = head_mask(tile, head)
                    query_tile = jnp.where(mine, q_ref[span, :], jnp.zeros((), BF16))
                    head_grad = jnp.where(mine, grad_tile, jnp.zeros((), BF16))
                    inner = jnp.sum(
                        products[head * HEAD_DIM : (head + 1) * HEAD_DIM], axis=0, keepdims=True
                    )
                    scores = tile_scores(
                        k_ref[:seen, :], query_tile, mask_ref, part, first, tile, region
                    )
                    weights = jnp.exp(scores - log_ref[0, head : head + 1, span])
                    pulls = dot_nt(v_ref[:seen, :], head_grad)
                    score_grad = (weights * (pulls - inner)).astype(BF16)
                    dv_ref[:seen, :] += dot_nn(weights.astype(BF16), head_grad)
                    dk_ref[:seen, :] += dot_nn(score_grad, query_tile)
                    query_grads.append(
                        dot_nn(
                            key_columns[head * HEAD_DIM : (head + 1) * HEAD_DIM, :seen], score_grad
                        )
                    )
                dq_ref[span, :] = jnp.transpose(jnp.concatenate(query_grads, axis=0)) * scale
            bias_ref[...] = jnp.zeros_like(bias_ref)
            for number in range(4):
                span = slice(number * tile, (number + 1) * tile)
                origin = pl.ds(
                    pl.multiple_of(jnp.bitwise_xor(row_ref[0], number) * tile, tile), tile
                )
                turns = (keep_ref[span, :], -lower_ref[span, :], -upper_ref[span, :])
                parts = (
                    turn(dq_ref[span, :], *turns),
                    turn(dk_ref[span, :], *turns),
                    dv_ref[span, :],
                )
                for kind in range(3):
                    low = parts[kind].astype(BF16)
                    low_ref[kind, origin, :] = low
                    bias_ref[kind, 0:1, :] += jnp.sum(low.astype(F32), axis=0, keepdims=True)

        out_ref[...] = low_ref[pl.program_id(1)]
        sum_ref[...] = bias_ref[pl.program_id(1)]

    columns = pl.BlockSpec((seq_len, LANES), lambda h, j: (0, h))
    table = pl.BlockSpec((seq_len, LANES), lambda h, j: (0, 0))
    return pl.pallas_call(
        kernel,
        grid=(pairs, 3),
        in_specs=[smem(), smem()]
        + [columns] * 3
        + [pl.BlockSpec((1, 8, seq_len), lambda h, j: (h, 0, 0))]
        + [columns] * 2
        + [table] * 3,
        out_specs=[
            pl.BlockSpec((seq_len, LANES), lambda h, j: (0, j * pairs + h)),
            pl.BlockSpec((8, LANES), lambda h, j: (0, j * pairs + h)),
        ],
        out_shape=[
            jax.ShapeDtypeStruct((seq_len, 3 * width), BF16),
            jax.ShapeDtypeStruct((8, 3 * width), F32),
        ],
        scratch_shapes=[
            pltpu.VMEM((2, region, region), F32),
            pltpu.VMEM((seq_len, LANES), F32),
            pltpu.VMEM((seq_len, LANES), F32),
            pltpu.VMEM((seq_len, LANES), F32),
            pltpu.VMEM((3, seq_len, LANES), BF16),
            pltpu.VMEM((3, 8, LANES), F32),
        ],
        compiler_params=params(48),
        cost_estimate=cost(
            8 * seq_len * seq_len * width * 4, 20 * seq_len * width, seq_len * seq_len * 2 * pairs
        ),
        name="attend_back",
    )(row, starts, queries, keys, values, logs, outputs, grads, *tables)


def gate_up(rows_two, w_gate):
    tokens, width = rows_two.shape
    tiles = w_gate.shape[1] // (2 * LANES)

    def kernel(in_ref, w_ref, gate_ref, up_ref, hidden_ref):
        both = dot_nn(in_ref[...], w_ref[...])
        gate, up = both[:, :LANES], both[:, LANES:]
        gate_ref[...] = gate.astype(BF16)
        up_ref[...] = up.astype(BF16)
        hidden_ref[...] = (gate * jax.nn.sigmoid(gate) * up).astype(BF16)

    out = pl.BlockSpec((tokens, LANES), lambda i: (0, i))
    return pl.pallas_call(
        kernel,
        grid=(tiles,),
        in_specs=[whole(tokens, width), pl.BlockSpec((width, 2 * LANES), lambda i: (0, i))],
        out_specs=[out] * 3,
        out_shape=[jax.ShapeDtypeStruct((tokens, tiles * LANES), BF16)] * 3,
        compiler_params=params(40),
        cost_estimate=cost(
            2 * tokens * w_gate.size,
            2 * (rows_two.size + w_gate.size) + 6 * tokens * tiles * LANES,
            tokens * tiles * LANES,
        ),
        name="gate_up",
    )(rows_two, w_gate)


def gate_up_back(rows_grad, w_down, gate, up):
    tokens, width = rows_grad.shape
    hidden = w_down.shape[1]
    tile = 256

    def kernel(in_ref, w_ref, gate_ref, up_ref, out_ref):
        pulled = dot_nn(in_ref[...], w_ref[...])
        for number in range(hidden // LANES):
            span = slice(number * LANES, (number + 1) * LANES)
            grad = pulled[:, span]
            gate_part = gate_ref[:, span].astype(F32)
            up_part = up_ref[:, span].astype(F32)
            squash = jax.nn.sigmoid(gate_part)
            first = 2 * number * LANES
            out_ref[:, first : first + LANES] = (
                grad * up_part * squash * (1.0 + gate_part * (1.0 - squash))
            ).astype(BF16)
            out_ref[:, first + LANES : first + 2 * LANES] = (grad * gate_part * squash).astype(BF16)

    return pl.pallas_call(
        kernel,
        grid=(tokens // tile,),
        in_specs=[
            row_blocks(tile, width),
            whole(width, hidden),
            row_blocks(tile, hidden),
            row_blocks(tile, hidden),
        ],
        out_specs=row_blocks(tile, 2 * hidden),
        out_shape=jax.ShapeDtypeStruct((tokens, 2 * hidden), BF16),
        compiler_params=params(40),
        cost_estimate=cost(
            2 * tokens * w_down.size,
            2 * (rows_grad.size + w_down.size) + 8 * tokens * hidden,
            tokens * hidden,
        ),
        name="gate_up_back",
    )(rows_grad, w_down, gate, up)


def adam_update(master, first, second, gradient, keep, rate):
    correction = 1.0 - MOMENT_DECAY**STEP
    new_first = MOMENT_DECAY * first + (1.0 - MOMENT_DECAY) * gradient
    new_second = MOMENT_DECAY * second + (1.0 - MOMENT_DECAY) * gradient * gradient
    direction = new_first / correction / (jnp.sqrt(new_second / correction) + ADAM_EPSILON)
    new_master = master - rate * (direction + WEIGHT_DECAY * master)
    return (
        jnp.where(keep, new_master, master),
        jnp.where(keep, new_first, first),
        jnp.where(keep, new_second, second),
    )


def adam_call(name, keep, states, gradient, rate, grid, state_spec, grad_spec, pieces):
    def kernel(keep_ref, m_ref, f_ref, s_ref, g_ref, mo_ref, fo_ref, so_ref):
        live = keep_ref[LIVE + pl.program_id(0)] > 0
        for state_at, grad_at in pieces:
            results = adam_update(
                m_ref[state_at],
                f_ref[state_at],
                s_ref[state_at],
                g_ref[grad_at].astype(F32),
                live,
                rate,
            )
            mo_ref[state_at], fo_ref[state_at], so_ref[state_at] = results

    return pl.pallas_call(
        kernel,
        grid=grid,
        in_specs=[smem()] + [state_spec] * 3 + [grad_spec],
        out_specs=[state_spec] * 3,
        out_shape=[jax.ShapeDtypeStruct(states[0].shape, F32)] * 3,
        compiler_params=params(58),
        cost_estimate=cost(12 * states[0].size, 26 * states[0].size, states[0].size),
        name=name,
    )(keep, *states, gradient)


def adam_query(keep, states, gradient, rate):
    kinds, rows, width = states[0].shape
    block = rows // CAP
    return adam_call(
        "adam_query",
        keep,
        states,
        gradient,
        rate,
        (CAP, kinds),
        pl.BlockSpec((1, block, width), lambda s, j: (j, s, 0)),
        pl.BlockSpec((1, block, width), lambda s, j: (s, 0, j)),
        [((0,), (0,))],
    )


def adam_flat(name, keep, states, gradient, rate):
    rows, width = states[0].shape
    block = rows // CAP
    return adam_call(
        name,
        keep,
        states,
        gradient,
        rate,
        (CAP,),
        pl.BlockSpec((block, width), lambda s: (s, 0)),
        pl.BlockSpec((1, block, width), lambda s: (s, 0, 0)),
        [((slice(None), slice(None)), (0,))],
    )


def adam_gate(keep, states, gradient, rate):
    block, width = gradient.shape[1:]
    tiles = width // LANES
    part = block // 2
    pieces = [
        (
            (pl.ds(tile, part, stride=tiles), slice(None)),
            (0, slice(None), slice(tile * LANES, (tile + 1) * LANES)),
        )
        for tile in range(tiles)
    ]
    return adam_call(
        "adam_gate",
        keep,
        states,
        gradient,
        rate,
        (CAP, 2),
        pl.BlockSpec((part * tiles, LANES), lambda s, i: (2 * s + i, 0)),
        pl.BlockSpec((1, part, width), lambda s, i: (s, i, 0)),
        pieces,
    )


def matmul(left, right, left_dim, right_dim, dtype):
    return lax.dot_general(
        left, right, (((left_dim,), (right_dim,)), ((), ())), preferred_element_type=F32
    ).astype(dtype)


def flips(axis, reach):
    return [(index, index ^ reach) for index in range(lax.axis_size(axis))]


def x_pairs():
    return flips("row", 1)


def y_pairs():
    return flips("row", 2)


def share_rows(own):
    half = own.shape[0] // 2
    by_x = lax.ppermute(own, "row", x_pairs())
    by_y = lax.ppermute(own, "row", y_pairs())
    top = lax.ppermute(by_x[:half], "row", y_pairs())
    bottom = lax.ppermute(by_y[half:], "row", x_pairs())
    return jnp.concatenate([own, by_x, by_y, top, bottom], axis=0), by_x, by_y


def fold_rows(sums, top, bottom):
    half, width = top.shape

    def kernel(one_ref, two_ref, top_ref, bottom_ref, x_ref, y_ref):
        first = pl.program_id(0) == 0
        one, two = one_ref[...].astype(F32), two_ref[...].astype(F32)
        x_ref[...] = jnp.where(first, one + top_ref[...].astype(F32), one).astype(BF16)
        y_ref[...] = jnp.where(first, two, two + bottom_ref[...].astype(F32)).astype(BF16)

    out = jax.ShapeDtypeStruct((2 * half, width), BF16)
    return pl.pallas_call(
        kernel,
        grid=(2,),
        in_specs=[
            row_blocks(half, width, 2),
            row_blocks(half, width, 4),
            whole(half, width),
            whole(half, width),
        ],
        out_specs=[row_blocks(half, width)] * 2,
        out_shape=[out, out],
        compiler_params=params(),
        cost_estimate=cost(0, 10 * half * width),
        name="fold_rows",
    )(sums, sums, top, bottom)


def scatter_rows(sums, *others):
    rows = sums.shape[0] // 4
    half = rows // 2
    top = lax.ppermute(sums[3 * rows : 3 * rows + half], "row", y_pairs())
    bottom = lax.ppermute(sums[3 * rows + half :], "row", x_pairs())
    if others:
        top = after(top, *others)
    to_x, to_y = fold_rows(sums, top, bottom)
    return (
        (sums, lax.ppermute(to_x, "row", x_pairs()), lax.ppermute(to_y, "row", y_pairs())),
        to_x,
        to_y,
    )


def chip_moves(columns, moves):
    chips = columns // 2
    return [
        (2 * chip + core, 2 * (chip + moves[core]) + core)
        for chip in range(chips)
        for core in range(2)
        if 0 <= chip + moves[core] < chips
    ]


def swap_cores(values, columns):
    return lax.ppermute(values, "col", [(index, index ^ 1) for index in range(columns)])


def both_cores(values, columns):
    return values, swap_cores(values, columns)


def local_line(
    inputs,
    cotangent,
    image_starts,
    owners,
    query_master,
    query_first,
    query_second,
    output_master,
    output_first,
    output_second,
    gate_master,
    gate_first,
    gate_second,
    down_master,
    down_first,
    down_second,
    vector_master,
    vector_first,
    vector_second,
):
    columns = lax.axis_size("col")
    col_index = lax.axis_index("col")
    row_index = lax.axis_index("row")
    blocks = owners.shape[0]
    block_rows = D // blocks
    head_blocks = query_master.shape[2] // LANES
    codes, order, sorted_slots, head_slots, head_places = plan_blocks(
        owners, jnp.stack([col_index, row_index]), columns, head_blocks
    )
    uneven = codes[UNEVEN] > 0

    inward = chip_moves(columns, (1, -1))
    outward = chip_moves(columns, (-1, 1))

    def spread_out(own, send_codes, keep_codes):
        partner = swap_cores(own, columns)
        sent = pick_blocks(send_codes, 0, 2, [own, partner])
        near = lax.ppermute(sent, "col", inward)

        def farther():
            far = lax.ppermute(pick_blocks(codes, 2, 2, [own, partner]), "col", outward)
            return pick_blocks(keep_codes, 4, 2, [own, partner, near, far])

        kept = lax.cond(
            uneven, farther, lambda: pick_blocks(keep_codes, 4, 2, [own, partner, near])
        )
        return sent, kept.reshape(2 * block_rows, own.shape[2])

    def gather(part):
        return lax.all_gather(part, "col", axis=0, tiled=True)

    def sum_up(gradient):
        own = lax.psum_scatter(gradient, "col", scatter_dimension=0, tiled=True)
        return own.reshape(2, block_rows, own.shape[1])

    def start_home(own):
        return own, lax.ppermute(own, "col", outward)

    def finish_home(own, near, codes):
        held = [own, near, swap_cores(own, columns), swap_cores(near, columns)]

        def farther():
            far = lax.ppermute(own, "col", inward)
            return pick_blocks(codes, 6, CAP, held + [far, swap_cores(far, columns)])

        return lax.cond(uneven, farther, lambda: pick_blocks(codes, 6, CAP, held))

    local_in = inputs[0]
    upstream = cotangent[0]
    row = row_index.reshape(1)
    tables = lane_tables(inputs.shape[1] * 4)
    rates = step_rates()

    query_slabs = [
        jnp.transpose(part, (1, 0, 2)) for part in (query_master, query_first, query_second)
    ]
    query_width = 3 * query_slabs[0].shape[2]
    sent_attention, attention_part = spread_out(
        pack_attention(query_slabs[0], output_master), codes, codes
    )
    plain_one = norm_one(after(order, sent_attention), local_in)
    rows_plain, *plain_parts = share_rows(plain_one)
    w_attention = gather(attention_part)
    w_query, w_output = w_attention[:, :query_width], w_attention[:, query_width:]
    vector_rows = jnp.pad(vector_master.T, ((0, 9), (0, 0))).astype(BF16)
    vector_blocks = jnp.transpose(vector_rows.reshape(16, CAP, block_rows), (1, 0, 2))
    vectors, bias = spread_vectors(
        sorted_slots, head_slots, gather(after(vector_blocks, attention_part, *plain_parts))
    )
    gate_states = [gate_lines(part) for part in (gate_master, gate_first, gate_second)]
    rows_grad = share_rows(order_grad(after(order, rows_plain), upstream))[0]
    rows_one = scale_rows(rows_plain, vectors)
    unused, gate_part = spread_out(
        pack_gate(gate_states[0], gate_master.shape[0]),
        after(codes, vectors),
        after(codes, rows_grad, rows_one),
    )
    w_gate = gather(gate_part)
    mixed = matmul(rows_one, w_query, 1, 0, F32)
    unused, down_part = spread_out(
        pack_flat("pack_down", down_master), after(codes, gate_part), after(codes, mixed)
    )
    w_down = gather(down_part)
    attended, queries, keys, values, logs = attend(
        after(row, down_part), image_starts, mixed, bias, tables
    )
    middle, normed_two = norm_two(
        order, local_in, scatter_rows(matmul(attended, w_output, 1, 1, BF16))[0], vectors
    )
    rows_two = share_rows(normed_two)[0]
    gate, up, hidden = gate_up(rows_two, w_gate)

    down_sums = matmul(rows_grad, hidden, 0, 0, BF16)
    down_own = sum_up(down_sums)
    gate_up_grad = gate_up_back(rows_grad, w_down, after(gate, down_sums), up)
    pulled_two = matmul(gate_up_grad, w_gate, 1, 1, BF16)
    gate_sums = matmul(rows_two, after(gate_up_grad, pulled_two), 0, 0, BF16)
    gate_own = sum_up(gate_sums)
    out_sums = matmul(after(hidden, gate_sums), w_down, 1, 1, BF16)
    middle_grad, low_middle, sums_two = norm_two_back(
        order, upstream, middle, scatter_rows(pulled_two)[0], after(vectors, gate_sums, out_sums)
    )
    rows_mid = share_rows(low_middle)[0]
    down_home = start_home(after(down_own, low_middle))
    attended_grad = matmul(rows_mid, w_output, 1, 0, BF16)
    output_sums = matmul(rows_mid, after(attended, attended_grad), 0, 0, BF16)
    output_own = sum_up(output_sums)
    out_partial, *out_parts = scatter_rows(after(out_sums, rows_mid), output_sums)
    mixed_grad, bias_sums = attend_back(
        after(row, *out_parts),
        image_starts,
        queries,
        keys,
        values,
        logs,
        attended,
        attended_grad,
        tables,
    )
    layer_out = finish_out(order, after(middle, mixed_grad), out_partial)
    pulled_one = matmul(after(mixed_grad, layer_out), w_query, 1, 1, BF16)
    query_sums = matmul(rows_one, after(mixed_grad, pulled_one, down_home[1]), 0, 0, BF16)
    query_own = sum_up(query_sums)
    gate_home = start_home(after(gate_own, query_sums))
    new_down = adam_flat(
        "adam_down",
        codes,
        (down_master, down_first, down_second),
        finish_home(*down_home, after(codes, query_sums)),
        rates[3],
    )
    input_grad, sums_one = norm_one_back(
        order,
        local_in,
        middle_grad,
        scatter_rows(pulled_one)[0],
        after(vectors, new_down[0]),
    )
    vector_sums = place_vector_grads(head_places, sums_one, sums_two, bias_sums)
    for axis, reach in (("row", 1), ("row", 2), ("col", 1), ("col", 2), ("col", 4)):
        vector_sums = vector_sums + lax.ppermute(vector_sums, axis, flips(axis, reach))
    new_gate = [
        gate_unlines(part, gate_master.shape)
        for part in adam_gate(
            codes,
            gate_states,
            finish_home(gate_home[0], after(gate_home[1], input_grad), codes),
            rates[2],
        )
    ]
    output_home = start_home(after(output_own, input_grad))
    new_output = adam_flat(
        "adam_output",
        codes,
        (output_master, output_first, output_second),
        finish_home(output_home[0], after(output_home[1], new_gate[0]), codes),
        rates[1],
    )
    new_vector = [
        part.T
        for part in adam_vector(
            codes,
            [part.T for part in (vector_master, vector_first, vector_second)],
            vector_sums,
            rates[4],
        )
    ]
    query_own = after(query_own, new_output[0], new_vector[0])
    new_query = [
        jnp.transpose(part, (1, 0, 2))
        for part in adam_query(
            codes, query_slabs, finish_home(*start_home(query_own), codes), rates[0]
        )
    ]
    return (
        layer_out[None],
        input_grad[None],
        *new_query,
        *new_output,
        *new_gate,
        *new_down,
        *new_vector,
    )


def solution(mesh):
    one_hop_line = mesh.shape["row"] == 4 and mesh.shape["col"] == 8
    return jax.shard_map(
        local_line if one_hop_line else local,
        mesh=mesh,
        in_specs=(
            P("col", "row", None),
            P("col", "row", None),
            P("col", None),
            P(),
            P("col", None, "row"),
            P("col", None, "row"),
            P("col", None, "row"),
            P("col", "row"),
            P("col", "row"),
            P("col", "row"),
            P("col", None, "row"),
            P("col", None, "row"),
            P("col", None, "row"),
            P("col", "row"),
            P("col", "row"),
            P("col", "row"),
            P("col", None),
            P("col", None),
            P("col", None),
        ),
        out_specs=(
            P("col", "row", None),
            P("col", "row", None),
            P("col", None, "row"),
            P("col", None, "row"),
            P("col", None, "row"),
            P("col", "row"),
            P("col", "row"),
            P("col", "row"),
            P("col", None, "row"),
            P("col", None, "row"),
            P("col", None, "row"),
            P("col", "row"),
            P("col", "row"),
            P("col", "row"),
            P("col", None),
            P("col", None),
            P("col", None),
        ),
        check_vma=False,
    )
```

```python
import math

import jax
import jax.numpy as jnp
import numpy as np
from jax import lax
from jax.experimental import pallas as pl
from jax.experimental.layout import Layout, with_layout_constraint
from jax.experimental.pallas import tpu as pltpu
from jax.sharding import PartitionSpec as P

D = 2048
HEAD_DIM = 64
FF = 5632
ROT = 16
SEQ = 1024
IMG = 256
STEP = 5
CAP = 4

LANES = 128
MIB = 1 << 20

NORM_EPSILON = 1e-05
ADAM_EPSILON = 1e-08
MOMENT_DECAY = 0.5
WEIGHT_DECAY = 0.1
ROTARY_BASE = 10000.0
MASKED_SCORE = -1e30


def owner_slots(owners):
    block_count = owners.shape[0]
    block_order = jnp.arange(block_count, dtype=jnp.int32)
    before = (owners[:, None] == owners[None, :]) & (block_order[None, :] < block_order[:, None])
    return owners * CAP + jnp.sum(before.astype(jnp.int32), axis=1)


def slot_sources(slot_of, slot_count):
    matches = slot_of[None, :] == jnp.arange(slot_count, dtype=jnp.int32)[:, None]
    filled = jnp.any(matches, axis=1)
    numbers = jnp.arange(slot_of.shape[0], dtype=jnp.int32)
    source = jnp.sum(jnp.where(matches, numbers[None, :], 0), axis=1)
    return (source, filled)


def unpack(gathered, slot_of, block_rows):
    shaped = gathered.reshape((-1, block_rows) + gathered.shape[1:])
    return jnp.take(shaped, slot_of, axis=0).reshape((-1,) + gathered.shape[1:])


def own_blocks(gradient, own_source, block_rows):
    shaped = gradient.reshape((-1, block_rows) + gradient.shape[1:])
    return jnp.take(shaped, own_source, axis=0).reshape((-1,) + gradient.shape[1:])


def normalize(values):
    center = jnp.mean(values, axis=-1, keepdims=True)
    spread = jnp.mean(values * values, axis=-1, keepdims=True) - center * center
    inverse = lax.rsqrt(spread + NORM_EPSILON)
    return ((values - center) * inverse, inverse)


def norm_back(upstream, plain_rows, inverse, gain_row):
    scaled = upstream * gain_row
    return inverse * (
        scaled
        - jnp.mean(scaled, axis=-1, keepdims=True)
        - plain_rows * jnp.mean(scaled * plain_rows, axis=-1, keepdims=True)
    )


def rotary_tables(seq_len):
    half_rot = ROT // 2
    frequency = ROTARY_BASE ** (-2.0 * jnp.arange(half_rot, dtype=jnp.float32) / ROT)
    angles = jnp.arange(seq_len, dtype=jnp.float32)[:, None] * frequency[None, :]
    return (jnp.cos(angles), jnp.sin(angles))


def rotate(values, cosine_table, sine_table):
    half_rot = ROT // 2
    first_half = values[..., :half_rot]
    second_half = values[..., half_rot:ROT]
    cosine_part = cosine_table[:, None, :]
    sine_part = sine_table[:, None, :]
    return jnp.concatenate(
        [
            first_half * cosine_part - second_half * sine_part,
            second_half * cosine_part + first_half * sine_part,
            values[..., ROT:],
        ],
        axis=-1,
    )


def rotate_back(values, cosine_table, sine_table):
    half_rot = ROT // 2
    first_half = values[..., :half_rot]
    second_half = values[..., half_rot:ROT]
    cosine_part = cosine_table[:, None, :]
    sine_part = sine_table[:, None, :]
    return jnp.concatenate(
        [
            first_half * cosine_part + second_half * sine_part,
            second_half * cosine_part - first_half * sine_part,
            values[..., ROT:],
        ],
        axis=-1,
    )


def block_ids(starts, seq_len):
    positions = jnp.arange(seq_len, dtype=jnp.int32)
    inside = (positions[None, :] >= starts[:, None]) & (positions[None, :] < starts[:, None] + IMG)
    numbers = jnp.arange(1, starts.shape[0] + 1, dtype=jnp.int32)
    return jnp.sum(jnp.where(inside, numbers[:, None], 0), axis=0)


def adam_step(master, first_state, second_state, gradient, keep_rows, rate):
    new_first = MOMENT_DECAY * first_state + (1.0 - MOMENT_DECAY) * gradient
    new_second = MOMENT_DECAY * second_state + (1.0 - MOMENT_DECAY) * gradient * gradient
    correction = 1.0 - MOMENT_DECAY**STEP
    direction = new_first / correction / (jnp.sqrt(new_second / correction) + ADAM_EPSILON)
    new_master = master - rate * (direction + WEIGHT_DECAY * master)
    keep_mask = keep_rows.reshape(keep_rows.shape + (1,) * (master.ndim - 1))
    return (
        jnp.where(keep_mask, new_master, master),
        jnp.where(keep_mask, new_first, first_state),
        jnp.where(keep_mask, new_second, second_state),
    )


def step_rates():
    return (
        2.0 / math.sqrt(D),
        2.0 / math.sqrt(D * 16 // SEQ),
        2.0 / math.sqrt(D),
        2.0 / math.sqrt(FF),
        0.5,
    )


def local(
    inputs,
    cotangent,
    image_starts,
    owners,
    query_master,
    query_first,
    query_second,
    output_master,
    output_first,
    output_second,
    gate_master,
    gate_first,
    gate_second,
    down_master,
    down_first,
    down_second,
    vector_master,
    vector_first,
    vector_second,
):
    columns = lax.axis_size("col")
    col_index = lax.axis_index("col")
    row_index = lax.axis_index("row")
    block_rows = D // owners.shape[0]
    slot_of = owner_slots(owners)
    source, filled = slot_sources(slot_of, CAP * columns)
    shared = (
        lax.all_gather(query_master.astype(jnp.bfloat16), "col", axis=0, tiled=True),
        lax.all_gather(output_master.astype(jnp.bfloat16), "col", axis=0, tiled=True),
        lax.all_gather(gate_master.astype(jnp.bfloat16), "col", axis=0, tiled=True),
        lax.all_gather(down_master.astype(jnp.bfloat16), "col", axis=0, tiled=True),
        lax.all_gather(vector_master.astype(jnp.bfloat16), "col", axis=0, tiled=True),
    )
    w_query = unpack(shared[0], slot_of, block_rows)
    w_output = unpack(shared[1], slot_of, block_rows)
    w_gate = unpack(shared[2], slot_of, block_rows)
    w_down = unpack(shared[3], slot_of, block_rows)
    vectors = unpack(shared[4], slot_of, block_rows).astype(jnp.float32)
    local_in = inputs[0]
    width = local_in.shape[1]
    head_cols = w_query.shape[2]
    local_heads = head_cols // HEAD_DIM
    score_scale = 1.0 / math.sqrt(HEAD_DIM)
    qkv_bias = lax.dynamic_slice_in_dim(vectors[:, 4:7], row_index * head_cols, head_cols, 0).T
    plain_one, inverse_one = normalize(local_in)
    normed_one = (plain_one * vectors[:, 0] + vectors[:, 1]).astype(jnp.bfloat16)
    rows_one = lax.all_gather(normed_one, "row", axis=0, tiled=True)
    seq_len = rows_one.shape[0]
    mixed_proj = (
        jnp.einsum("td,djh->tjh", rows_one, w_query, preferred_element_type=jnp.float32)
        + qkv_bias[None]
    )
    cosine_table, sine_table = rotary_tables(seq_len)
    queries = rotate(
        mixed_proj[:, 0].reshape(seq_len, local_heads, HEAD_DIM), cosine_table, sine_table
    ).astype(jnp.bfloat16)
    key_rows = rotate(
        mixed_proj[:, 1].reshape(seq_len, local_heads, HEAD_DIM), cosine_table, sine_table
    ).astype(jnp.bfloat16)
    value_rows = mixed_proj[:, 2].reshape(seq_len, local_heads, HEAD_DIM).astype(jnp.bfloat16)
    labels = block_ids(image_starts[0], seq_len)
    block_size = min(512, seq_len)
    block_count = seq_len // block_size
    positions = jnp.arange(seq_len, dtype=jnp.int32)

    def scores_at(first_row):
        row_pos = first_row + jnp.arange(block_size, dtype=jnp.int32)
        row_label = lax.dynamic_slice_in_dim(labels, first_row, block_size, 0)
        allowed = (positions[None, :] <= row_pos[:, None]) | (
            row_label[:, None] == labels[None, :]
        ) & (row_label[:, None] > 0)
        query_rows = lax.dynamic_slice_in_dim(queries, first_row, block_size, 0)
        raw_scores = (
            jnp.einsum("qhe,khe->hqk", query_rows, key_rows, preferred_element_type=jnp.float32)
            * score_scale
        )
        return (jnp.where(allowed[None], raw_scores, MASKED_SCORE), query_rows)

    def forward_block(block_index):
        scores, query_rows = scores_at(block_index * block_size)
        row_peak = jnp.max(scores, axis=-1, keepdims=True)
        powers = jnp.exp(scores - row_peak)
        row_total = jnp.sum(powers, axis=-1, keepdims=True)
        weights = (powers / row_total).astype(jnp.bfloat16)
        output = jnp.einsum("hqk,khe->qhe", weights, value_rows, preferred_element_type=jnp.float32)
        return (output, (row_peak + jnp.log(row_total))[..., 0])

    output_blocks, log_totals = lax.map(forward_block, jnp.arange(block_count, dtype=jnp.int32))
    attended = output_blocks.reshape(seq_len, head_cols).astype(jnp.bfloat16)
    picked_rows = attended
    middle = local_in + lax.psum_scatter(
        jnp.einsum("th,dh->td", picked_rows, w_output, preferred_element_type=jnp.float32),
        "row",
        scatter_dimension=0,
        tiled=True,
    )
    plain_two, inverse_two = normalize(middle)
    normed_two = (plain_two * vectors[:, 2] + vectors[:, 3]).astype(jnp.bfloat16)
    rows_two = lax.all_gather(normed_two, "row", axis=0, tiled=True)
    gate_up = jnp.einsum("td,djf->tjf", rows_two, w_gate, preferred_element_type=jnp.float32)
    gate_part = gate_up[:, 0]
    up_part = gate_up[:, 1]
    gate_sigmoid = jax.nn.sigmoid(gate_part)
    activated = gate_part * gate_sigmoid
    hidden = (activated * up_part).astype(jnp.bfloat16)
    picked_rows = hidden
    layer_out = middle + lax.psum_scatter(
        jnp.einsum("tf,df->td", picked_rows, w_down, preferred_element_type=jnp.float32).astype(
            jnp.bfloat16
        ),
        "row",
        scatter_dimension=0,
        tiled=True,
    ).astype(jnp.float32)
    upstream = cotangent[0]
    rows_grad = lax.all_gather(upstream.astype(jnp.bfloat16), "row", axis=0, tiled=True)
    hidden_grad = jnp.einsum("td,df->tf", rows_grad, w_down, preferred_element_type=jnp.float32)
    down_grad = jnp.einsum("tf,td->df", hidden, rows_grad, preferred_element_type=jnp.float32)
    gate_grad = hidden_grad * up_part * gate_sigmoid * (1.0 + gate_part * (1.0 - gate_sigmoid))
    up_grad = hidden_grad * activated
    gate_up_grad = jnp.stack([gate_grad, up_grad], axis=1).astype(jnp.bfloat16)
    gate_weight_grad = jnp.einsum(
        "td,tjf->djf", rows_two, gate_up_grad, preferred_element_type=jnp.float32
    )
    picked_rows = gate_up_grad
    normed_two_grad = lax.psum_scatter(
        jnp.einsum("tjf,djf->td", picked_rows, w_gate, preferred_element_type=jnp.float32),
        "row",
        scatter_dimension=0,
        tiled=True,
    )
    middle_grad = upstream + norm_back(normed_two_grad, plain_two, inverse_two, vectors[:, 2])
    rows_mid = lax.all_gather(middle_grad.astype(jnp.bfloat16), "row", axis=0, tiled=True)
    attended_grad = jnp.einsum(
        "td,dh->th", rows_mid, w_output, preferred_element_type=jnp.float32
    ).astype(jnp.bfloat16)
    output_grad = jnp.einsum("th,td->dh", attended, rows_mid, preferred_element_type=jnp.float32)
    head_grad = attended_grad.reshape(seq_len, local_heads, HEAD_DIM)

    def backward_block(running, block_index):
        key_total, value_total = running
        first_row = block_index * block_size
        scores, query_rows = scores_at(first_row)
        probabilities = jnp.exp(scores - log_totals[block_index][..., None])
        row_grad = lax.dynamic_slice_in_dim(head_grad, first_row, block_size, 0)
        prob_grad = jnp.einsum(
            "qhe,khe->hqk", row_grad, value_rows, preferred_element_type=jnp.float32
        )
        inner = jnp.sum(prob_grad * probabilities, axis=-1, keepdims=True)
        score_grad = (probabilities * (prob_grad - inner)).astype(jnp.bfloat16)
        query_grad = (
            jnp.einsum("hqk,khe->qhe", score_grad, key_rows, preferred_element_type=jnp.float32)
            * score_scale
        )
        key_total = (
            key_total
            + jnp.einsum("hqk,qhe->khe", score_grad, query_rows, preferred_element_type=jnp.float32)
            * score_scale
        )
        value_total = value_total + jnp.einsum(
            "hqk,qhe->khe",
            probabilities.astype(jnp.bfloat16),
            row_grad,
            preferred_element_type=jnp.float32,
        )
        return ((key_total, value_total), query_grad)

    empty_heads = jnp.zeros((seq_len, local_heads, HEAD_DIM), jnp.float32)
    (key_grad, value_grad), query_blocks = lax.scan(
        backward_block, (empty_heads, empty_heads), jnp.arange(block_count, dtype=jnp.int32)
    )
    query_grad = query_blocks.reshape(seq_len, local_heads, HEAD_DIM)
    mixed_grad = jnp.stack(
        [
            rotate_back(query_grad, cosine_table, sine_table).reshape(seq_len, head_cols),
            rotate_back(key_grad, cosine_table, sine_table).reshape(seq_len, head_cols),
            value_grad.reshape(seq_len, head_cols),
        ],
        axis=1,
    ).astype(jnp.bfloat16)
    bias_grad = jnp.sum(mixed_grad, axis=0, dtype=jnp.float32)
    query_weight_grad = jnp.einsum(
        "td,tjh->djh", rows_one, mixed_grad, preferred_element_type=jnp.float32
    )
    picked_rows = mixed_grad
    normed_one_grad = lax.psum_scatter(
        jnp.einsum("tjh,djh->td", picked_rows, w_query, preferred_element_type=jnp.float32).astype(
            jnp.bfloat16
        ),
        "row",
        scatter_dimension=0,
        tiled=True,
    ).astype(jnp.float32)
    input_grad = middle_grad + norm_back(normed_one_grad, plain_one, inverse_one, vectors[:, 0])
    norm_grads = jnp.stack(
        [
            jnp.sum(normed_one_grad * plain_one, axis=0),
            jnp.sum(normed_one_grad, axis=0),
            jnp.sum(normed_two_grad * plain_two, axis=0),
            jnp.sum(normed_two_grad, axis=0),
        ],
        axis=1,
    )
    placed = lax.dynamic_update_slice_in_dim(
        jnp.zeros((width, 3), jnp.float32), bias_grad.T, row_index * head_cols, 0
    )
    vector_grad = lax.psum(
        jnp.concatenate([norm_grads, placed], axis=1).astype(jnp.bfloat16), "row"
    )
    own_filled = lax.dynamic_slice_in_dim(filled, col_index * CAP, CAP, 0)
    own_source = lax.dynamic_slice_in_dim(source, col_index * CAP, CAP, 0)
    summed = (
        lax.psum(query_weight_grad.astype(jnp.bfloat16), "col").astype(jnp.float32),
        lax.psum(output_grad.astype(jnp.bfloat16), "col").astype(jnp.float32),
        lax.psum(gate_weight_grad.astype(jnp.bfloat16), "col").astype(jnp.float32),
        lax.psum(down_grad.astype(jnp.bfloat16), "col").astype(jnp.float32),
        lax.psum(vector_grad, "col").astype(jnp.float32),
    )
    owned_grads = tuple((own_blocks(whole_grad, own_source, block_rows) for whole_grad in summed))
    keep_rows = jnp.repeat(own_filled, block_rows)
    masters = (query_master, output_master, gate_master, down_master, vector_master)
    firsts = (query_first, output_first, gate_first, down_first, vector_first)
    seconds = (query_second, output_second, gate_second, down_second, vector_second)
    rates = step_rates()
    updated = [
        adam_step(
            masters[kind_index],
            firsts[kind_index],
            seconds[kind_index],
            owned_grads[kind_index],
            keep_rows,
            rates[kind_index],
        )
        for kind_index in range(5)
    ]
    return (
        layer_out[None],
        input_grad[None],
        updated[0][0],
        updated[0][1],
        updated[0][2],
        updated[1][0],
        updated[1][1],
        updated[1][2],
        updated[2][0],
        updated[2][1],
        updated[2][2],
        updated[3][0],
        updated[3][1],
        updated[3][2],
        updated[4][0],
        updated[4][1],
        updated[4][2],
    )


BF16 = jnp.bfloat16
F32 = jnp.float32


def smem():
    return pl.BlockSpec(memory_space=pltpu.SMEM)


def params(mib=16):
    return pltpu.CompilerParams(vmem_limit_bytes=mib * MIB)


def cost(flops, nbytes, powers=0):
    return pl.CostEstimate(flops=int(flops), bytes_accessed=int(nbytes), transcendentals=int(powers))


def lane_block(number):
    return pl.ds(pl.multiple_of(number * LANES, LANES), LANES)


def after(value, *others):
    return lax.optimization_barrier((value, *others))[0]


LIVE, PLACES, UNEVEN, TABLE = 10, 14, 18, 32


def plan_blocks(owners, places, columns, head_blocks):
    blocks = owners.shape[0]
    half = blocks // (columns // 2)

    def kernel(owner_ref, at_ref, table_ref, order_ref, sorted_ref, head_slot_ref, head_ref):
        held = [owner_ref[block] for block in range(blocks)]
        col, row = at_ref[0], at_ref[1]
        chip = lax.shift_right_logical(col, 1)
        core = jnp.bitwise_and(col, 1)

        def total(flags):
            return sum(flag.astype(jnp.int32) for flag in flags)

        def below(index):
            return total(owner < index for owner in held)

        for block in range(blocks):
            rank = total(held[other] == held[block] for other in range(block)) + jnp.int32(0)
            place = below(held[block]) + rank
            slot = held[block] * CAP + rank
            order_ref[place] = jnp.int32(block)
            sorted_ref[place] = slot
            head = block - row * head_blocks

            @pl.when((head >= 0) & (head < head_blocks))
            def mine(head=head, slot=slot, place=place):
                head_slot_ref[head] = slot
                head_ref[head] = place

        first = below(2 * chip)
        middle = below(2 * chip + 1)
        end = below(2 * chip + 2)
        own_first = below(col)
        own_count = below(col + 1) - own_first

        def chip_code(place):
            second = place >= middle
            rank = place - jnp.where(second, middle, first)
            code = jnp.where(second.astype(jnp.int32) == core, 0, 16) + rank
            return jnp.where((place >= first) & (place < end), code, 0)

        toward = 1 - 2 * core
        for index in range(2):
            offset = 2 * core + index
            table_ref[index] = chip_code(half * (chip + toward) + offset)
            table_ref[2 + index] = chip_code(half * (chip - toward) + offset)
            kept = half * chip + offset
            near, far = 32 + index, 48 + index
            table_ref[4 + index] = jnp.where(
                kept < first,
                jnp.where(core == 0, near, far),
                jnp.where(kept >= end, jnp.where(core == 0, far, near), chip_code(kept)),
            )
        for rank in range(CAP):
            live = rank < own_count
            place = own_first + jnp.minimum(rank, own_count - 1)
            there = lax.shift_right_logical(place, 2)
            side = there - chip
            other = lax.shift_right_logical(place - half * there, 1)
            near_side = 1 - 2 * other
            same = other == core
            source = jnp.where(
                side == 0,
                jnp.where(same, 0, 2),
                jnp.where(side == near_side, jnp.where(same, 1, 3), jnp.where(same, 4, 5)),
            )
            table_ref[6 + rank] = 16 * source + jnp.bitwise_and(place, 1)
            table_ref[LIVE + rank] = live.astype(jnp.int32)
            table_ref[PLACES + rank] = place
        widest = jnp.int32(0)
        for number in range(1, columns // 2):
            widest = jnp.maximum(widest, jnp.abs(below(2 * number) - half * number))
        table_ref[UNEVEN] = jnp.clip(widest - 2, 0, 2)
        table_ref[UNEVEN + 1] = chip_code(half * (chip - toward) + 1 + core)
        for index in range(UNEVEN + 2, TABLE):
            table_ref[index] = jnp.int32(0)

    def ints(size):
        return jax.ShapeDtypeStruct((size,), jnp.int32)

    return pl.pallas_call(
        kernel,
        in_specs=[smem(), smem()],
        out_specs=[smem()] * 5,
        out_shape=[ints(TABLE), ints(blocks), ints(blocks), ints(head_blocks), ints(head_blocks)],
        compiler_params=params(),
        name="plan_blocks",
    )(owners, places)


def pack_attention(slabs, output):
    kinds, rows, width = slabs.shape
    block = rows // CAP
    total = kinds * width + output.shape[1]

    def kernel(in_ref, output_ref, out_ref):
        for kind in range(kinds):
            out_ref[0, :, kind * width : (kind + 1) * width] = in_ref[kind].astype(BF16)
        out_ref[0, :, kinds * width :] = output_ref[...].astype(BF16)

    return pl.pallas_call(
        kernel,
        grid=(CAP,),
        in_specs=[
            pl.BlockSpec((kinds, block, width), lambda s: (0, s, 0)),
            pl.BlockSpec((block, output.shape[1]), lambda s: (s, 0)),
        ],
        out_specs=pl.BlockSpec((1, block, total), lambda s: (s, 0, 0)),
        out_shape=jax.ShapeDtypeStruct((CAP, block, total), BF16),
        compiler_params=params(58),
        cost_estimate=cost(0, 6 * rows * total),
        name="pack_attention",
    )(slabs, output)


def after(value, *others):
    return lax.optimization_barrier((value, *others))[0]


def gate_lines(values):
    rows, kinds, width = values.shape
    split = with_layout_constraint(
        values.reshape(rows, kinds, width // LANES, LANES), Layout(major_to_minor=(0, 2, 1, 3))
    )
    return jnp.transpose(split, (0, 2, 1, 3)).reshape(rows * kinds * width // LANES, LANES)


def gate_unlines(lines, shape):
    rows, kinds, width = shape
    split = jnp.transpose(lines.reshape(rows, width // LANES, kinds, LANES), (0, 2, 1, 3))
    return with_layout_constraint(split, Layout(major_to_minor=(0, 2, 1, 3))).reshape(shape)


def pack_flat(name, master):
    rows, width = master.shape
    block = rows // CAP

    def kernel(in_ref, out_ref):
        out_ref[0] = in_ref[...].astype(BF16)

    return pl.pallas_call(
        kernel,
        grid=(CAP,),
        in_specs=[pl.BlockSpec((block, width), lambda s: (s, 0))],
        out_specs=pl.BlockSpec((1, block, width), lambda s: (s, 0, 0)),
        out_shape=jax.ShapeDtypeStruct((CAP, block, width), BF16),
        compiler_params=params(),
        cost_estimate=cost(0, 6 * rows * width),
        name=name,
    )(master)


def pack_gate(lines, rows):
    block = rows // CAP
    tiles = lines.shape[0] // rows

    def kernel(in_ref, out_ref):
        for tile in range(tiles):
            out_ref[0, :, tile * LANES : (tile + 1) * LANES] = in_ref[
                pl.ds(tile, block, stride=tiles), :
            ].astype(BF16)

    return pl.pallas_call(
        kernel,
        grid=(CAP,),
        in_specs=[pl.BlockSpec((block * tiles, LANES), lambda s: (s, 0))],
        out_specs=pl.BlockSpec((1, block, tiles * LANES), lambda s: (s, 0, 0)),
        out_shape=jax.ShapeDtypeStruct((CAP, block, tiles * LANES), BF16),
        compiler_params=params(58),
        cost_estimate=cost(0, 6 * lines.size),
        name="pack_gate",
    )(lines)


def pick_blocks(codes, first, count, sources):
    shape = sources[0].shape[1:]

    def kernel(code_ref, *refs):
        ins, out, sems = refs[: len(sources)], refs[-2], refs[-1]
        for place in range(count):
            code = code_ref[first + place]
            index = jnp.bitwise_and(code, 15)
            origin = lax.shift_right_logical(code, 4)
            for number, source in enumerate(ins):

                @pl.when(origin == number)
                def start(source=source, index=index, place=place):
                    held = source.at[index if source.shape[0] > 1 else 0]
                    pltpu.make_async_copy(held, out.at[place], sems.at[place]).start()

        for place in range(count):
            pltpu.make_async_copy(ins[0].at[0], out.at[place], sems.at[place]).wait()

    moved = count * shape[0] * shape[1]
    return pl.pallas_call(
        kernel,
        in_specs=[smem()] + [pl.BlockSpec(memory_space=pl.ANY)] * len(sources),
        out_specs=pl.BlockSpec(memory_space=pltpu.VMEM),
        out_shape=jax.ShapeDtypeStruct((count, *shape), BF16),
        scratch_shapes=[pltpu.SemaphoreType.DMA((count,))],
        compiler_params=params(),
        cost_estimate=cost(0, 4 * moved),
        name="pick_blocks",
    )(codes, *sources)


def row_blocks(height, width, first=0):
    return pl.BlockSpec((height, width), lambda i: (i + first, 0))


def whole(height, width):
    return pl.BlockSpec((height, width), lambda i: (0, 0))


NORM_ROWS = 64


def statistics(values):
    center = jnp.mean(values, axis=-1, keepdims=True)
    spread = jnp.mean(values * values, axis=-1, keepdims=True) - center * center
    return center, lax.rsqrt(spread + NORM_EPSILON)


def order_grad(order, cotangent):
    rows, width = cotangent.shape

    def kernel(order_ref, in_ref, out_ref):
        for place in range(width // LANES):
            out_ref[:, place * LANES : (place + 1) * LANES] = in_ref[
                :, lane_block(order_ref[place])
            ].astype(BF16)

    return pl.pallas_call(
        kernel,
        grid=(rows // NORM_ROWS,),
        in_specs=[smem(), row_blocks(NORM_ROWS, width)],
        out_specs=row_blocks(NORM_ROWS, width),
        out_shape=jax.ShapeDtypeStruct((rows, width), BF16),
        compiler_params=params(),
        cost_estimate=cost(0, 6 * rows * width),
        name="order_grad",
    )(order, cotangent)


def norm_one(order, inputs):
    rows, width = inputs.shape

    def kernel(order_ref, in_ref, out_ref):
        center, inverse = statistics(in_ref[...])
        for place in range(width // LANES):
            span = slice(place * LANES, (place + 1) * LANES)
            plain = (in_ref[:, lane_block(order_ref[place])] - center) * inverse
            out_ref[:, span] = plain.astype(BF16)

    return pl.pallas_call(
        kernel,
        grid=(rows // NORM_ROWS,),
        in_specs=[smem(), row_blocks(NORM_ROWS, width)],
        out_specs=row_blocks(NORM_ROWS, width),
        out_shape=jax.ShapeDtypeStruct((rows, width), BF16),
        compiler_params=params(),
        cost_estimate=cost(0, 6 * rows * width),
        name="norm_one",
    )(order, inputs)


def scale_rows(plain, vectors):
    rows, width = plain.shape
    tile = 256

    def kernel(in_ref, vec_ref, out_ref):
        out_ref[...] = (in_ref[...].astype(F32) * vec_ref[0:1, :] + vec_ref[1:2, :]).astype(BF16)

    return pl.pallas_call(
        kernel,
        grid=(rows // tile,),
        in_specs=[row_blocks(tile, width), whole(8, width)],
        out_specs=row_blocks(tile, width),
        out_shape=jax.ShapeDtypeStruct((rows, width), BF16),
        compiler_params=params(),
        cost_estimate=cost(0, 4 * rows * width),
        name="scale_rows",
    )(plain, vectors)


def norm_two(order, inputs, partial, vectors):
    rows, width = inputs.shape
    own, from_x, from_y = partial

    def kernel(order_ref, in_ref, own_ref, x_ref, y_ref, vec_ref, mid_ref, out_ref):
        for place in range(width // LANES):
            span = slice(place * LANES, (place + 1) * LANES)
            mid_ref[:, span] = (
                in_ref[:, lane_block(order_ref[place])]
                + own_ref[:, span].astype(F32)
                + x_ref[:, span].astype(F32)
                + y_ref[:, span].astype(F32)
            )
        middle = mid_ref[...]
        center, inverse = statistics(middle)
        plain = (middle - center) * inverse
        out_ref[...] = (plain * vec_ref[2:3, :] + vec_ref[3:4, :]).astype(BF16)

    spec = row_blocks(NORM_ROWS, width)
    return pl.pallas_call(
        kernel,
        grid=(rows // NORM_ROWS,),
        in_specs=[smem(), spec, spec, spec, spec, whole(8, width)],
        out_specs=[spec, spec],
        out_shape=[
            jax.ShapeDtypeStruct((rows, width), F32),
            jax.ShapeDtypeStruct((rows, width), BF16),
        ],
        compiler_params=params(),
        cost_estimate=cost(0, 16 * rows * width),
        name="norm_two",
    )(order, inputs, own, from_x, from_y, vectors)


def finish_out(order, middle, partial):
    rows, width = middle.shape
    own, from_x, from_y = partial

    def kernel(order_ref, mid_ref, own_ref, x_ref, y_ref, out_ref):
        for place in range(width // LANES):
            span = slice(place * LANES, (place + 1) * LANES)
            out_ref[:, lane_block(order_ref[place])] = (
                mid_ref[:, span]
                + own_ref[:, span].astype(F32)
                + x_ref[:, span].astype(F32)
                + y_ref[:, span].astype(F32)
            )

    spec = row_blocks(NORM_ROWS, width)
    return pl.pallas_call(
        kernel,
        grid=(rows // NORM_ROWS,),
        in_specs=[smem(), spec, spec, spec, spec],
        out_specs=spec,
        out_shape=jax.ShapeDtypeStruct((rows, width), F32),
        compiler_params=params(),
        cost_estimate=cost(0, 14 * rows * width),
        name="finish_out",
    )(order, middle, own, from_x, from_y)


def norm_pull(upstream, plain, inverse, gain):
    scaled = upstream * gain
    return inverse * (
        scaled
        - jnp.mean(scaled, axis=-1, keepdims=True)
        - plain * jnp.mean(scaled * plain, axis=-1, keepdims=True)
    )


def add_sums(sum_ref, upstream, plain):
    @pl.when(pl.program_id(0) == 0)
    def clear():
        sum_ref[...] = jnp.zeros_like(sum_ref)

    sum_ref[0:1, :] += jnp.sum(upstream * plain, axis=0, keepdims=True)
    sum_ref[1:2, :] += jnp.sum(upstream, axis=0, keepdims=True)


def norm_two_back(order, cotangent, middle, partial, vectors):
    rows, width = middle.shape
    own, from_x, from_y = partial

    def kernel(
        order_ref, cot_ref, mid_ref, own_ref, x_ref, y_ref, vec_ref, grad_ref, low_ref, sum_ref
    ):
        middle_rows = mid_ref[...]
        center, inverse = statistics(middle_rows)
        plain = (middle_rows - center) * inverse
        upstream = own_ref[...].astype(F32) + x_ref[...].astype(F32) + y_ref[...].astype(F32)
        add_sums(sum_ref, upstream, plain)
        grad_ref[...] = norm_pull(upstream, plain, inverse, vec_ref[2:3, :])
        for place in range(width // LANES):
            span = slice(place * LANES, (place + 1) * LANES)
            total = grad_ref[:, span] + cot_ref[:, lane_block(order_ref[place])]
            grad_ref[:, span] = total
            low_ref[:, span] = total.astype(BF16)

    spec = row_blocks(NORM_ROWS, width)
    return pl.pallas_call(
        kernel,
        grid=(rows // NORM_ROWS,),
        in_specs=[smem(), spec, spec, spec, spec, spec, whole(8, width)],
        out_specs=[spec, spec, whole(8, width)],
        out_shape=[
            jax.ShapeDtypeStruct((rows, width), F32),
            jax.ShapeDtypeStruct((rows, width), BF16),
            jax.ShapeDtypeStruct((8, width), F32),
        ],
        compiler_params=params(),
        cost_estimate=cost(0, 20 * rows * width),
        name="norm_two_back",
    )(order, cotangent, middle, own, from_x, from_y, vectors)


def norm_one_back(order, inputs, middle_grad, partial, vectors):
    rows, width = inputs.shape
    own, from_x, from_y = partial

    def kernel(
        order_ref,
        in_ref,
        mid_ref,
        own_ref,
        x_ref,
        y_ref,
        vec_ref,
        out_ref,
        sum_ref,
        plain_ref,
        pull_ref,
    ):
        center, inverse = statistics(in_ref[...])
        for place in range(width // LANES):
            span = slice(place * LANES, (place + 1) * LANES)
            plain_ref[:, span] = (in_ref[:, lane_block(order_ref[place])] - center) * inverse
        plain = plain_ref[...]
        upstream = own_ref[...].astype(F32) + x_ref[...].astype(F32) + y_ref[...].astype(F32)
        add_sums(sum_ref, upstream, plain)
        pull_ref[...] = norm_pull(upstream, plain, inverse, vec_ref[0:1, :])
        for place in range(width // LANES):
            span = slice(place * LANES, (place + 1) * LANES)
            out_ref[:, lane_block(order_ref[place])] = mid_ref[:, span] + pull_ref[:, span]

    spec = row_blocks(NORM_ROWS, width)
    return pl.pallas_call(
        kernel,
        grid=(rows // NORM_ROWS,),
        in_specs=[smem(), spec, spec, spec, spec, spec, whole(8, width)],
        out_specs=[spec, whole(8, width)],
        out_shape=[
            jax.ShapeDtypeStruct((rows, width), F32),
            jax.ShapeDtypeStruct((8, width), F32),
        ],
        scratch_shapes=[pltpu.VMEM((NORM_ROWS, width), F32), pltpu.VMEM((NORM_ROWS, width), F32)],
        compiler_params=params(),
        cost_estimate=cost(0, 18 * rows * width),
        name="norm_one_back",
    )(order, inputs, middle_grad, own, from_x, from_y, vectors)


def spread_vectors(sorted_slots, head_slots, gathered):
    places = sorted_slots.shape[0]
    heads = head_slots.shape[0]

    def kernel(sorted_ref, head_ref, in_ref, vec_ref, bias_ref):
        for place in range(places):
            vec_ref[:, place * LANES : (place + 1) * LANES] = in_ref[sorted_ref[place]].astype(F32)
        for place in range(heads):
            bias_ref[:, place * LANES : (place + 1) * LANES] = in_ref[head_ref[place]].astype(F32)

    return pl.pallas_call(
        kernel,
        in_specs=[smem(), smem(), pl.BlockSpec(memory_space=pltpu.VMEM)],
        out_shape=[
            jax.ShapeDtypeStruct((16, places * LANES), F32),
            jax.ShapeDtypeStruct((16, heads * LANES), F32),
        ],
        compiler_params=params(),
        name="spread_vectors",
    )(sorted_slots, head_slots, gathered)


def place_vector_grads(head_places, sums_one, sums_two, bias_sums):
    heads = head_places.shape[0]

    def kernel(head_ref, one_ref, two_ref, bias_ref, out_ref):
        out_ref[0:2, :] = one_ref[0:2, :]
        out_ref[2:4, :] = two_ref[0:2, :]
        out_ref[4:8, :] = jnp.zeros((4, out_ref.shape[1]), F32)
        for place in range(heads):
            for kind in range(3):
                first = (kind * heads + place) * LANES
                out_ref[4 + kind : 5 + kind, lane_block(head_ref[place])] = bias_ref[
                    0:1, first : first + LANES
                ]

    return pl.pallas_call(
        kernel,
        in_specs=[smem()] + [pl.BlockSpec(memory_space=pltpu.VMEM)] * 3,
        out_shape=jax.ShapeDtypeStruct(sums_one.shape, F32),
        compiler_params=params(),
        name="place_vector_grads",
    )(head_places, sums_one, sums_two, bias_sums)


def adam_vector(keep, states, gradient, rate):
    kinds, rows = states[0].shape
    block = rows // CAP

    def kernel(keep_ref, m_ref, f_ref, s_ref, g_ref, mo_ref, fo_ref, so_ref):
        for slot in range(CAP):
            span = slice(slot * block, (slot + 1) * block)
            grad = g_ref[:, lane_block(keep_ref[PLACES + slot])][:kinds]
            mo_ref[:, span], fo_ref[:, span], so_ref[:, span] = adam_update(
                m_ref[:, span], f_ref[:, span], s_ref[:, span], grad, keep_ref[LIVE + slot] > 0, rate
            )

    return pl.pallas_call(
        kernel,
        in_specs=[smem()] + [pl.BlockSpec(memory_space=pltpu.VMEM)] * 4,
        out_shape=[jax.ShapeDtypeStruct(states[0].shape, F32)] * 3,
        compiler_params=params(),
        name="adam_vector",
    )(keep, *states, gradient)


def lane_tables(seq_len):
    half = ROT // 2
    frequency = (ROTARY_BASE ** (-2.0 * np.arange(half, dtype=np.float32) / ROT)).astype(np.float32)
    angles = np.arange(seq_len, dtype=np.float32)[:, None] * frequency[None, :]
    cosine = np.cos(angles).astype(np.float32)
    sine = np.sin(angles).astype(np.float32)
    rest = HEAD_DIM - ROT
    ones = np.ones((seq_len, rest), np.float32)
    none = np.zeros((seq_len, rest), np.float32)
    blank = np.zeros((seq_len, half), np.float32)
    keep = np.concatenate([cosine, cosine, ones], axis=1)
    lower = np.concatenate([-sine, blank, none], axis=1)
    upper = np.concatenate([blank, sine, none], axis=1)
    return tuple(jnp.asarray(np.concatenate([table, table], axis=1)) for table in (keep, lower, upper))


def turn(values, keep, lower, upper):
    half = ROT // 2
    return (
        values * keep
        + pltpu.roll(values, LANES - half, 1) * lower
        + pltpu.roll(values, half, 1) * upper
    )


def head_mask(rows, head):
    lanes = lax.broadcasted_iota(jnp.int32, (rows, LANES), 1)
    return (lanes // HEAD_DIM) == head


def dot_nt(left, right):
    return lax.dot_general(left, right, (((1,), (1,)), ((), ())), preferred_element_type=F32)


def dot_nn(left, right):
    return lax.dot_general(left, right, (((1,), (0,)), ((), ())), preferred_element_type=F32)


def fill_masks(starts_ref, mask_ref, region):
    for part in range(2):
        keys = part * region + lax.broadcasted_iota(jnp.int32, (region, region), 0)
        queries = part * region + lax.broadcasted_iota(jnp.int32, (region, region), 1)
        visible = keys <= queries
        for image in range(starts_ref.shape[1]):
            first = starts_ref[0, image]
            visible = visible | (
                (keys >= first)
                & (keys < first + IMG)
                & (queries >= first)
                & (queries < first + IMG)
            )
        mask_ref[part] = jnp.where(visible, 0.0, MASKED_SCORE)


def tile_scores(key_rows, query_tile, mask_ref, part, first, tile, region):
    scores = dot_nt(key_rows, query_tile)
    mask = mask_ref[part, :, first : first + tile]
    if part == 0:
        return scores + mask
    return jnp.concatenate([scores[:region], scores[region:] + mask], axis=0)


def attend(row, starts, mixed, bias, tables):
    seq_len = mixed.shape[0]
    width = mixed.shape[1] // 3
    pairs = width // LANES
    tile = seq_len // 4
    region = seq_len // 2
    scale = 1.0 / math.sqrt(HEAD_DIM)

    def kernel(
        row_ref,
        starts_ref,
        q_ref,
        k_ref,
        v_ref,
        qb_ref,
        kb_ref,
        vb_ref,
        keep_ref,
        lower_ref,
        upper_ref,
        out_ref,
        qo_ref,
        ko_ref,
        vo_ref,
        log_ref,
        mask_ref,
    ):
        @pl.when(pl.program_id(0) == 0)
        def masks():
            fill_masks(starts_ref, mask_ref, region)

        for number in range(4):
            place = slice(number * tile, (number + 1) * tile)
            origin = pl.ds(pl.multiple_of(jnp.bitwise_xor(row_ref[0], number) * tile, tile), tile)
            turns = (keep_ref[place, :], lower_ref[place, :], upper_ref[place, :])
            turned = turn(q_ref[origin, :] + qb_ref[4:5, :], *turns)
            qo_ref[place, :] = (turned.astype(BF16).astype(F32) * scale).astype(BF16)
            ko_ref[place, :] = turn(k_ref[origin, :] + kb_ref[5:6, :], *turns).astype(BF16)
            vo_ref[place, :] = (v_ref[origin, :] + vb_ref[6:7, :]).astype(BF16)
        value_columns = jnp.transpose(vo_ref[...])
        for number in range(4):
            part = number // 2
            seen = region * (part + 1)
            first = (number % 2) * tile
            outs = []
            for head in range(2):
                query_tile = jnp.where(
                    head_mask(tile, head),
                    qo_ref[number * tile : (number + 1) * tile, :],
                    jnp.zeros((), BF16),
                )
                scores = tile_scores(
                    ko_ref[:seen, :], query_tile, mask_ref, part, first, tile, region
                )
                peak = jnp.max(scores, axis=0, keepdims=True)
                powers = jnp.exp(scores - peak)
                total = jnp.sum(powers, axis=0, keepdims=True)
                log_ref[0, head : head + 1, number * tile : (number + 1) * tile] = peak + jnp.log(
                    total
                )
                mixed_values = dot_nn(
                    value_columns[head * HEAD_DIM : (head + 1) * HEAD_DIM, :seen],
                    powers.astype(BF16),
                )
                outs.append(mixed_values / total)
            place = pl.ds(pl.multiple_of(jnp.bitwise_xor(row_ref[0], number) * tile, tile), tile)
            out_ref[place, :] = jnp.transpose(jnp.concatenate(outs, axis=0)).astype(BF16)

    def columns(kind):
        return pl.BlockSpec((seq_len, LANES), lambda h: (0, kind * pairs + h))

    bias_block = pl.BlockSpec((8, LANES), lambda h: (0, h))
    table = pl.BlockSpec((seq_len, LANES), lambda h: (0, 0))
    low = jax.ShapeDtypeStruct((seq_len, width), BF16)
    return pl.pallas_call(
        kernel,
        grid=(pairs,),
        in_specs=[smem(), smem()]
        + [columns(0), columns(1), columns(2)]
        + [bias_block] * 3
        + [table] * 3,
        out_specs=[columns(0)] * 4 + [pl.BlockSpec((1, 8, seq_len), lambda h: (h, 0, 0))],
        out_shape=[low] * 4 + [jax.ShapeDtypeStruct((pairs, 8, seq_len), F32)],
        scratch_shapes=[pltpu.VMEM((2, region, region), F32)],
        compiler_params=params(40),
        cost_estimate=cost(
            3 * seq_len * seq_len * width * 4, 20 * seq_len * width, seq_len * seq_len * 2 * pairs
        ),
        name="attend",
    )(row, starts, mixed, mixed, mixed, bias, bias, bias, *tables)


def attend_back(row, starts, queries, keys, values, logs, outputs, grads, tables):
    seq_len, width = queries.shape
    pairs = width // LANES
    tile = seq_len // 4
    region = seq_len // 2
    scale = 1.0 / math.sqrt(HEAD_DIM)

    def kernel(
        row_ref,
        starts_ref,
        q_ref,
        k_ref,
        v_ref,
        log_ref,
        o_ref,
        g_ref,
        keep_ref,
        lower_ref,
        upper_ref,
        out_ref,
        sum_ref,
        mask_ref,
        dq_ref,
        dk_ref,
        dv_ref,
        low_ref,
        bias_ref,
    ):
        @pl.when((pl.program_id(0) == 0) & (pl.program_id(1) == 0))
        def masks():
            fill_masks(starts_ref, mask_ref, region)

        @pl.when(pl.program_id(1) == 0)
        def work():
            dk_ref[...] = jnp.zeros_like(dk_ref)
            dv_ref[...] = jnp.zeros_like(dv_ref)
            key_columns = jnp.transpose(k_ref[...])
            for number in range(4):
                part = number // 2
                seen = region * (part + 1)
                first = (number % 2) * tile
                span = slice(number * tile, (number + 1) * tile)
                origin = pl.ds(
                    pl.multiple_of(jnp.bitwise_xor(row_ref[0], number) * tile, tile), tile
                )
                grad_tile = g_ref[origin, :]
                products = jnp.transpose(grad_tile.astype(F32) * o_ref[origin, :].astype(F32))
                query_grads = []
                for head in range(2):
                    mine = head_mask(tile, head)
                    query_tile = jnp.where(mine, q_ref[span, :], jnp.zeros((), BF16))
                    head_grad = jnp.where(mine, grad_tile, jnp.zeros((), BF16))
                    inner = jnp.sum(
                        products[head * HEAD_DIM : (head + 1) * HEAD_DIM], axis=0, keepdims=True
                    )
                    scores = tile_scores(
                        k_ref[:seen, :], query_tile, mask_ref, part, first, tile, region
                    )
                    weights = jnp.exp(scores - log_ref[0, head : head + 1, span])
                    pulls = dot_nt(v_ref[:seen, :], head_grad)
                    score_grad = (weights * (pulls - inner)).astype(BF16)
                    dv_ref[:seen, :] += dot_nn(weights.astype(BF16), head_grad)
                    dk_ref[:seen, :] += dot_nn(score_grad, query_tile)
                    query_grads.append(
                        dot_nn(
                            key_columns[head * HEAD_DIM : (head + 1) * HEAD_DIM, :seen], score_grad
                        )
                    )
                dq_ref[span, :] = jnp.transpose(jnp.concatenate(query_grads, axis=0)) * scale
            bias_ref[...] = jnp.zeros_like(bias_ref)
            for number in range(4):
                span = slice(number * tile, (number + 1) * tile)
                origin = pl.ds(
                    pl.multiple_of(jnp.bitwise_xor(row_ref[0], number) * tile, tile), tile
                )
                turns = (keep_ref[span, :], -lower_ref[span, :], -upper_ref[span, :])
                parts = (
                    turn(dq_ref[span, :], *turns),
                    turn(dk_ref[span, :], *turns),
                    dv_ref[span, :],
                )
                for kind in range(3):
                    low = parts[kind].astype(BF16)
                    low_ref[kind, origin, :] = low
                    bias_ref[kind, 0:1, :] += jnp.sum(low.astype(F32), axis=0, keepdims=True)

        out_ref[...] = low_ref[pl.program_id(1)]
        sum_ref[...] = bias_ref[pl.program_id(1)]

    columns = pl.BlockSpec((seq_len, LANES), lambda h, j: (0, h))
    table = pl.BlockSpec((seq_len, LANES), lambda h, j: (0, 0))
    return pl.pallas_call(
        kernel,
        grid=(pairs, 3),
        in_specs=[smem(), smem()]
        + [columns] * 3
        + [pl.BlockSpec((1, 8, seq_len), lambda h, j: (h, 0, 0))]
        + [columns] * 2
        + [table] * 3,
        out_specs=[
            pl.BlockSpec((seq_len, LANES), lambda h, j: (0, j * pairs + h)),
            pl.BlockSpec((8, LANES), lambda h, j: (0, j * pairs + h)),
        ],
        out_shape=[
            jax.ShapeDtypeStruct((seq_len, 3 * width), BF16),
            jax.ShapeDtypeStruct((8, 3 * width), F32),
        ],
        scratch_shapes=[
            pltpu.VMEM((2, region, region), F32),
            pltpu.VMEM((seq_len, LANES), F32),
            pltpu.VMEM((seq_len, LANES), F32),
            pltpu.VMEM((seq_len, LANES), F32),
            pltpu.VMEM((3, seq_len, LANES), BF16),
            pltpu.VMEM((3, 8, LANES), F32),
        ],
        compiler_params=params(48),
        cost_estimate=cost(
            8 * seq_len * seq_len * width * 4, 20 * seq_len * width, seq_len * seq_len * 2 * pairs
        ),
        name="attend_back",
    )(row, starts, queries, keys, values, logs, outputs, grads, *tables)


def gate_up(rows_two, w_gate):
    tokens, width = rows_two.shape
    tiles = w_gate.shape[1] // (2 * LANES)

    def kernel(in_ref, w_ref, gate_ref, up_ref, hidden_ref):
        both = dot_nn(in_ref[...], w_ref[...])
        gate, up = both[:, :LANES], both[:, LANES:]
        gate_ref[...] = gate.astype(BF16)
        up_ref[...] = up.astype(BF16)
        hidden_ref[...] = (gate * jax.nn.sigmoid(gate) * up).astype(BF16)

    out = pl.BlockSpec((tokens, LANES), lambda i: (0, i))
    return pl.pallas_call(
        kernel,
        grid=(tiles,),
        in_specs=[whole(tokens, width), pl.BlockSpec((width, 2 * LANES), lambda i: (0, i))],
        out_specs=[out] * 3,
        out_shape=[jax.ShapeDtypeStruct((tokens, tiles * LANES), BF16)] * 3,
        compiler_params=params(40),
        cost_estimate=cost(
            2 * tokens * w_gate.size,
            2 * (rows_two.size + w_gate.size) + 6 * tokens * tiles * LANES,
            tokens * tiles * LANES,
        ),
        name="gate_up",
    )(rows_two, w_gate)


def gate_up_back(rows_grad, w_down, gate, up):
    tokens, width = rows_grad.shape
    hidden = w_down.shape[1]
    tile = 256

    def kernel(in_ref, w_ref, gate_ref, up_ref, out_ref):
        pulled = dot_nn(in_ref[...], w_ref[...])
        for number in range(hidden // LANES):
            span = slice(number * LANES, (number + 1) * LANES)
            grad = pulled[:, span]
            gate_part = gate_ref[:, span].astype(F32)
            up_part = up_ref[:, span].astype(F32)
            squash = jax.nn.sigmoid(gate_part)
            first = 2 * number * LANES
            out_ref[:, first : first + LANES] = (
                grad * up_part * squash * (1.0 + gate_part * (1.0 - squash))
            ).astype(BF16)
            out_ref[:, first + LANES : first + 2 * LANES] = (grad * gate_part * squash).astype(BF16)

    return pl.pallas_call(
        kernel,
        grid=(tokens // tile,),
        in_specs=[
            row_blocks(tile, width),
            whole(width, hidden),
            row_blocks(tile, hidden),
            row_blocks(tile, hidden),
        ],
        out_specs=row_blocks(tile, 2 * hidden),
        out_shape=jax.ShapeDtypeStruct((tokens, 2 * hidden), BF16),
        compiler_params=params(40),
        cost_estimate=cost(
            2 * tokens * w_down.size,
            2 * (rows_grad.size + w_down.size) + 8 * tokens * hidden,
            tokens * hidden,
        ),
        name="gate_up_back",
    )(rows_grad, w_down, gate, up)


def adam_update(master, first, second, gradient, keep, rate):
    correction = 1.0 - MOMENT_DECAY**STEP
    new_first = MOMENT_DECAY * first + (1.0 - MOMENT_DECAY) * gradient
    new_second = MOMENT_DECAY * second + (1.0 - MOMENT_DECAY) * gradient * gradient
    direction = new_first / correction / (jnp.sqrt(new_second / correction) + ADAM_EPSILON)
    new_master = master - rate * (direction + WEIGHT_DECAY * master)
    return (
        jnp.where(keep, new_master, master),
        jnp.where(keep, new_first, first),
        jnp.where(keep, new_second, second),
    )


def adam_call(name, keep, states, gradient, rate, grid, state_spec, grad_spec, pieces):
    def kernel(keep_ref, m_ref, f_ref, s_ref, g_ref, mo_ref, fo_ref, so_ref):
        live = keep_ref[LIVE + pl.program_id(0)] > 0
        for state_at, grad_at in pieces:
            results = adam_update(
                m_ref[state_at],
                f_ref[state_at],
                s_ref[state_at],
                g_ref[grad_at].astype(F32),
                live,
                rate,
            )
            mo_ref[state_at], fo_ref[state_at], so_ref[state_at] = results

    return pl.pallas_call(
        kernel,
        grid=grid,
        in_specs=[smem()] + [state_spec] * 3 + [grad_spec],
        out_specs=[state_spec] * 3,
        out_shape=[jax.ShapeDtypeStruct(states[0].shape, F32)] * 3,
        compiler_params=params(58),
        cost_estimate=cost(12 * states[0].size, 26 * states[0].size, states[0].size),
        name=name,
    )(keep, *states, gradient)


def adam_query(keep, states, gradient, rate):
    kinds, rows, width = states[0].shape
    block = rows // CAP
    return adam_call(
        "adam_query",
        keep,
        states,
        gradient,
        rate,
        (CAP,),
        pl.BlockSpec((kinds, block, width), lambda s: (0, s, 0)),
        pl.BlockSpec((1, block, kinds * width), lambda s: (s, 0, 0)),
        [
            ((kind,), (0, slice(None), slice(kind * width, (kind + 1) * width)))
            for kind in range(kinds)
        ],
    )


def adam_flat(name, keep, states, gradient, rate):
    rows, width = states[0].shape
    block = rows // CAP
    return adam_call(
        name,
        keep,
        states,
        gradient,
        rate,
        (CAP,),
        pl.BlockSpec((block, width), lambda s: (s, 0)),
        pl.BlockSpec((1, block, width), lambda s: (s, 0, 0)),
        [((slice(None), slice(None)), (0,))],
    )


def adam_gate(keep, states, gradient, rate):
    block, width = gradient.shape[1:]
    tiles = width // LANES
    pieces = [
        (
            (pl.ds(tile, block, stride=tiles), slice(None)),
            (0, slice(None), slice(tile * LANES, (tile + 1) * LANES)),
        )
        for tile in range(tiles)
    ]
    return adam_call(
        "adam_gate",
        keep,
        states,
        gradient,
        rate,
        (CAP,),
        pl.BlockSpec((block * tiles, LANES), lambda s: (s, 0)),
        pl.BlockSpec((1, block, width), lambda s: (s, 0, 0)),
        pieces,
    )


def matmul(left, right, left_dim, right_dim, dtype):
    return lax.dot_general(
        left, right, (((left_dim,), (right_dim,)), ((), ())), preferred_element_type=F32
    ).astype(dtype)


def flips(axis, reach):
    return [(index, index ^ reach) for index in range(lax.axis_size(axis))]


def x_pairs():
    return flips("row", 1)


def y_pairs():
    return flips("row", 2)


def share_rows(own):
    half = own.shape[0] // 2
    by_x = lax.ppermute(own, "row", x_pairs())
    by_y = lax.ppermute(own, "row", y_pairs())
    top = lax.ppermute(by_x[:half], "row", y_pairs())
    bottom = lax.ppermute(by_y[half:], "row", x_pairs())
    return jnp.concatenate([own, by_x, by_y, top, bottom], axis=0), by_x, by_y


def fold_rows(sums, top, bottom):
    half, width = top.shape

    def kernel(one_ref, two_ref, top_ref, bottom_ref, x_ref, y_ref):
        first = pl.program_id(0) == 0
        one, two = one_ref[...].astype(F32), two_ref[...].astype(F32)
        x_ref[...] = jnp.where(first, one + top_ref[...].astype(F32), one).astype(BF16)
        y_ref[...] = jnp.where(first, two, two + bottom_ref[...].astype(F32)).astype(BF16)

    out = jax.ShapeDtypeStruct((2 * half, width), BF16)
    return pl.pallas_call(
        kernel,
        grid=(2,),
        in_specs=[
            row_blocks(half, width, 2),
            row_blocks(half, width, 4),
            whole(half, width),
            whole(half, width),
        ],
        out_specs=[row_blocks(half, width)] * 2,
        out_shape=[out, out],
        compiler_params=params(),
        cost_estimate=cost(0, 10 * half * width),
        name="fold_rows",
    )(sums, sums, top, bottom)


def scatter_rows(sums, *others):
    rows = sums.shape[0] // 4
    half = rows // 2
    top = lax.ppermute(sums[3 * rows : 3 * rows + half], "row", y_pairs())
    bottom = lax.ppermute(sums[3 * rows + half :], "row", x_pairs())
    if others:
        top = after(top, *others)
    to_x, to_y = fold_rows(sums, top, bottom)
    return (
        (sums, lax.ppermute(to_x, "row", x_pairs()), lax.ppermute(to_y, "row", y_pairs())),
        to_x,
        to_y,
    )


def chip_moves(columns, moves):
    chips = columns // 2
    return [
        (2 * chip + core, 2 * (chip + moves[core]) + core)
        for chip in range(chips)
        for core in range(2)
        if 0 <= chip + moves[core] < chips
    ]


def swap_cores(values, columns):
    return lax.ppermute(values, "col", [(index, index ^ 1) for index in range(columns)])


def both_cores(values, columns):
    return values, swap_cores(values, columns)


def local_line(
    inputs,
    cotangent,
    image_starts,
    owners,
    query_master,
    query_first,
    query_second,
    output_master,
    output_first,
    output_second,
    gate_master,
    gate_first,
    gate_second,
    down_master,
    down_first,
    down_second,
    vector_master,
    vector_first,
    vector_second,
):
    columns = lax.axis_size("col")
    col_index = lax.axis_index("col")
    row_index = lax.axis_index("row")
    blocks = owners.shape[0]
    block_rows = D // blocks
    head_blocks = query_master.shape[2] // LANES
    codes, order, sorted_slots, head_slots, head_places = plan_blocks(
        owners, jnp.stack([col_index, row_index]), columns, head_blocks
    )
    uneven = codes[UNEVEN]

    inward = chip_moves(columns, (1, -1))
    outward = chip_moves(columns, (-1, 1))

    def spread_out(own, send_codes, keep_codes):
        partner = swap_cores(own, columns)
        sent = pick_blocks(send_codes, 0, 2, [own, partner])
        near = lax.ppermute(sent, "col", inward)

        def near_only():
            return pick_blocks(keep_codes, 4, 2, [own, partner, near])

        def farther(first, count):
            more = pick_blocks(codes, first, count, [own, partner])
            return pick_blocks(
                keep_codes, 4, 2, [own, partner, near, lax.ppermute(more, "col", outward)]
            )

        kept = lax.switch(
            uneven, [near_only, lambda: farther(UNEVEN + 1, 1), lambda: farther(2, 2)]
        )
        return sent, kept.reshape(2 * block_rows, own.shape[2])

    def gather(part):
        return lax.all_gather(part, "col", axis=0, tiled=True)

    def sum_up(gradient):
        own = lax.psum_scatter(gradient, "col", scatter_dimension=0, tiled=True)
        return own.reshape(2, block_rows, own.shape[1])

    def start_home(own):
        return own, lax.ppermute(own, "col", outward)

    def finish_home(own, near, codes):
        held = [own, near, swap_cores(own, columns), swap_cores(near, columns)]

        def near_only():
            return pick_blocks(codes, 6, CAP, held)

        def farther(more):
            far = lax.ppermute(more, "col", inward)
            return pick_blocks(codes, 6, CAP, held + [far, swap_cores(far, columns)])

        def one_farther():
            return farther(lax.dynamic_slice_in_dim(own, 1 - col_index % 2, 1, 0))

        return lax.switch(uneven, [near_only, one_farther, lambda: farther(own)])

    local_in = inputs[0]
    upstream = cotangent[0]
    row = row_index.reshape(1)
    tables = lane_tables(inputs.shape[1] * 4)
    rates = step_rates()

    query_slabs = [
        jnp.transpose(part, (1, 0, 2)) for part in (query_master, query_first, query_second)
    ]
    query_width = 3 * query_slabs[0].shape[2]
    sent_attention, attention_part = spread_out(
        pack_attention(query_slabs[0], output_master), codes, codes
    )
    plain_one = norm_one(after(order, sent_attention), local_in)
    rows_plain, *plain_parts = share_rows(plain_one)
    w_attention = gather(attention_part)
    w_query, w_output = w_attention[:, :query_width], w_attention[:, query_width:]
    vector_rows = jnp.pad(vector_master.T, ((0, 9), (0, 0))).astype(BF16)
    vector_blocks = jnp.transpose(vector_rows.reshape(16, CAP, block_rows), (1, 0, 2))
    vectors, bias = spread_vectors(
        sorted_slots, head_slots, gather(after(vector_blocks, attention_part, *plain_parts))
    )
    gate_states = [gate_lines(part) for part in (gate_master, gate_first, gate_second)]
    rows_grad = share_rows(order_grad(after(order, rows_plain), upstream))[0]
    rows_one = scale_rows(rows_plain, vectors)
    unused, gate_part = spread_out(
        pack_gate(gate_states[0], gate_master.shape[0]),
        after(codes, vectors),
        after(codes, rows_grad, rows_one),
    )
    w_gate = gather(gate_part)
    mixed = matmul(rows_one, w_query, 1, 0, F32)
    unused, down_part = spread_out(
        pack_flat("pack_down", down_master), after(codes, gate_part), after(codes, mixed)
    )
    w_down = gather(down_part)
    attended, queries, keys, values, logs = attend(
        after(row, down_part), image_starts, mixed, bias, tables
    )
    middle, normed_two = norm_two(
        order, local_in, scatter_rows(matmul(attended, w_output, 1, 1, BF16))[0], vectors
    )
    rows_two = share_rows(normed_two)[0]
    gate, up, hidden = gate_up(rows_two, w_gate)

    down_sums = matmul(rows_grad, hidden, 0, 0, BF16)
    down_own = sum_up(down_sums)
    gate_up_grad = gate_up_back(rows_grad, w_down, after(gate, down_sums), up)
    pulled_two = matmul(gate_up_grad, w_gate, 1, 1, BF16)
    gate_sums = matmul(rows_two, after(gate_up_grad, pulled_two), 0, 0, BF16)
    gate_own = sum_up(gate_sums)
    out_sums = matmul(after(hidden, gate_sums), w_down, 1, 1, BF16)
    middle_grad, low_middle, sums_two = norm_two_back(
        order, upstream, middle, scatter_rows(pulled_two)[0], after(vectors, gate_sums, out_sums)
    )
    rows_mid = share_rows(low_middle)[0]
    down_home = start_home(after(down_own, low_middle))
    attended_grad = matmul(rows_mid, w_output, 1, 0, BF16)
    output_sums = matmul(rows_mid, after(attended, attended_grad), 0, 0, BF16)
    output_own = sum_up(output_sums)
    out_partial, *out_parts = scatter_rows(after(out_sums, rows_mid), output_sums)
    mixed_grad, bias_sums = attend_back(
        after(row, *out_parts),
        image_starts,
        queries,
        keys,
        values,
        logs,
        attended,
        attended_grad,
        tables,
    )
    layer_out = finish_out(order, after(middle, mixed_grad), out_partial)
    pulled_one = matmul(after(mixed_grad, layer_out), w_query, 1, 1, BF16)
    query_sums = matmul(rows_one, after(mixed_grad, pulled_one, down_home[1]), 0, 0, BF16)
    query_own = sum_up(query_sums)
    gate_home = start_home(after(gate_own, query_sums))
    new_down = adam_flat(
        "adam_down",
        codes,
        (down_master, down_first, down_second),
        finish_home(*down_home, after(codes, query_sums)),
        rates[3],
    )
    input_grad, sums_one = norm_one_back(
        order,
        local_in,
        middle_grad,
        scatter_rows(pulled_one)[0],
        after(vectors, new_down[0]),
    )
    vector_sums = place_vector_grads(head_places, sums_one, sums_two, bias_sums)
    for axis, reach in (("row", 1), ("row", 2), ("col", 1), ("col", 2), ("col", 4)):
        vector_sums = vector_sums + lax.ppermute(vector_sums, axis, flips(axis, reach))
    new_gate = [
        gate_unlines(part, gate_master.shape)
        for part in adam_gate(
            codes,
            gate_states,
            finish_home(gate_home[0], after(gate_home[1], input_grad), codes),
            rates[2],
        )
    ]
    output_home = start_home(after(output_own, input_grad))
    new_output = adam_flat(
        "adam_output",
        codes,
        (output_master, output_first, output_second),
        finish_home(output_home[0], after(output_home[1], new_gate[0]), codes),
        rates[1],
    )
    new_vector = [
        part.T
        for part in adam_vector(
            codes,
            [part.T for part in (vector_master, vector_first, vector_second)],
            vector_sums,
            rates[4],
        )
    ]
    query_own = after(query_own, new_output[0], new_vector[0])
    new_query = [
        jnp.transpose(part, (1, 0, 2))
        for part in adam_query(
            codes, query_slabs, finish_home(*start_home(query_own), codes), rates[0]
        )
    ]
    return (
        layer_out[None],
        input_grad[None],
        *new_query,
        *new_output,
        *new_gate,
        *new_down,
        *new_vector,
    )


def solution(mesh):
    one_hop_line = mesh.shape["row"] == 4 and mesh.shape["col"] == 8
    return jax.shard_map(
        local_line if one_hop_line else local,
        mesh=mesh,
        in_specs=(
            P("col", "row", None),
            P("col", "row", None),
            P("col", None),
            P(),
            P("col", None, "row"),
            P("col", None, "row"),
            P("col", None, "row"),
            P("col", "row"),
            P("col", "row"),
            P("col", "row"),
            P("col", None, "row"),
            P("col", None, "row"),
            P("col", None, "row"),
            P("col", "row"),
            P("col", "row"),
            P("col", "row"),
            P("col", None),
            P("col", None),
            P("col", None),
        ),
        out_specs=(
            P("col", "row", None),
            P("col", "row", None),
            P("col", None, "row"),
            P("col", None, "row"),
            P("col", None, "row"),
            P("col", "row"),
            P("col", "row"),
            P("col", "row"),
            P("col", None, "row"),
            P("col", None, "row"),
            P("col", None, "row"),
            P("col", "row"),
            P("col", "row"),
            P("col", "row"),
            P("col", None),
            P("col", None),
            P("col", None),
        ),
        check_vma=False,
    )
```

```python
import math

import jax
import jax.numpy as jnp
import numpy as np
from jax import lax
from jax.experimental import pallas as pl
from jax.experimental.layout import Layout, with_layout_constraint
from jax.experimental.pallas import tpu as pltpu
from jax.sharding import PartitionSpec as P

D = 2048
HEAD_DIM = 64
FF = 5632
ROT = 16
SEQ = 1024
IMG = 256
STEP = 5
CAP = 4

LANES = 128
MIB = 1 << 20

NORM_EPSILON = 1e-05
ADAM_EPSILON = 1e-08
MOMENT_DECAY = 0.5
WEIGHT_DECAY = 0.1
ROTARY_BASE = 10000.0
MASKED_SCORE = -1e30


def owner_slots(owners):
    block_count = owners.shape[0]
    block_order = jnp.arange(block_count, dtype=jnp.int32)
    before = (owners[:, None] == owners[None, :]) & (block_order[None, :] < block_order[:, None])
    return owners * CAP + jnp.sum(before.astype(jnp.int32), axis=1)


def slot_sources(slot_of, slot_count):
    matches = slot_of[None, :] == jnp.arange(slot_count, dtype=jnp.int32)[:, None]
    filled = jnp.any(matches, axis=1)
    numbers = jnp.arange(slot_of.shape[0], dtype=jnp.int32)
    source = jnp.sum(jnp.where(matches, numbers[None, :], 0), axis=1)
    return (source, filled)


def unpack(gathered, slot_of, block_rows):
    shaped = gathered.reshape((-1, block_rows) + gathered.shape[1:])
    return jnp.take(shaped, slot_of, axis=0).reshape((-1,) + gathered.shape[1:])


def own_blocks(gradient, own_source, block_rows):
    shaped = gradient.reshape((-1, block_rows) + gradient.shape[1:])
    return jnp.take(shaped, own_source, axis=0).reshape((-1,) + gradient.shape[1:])


def normalize(values):
    center = jnp.mean(values, axis=-1, keepdims=True)
    spread = jnp.mean(values * values, axis=-1, keepdims=True) - center * center
    inverse = lax.rsqrt(spread + NORM_EPSILON)
    return ((values - center) * inverse, inverse)


def norm_back(upstream, plain_rows, inverse, gain_row):
    scaled = upstream * gain_row
    return inverse * (
        scaled
        - jnp.mean(scaled, axis=-1, keepdims=True)
        - plain_rows * jnp.mean(scaled * plain_rows, axis=-1, keepdims=True)
    )


def rotary_tables(seq_len):
    half_rot = ROT // 2
    frequency = ROTARY_BASE ** (-2.0 * jnp.arange(half_rot, dtype=jnp.float32) / ROT)
    angles = jnp.arange(seq_len, dtype=jnp.float32)[:, None] * frequency[None, :]
    return (jnp.cos(angles), jnp.sin(angles))


def rotate(values, cosine_table, sine_table):
    half_rot = ROT // 2
    first_half = values[..., :half_rot]
    second_half = values[..., half_rot:ROT]
    cosine_part = cosine_table[:, None, :]
    sine_part = sine_table[:, None, :]
    return jnp.concatenate(
        [
            first_half * cosine_part - second_half * sine_part,
            second_half * cosine_part + first_half * sine_part,
            values[..., ROT:],
        ],
        axis=-1,
    )


def rotate_back(values, cosine_table, sine_table):
    half_rot = ROT // 2
    first_half = values[..., :half_rot]
    second_half = values[..., half_rot:ROT]
    cosine_part = cosine_table[:, None, :]
    sine_part = sine_table[:, None, :]
    return jnp.concatenate(
        [
            first_half * cosine_part + second_half * sine_part,
            second_half * cosine_part - first_half * sine_part,
            values[..., ROT:],
        ],
        axis=-1,
    )


def block_ids(starts, seq_len):
    positions = jnp.arange(seq_len, dtype=jnp.int32)
    inside = (positions[None, :] >= starts[:, None]) & (positions[None, :] < starts[:, None] + IMG)
    numbers = jnp.arange(1, starts.shape[0] + 1, dtype=jnp.int32)
    return jnp.sum(jnp.where(inside, numbers[:, None], 0), axis=0)


def adam_step(master, first_state, second_state, gradient, keep_rows, rate):
    new_first = MOMENT_DECAY * first_state + (1.0 - MOMENT_DECAY) * gradient
    new_second = MOMENT_DECAY * second_state + (1.0 - MOMENT_DECAY) * gradient * gradient
    correction = 1.0 - MOMENT_DECAY**STEP
    direction = new_first / correction / (jnp.sqrt(new_second / correction) + ADAM_EPSILON)
    new_master = master - rate * (direction + WEIGHT_DECAY * master)
    keep_mask = keep_rows.reshape(keep_rows.shape + (1,) * (master.ndim - 1))
    return (
        jnp.where(keep_mask, new_master, master),
        jnp.where(keep_mask, new_first, first_state),
        jnp.where(keep_mask, new_second, second_state),
    )


def step_rates():
    return (
        2.0 / math.sqrt(D),
        2.0 / math.sqrt(D * 16 // SEQ),
        2.0 / math.sqrt(D),
        2.0 / math.sqrt(FF),
        0.5,
    )


def local(
    inputs,
    cotangent,
    image_starts,
    owners,
    query_master,
    query_first,
    query_second,
    output_master,
    output_first,
    output_second,
    gate_master,
    gate_first,
    gate_second,
    down_master,
    down_first,
    down_second,
    vector_master,
    vector_first,
    vector_second,
):
    columns = lax.axis_size("col")
    col_index = lax.axis_index("col")
    row_index = lax.axis_index("row")
    block_rows = D // owners.shape[0]
    slot_of = owner_slots(owners)
    source, filled = slot_sources(slot_of, CAP * columns)
    shared = (
        lax.all_gather(query_master.astype(jnp.bfloat16), "col", axis=0, tiled=True),
        lax.all_gather(output_master.astype(jnp.bfloat16), "col", axis=0, tiled=True),
        lax.all_gather(gate_master.astype(jnp.bfloat16), "col", axis=0, tiled=True),
        lax.all_gather(down_master.astype(jnp.bfloat16), "col", axis=0, tiled=True),
        lax.all_gather(vector_master.astype(jnp.bfloat16), "col", axis=0, tiled=True),
    )
    w_query = unpack(shared[0], slot_of, block_rows)
    w_output = unpack(shared[1], slot_of, block_rows)
    w_gate = unpack(shared[2], slot_of, block_rows)
    w_down = unpack(shared[3], slot_of, block_rows)
    vectors = unpack(shared[4], slot_of, block_rows).astype(jnp.float32)
    local_in = inputs[0]
    width = local_in.shape[1]
    head_cols = w_query.shape[2]
    local_heads = head_cols // HEAD_DIM
    score_scale = 1.0 / math.sqrt(HEAD_DIM)
    qkv_bias = lax.dynamic_slice_in_dim(vectors[:, 4:7], row_index * head_cols, head_cols, 0).T
    plain_one, inverse_one = normalize(local_in)
    normed_one = (plain_one * vectors[:, 0] + vectors[:, 1]).astype(jnp.bfloat16)
    rows_one = lax.all_gather(normed_one, "row", axis=0, tiled=True)
    seq_len = rows_one.shape[0]
    mixed_proj = (
        jnp.einsum("td,djh->tjh", rows_one, w_query, preferred_element_type=jnp.float32)
        + qkv_bias[None]
    )
    cosine_table, sine_table = rotary_tables(seq_len)
    queries = rotate(
        mixed_proj[:, 0].reshape(seq_len, local_heads, HEAD_DIM), cosine_table, sine_table
    ).astype(jnp.bfloat16)
    key_rows = rotate(
        mixed_proj[:, 1].reshape(seq_len, local_heads, HEAD_DIM), cosine_table, sine_table
    ).astype(jnp.bfloat16)
    value_rows = mixed_proj[:, 2].reshape(seq_len, local_heads, HEAD_DIM).astype(jnp.bfloat16)
    labels = block_ids(image_starts[0], seq_len)
    block_size = min(512, seq_len)
    block_count = seq_len // block_size
    positions = jnp.arange(seq_len, dtype=jnp.int32)

    def scores_at(first_row):
        row_pos = first_row + jnp.arange(block_size, dtype=jnp.int32)
        row_label = lax.dynamic_slice_in_dim(labels, first_row, block_size, 0)
        allowed = (positions[None, :] <= row_pos[:, None]) | (
            row_label[:, None] == labels[None, :]
        ) & (row_label[:, None] > 0)
        query_rows = lax.dynamic_slice_in_dim(queries, first_row, block_size, 0)
        raw_scores = (
            jnp.einsum("qhe,khe->hqk", query_rows, key_rows, preferred_element_type=jnp.float32)
            * score_scale
        )
        return (jnp.where(allowed[None], raw_scores, MASKED_SCORE), query_rows)

    def forward_block(block_index):
        scores, query_rows = scores_at(block_index * block_size)
        row_peak = jnp.max(scores, axis=-1, keepdims=True)
        powers = jnp.exp(scores - row_peak)
        row_total = jnp.sum(powers, axis=-1, keepdims=True)
        weights = (powers / row_total).astype(jnp.bfloat16)
        output = jnp.einsum("hqk,khe->qhe", weights, value_rows, preferred_element_type=jnp.float32)
        return (output, (row_peak + jnp.log(row_total))[..., 0])

    output_blocks, log_totals = lax.map(forward_block, jnp.arange(block_count, dtype=jnp.int32))
    attended = output_blocks.reshape(seq_len, head_cols).astype(jnp.bfloat16)
    picked_rows = attended
    middle = local_in + lax.psum_scatter(
        jnp.einsum("th,dh->td", picked_rows, w_output, preferred_element_type=jnp.float32),
        "row",
        scatter_dimension=0,
        tiled=True,
    )
    plain_two, inverse_two = normalize(middle)
    normed_two = (plain_two * vectors[:, 2] + vectors[:, 3]).astype(jnp.bfloat16)
    rows_two = lax.all_gather(normed_two, "row", axis=0, tiled=True)
    gate_up = jnp.einsum("td,djf->tjf", rows_two, w_gate, preferred_element_type=jnp.float32)
    gate_part = gate_up[:, 0]
    up_part = gate_up[:, 1]
    gate_sigmoid = jax.nn.sigmoid(gate_part)
    activated = gate_part * gate_sigmoid
    hidden = (activated * up_part).astype(jnp.bfloat16)
    picked_rows = hidden
    layer_out = middle + lax.psum_scatter(
        jnp.einsum("tf,df->td", picked_rows, w_down, preferred_element_type=jnp.float32).astype(
            jnp.bfloat16
        ),
        "row",
        scatter_dimension=0,
        tiled=True,
    ).astype(jnp.float32)
    upstream = cotangent[0]
    rows_grad = lax.all_gather(upstream.astype(jnp.bfloat16), "row", axis=0, tiled=True)
    hidden_grad = jnp.einsum("td,df->tf", rows_grad, w_down, preferred_element_type=jnp.float32)
    down_grad = jnp.einsum("tf,td->df", hidden, rows_grad, preferred_element_type=jnp.float32)
    gate_grad = hidden_grad * up_part * gate_sigmoid * (1.0 + gate_part * (1.0 - gate_sigmoid))
    up_grad = hidden_grad * activated
    gate_up_grad = jnp.stack([gate_grad, up_grad], axis=1).astype(jnp.bfloat16)
    gate_weight_grad = jnp.einsum(
        "td,tjf->djf", rows_two, gate_up_grad, preferred_element_type=jnp.float32
    )
    picked_rows = gate_up_grad
    normed_two_grad = lax.psum_scatter(
        jnp.einsum("tjf,djf->td", picked_rows, w_gate, preferred_element_type=jnp.float32),
        "row",
        scatter_dimension=0,
        tiled=True,
    )
    middle_grad = upstream + norm_back(normed_two_grad, plain_two, inverse_two, vectors[:, 2])
    rows_mid = lax.all_gather(middle_grad.astype(jnp.bfloat16), "row", axis=0, tiled=True)
    attended_grad = jnp.einsum(
        "td,dh->th", rows_mid, w_output, preferred_element_type=jnp.float32
    ).astype(jnp.bfloat16)
    output_grad = jnp.einsum("th,td->dh", attended, rows_mid, preferred_element_type=jnp.float32)
    head_grad = attended_grad.reshape(seq_len, local_heads, HEAD_DIM)

    def backward_block(running, block_index):
        key_total, value_total = running
        first_row = block_index * block_size
        scores, query_rows = scores_at(first_row)
        probabilities = jnp.exp(scores - log_totals[block_index][..., None])
        row_grad = lax.dynamic_slice_in_dim(head_grad, first_row, block_size, 0)
        prob_grad = jnp.einsum(
            "qhe,khe->hqk", row_grad, value_rows, preferred_element_type=jnp.float32
        )
        inner = jnp.sum(prob_grad * probabilities, axis=-1, keepdims=True)
        score_grad = (probabilities * (prob_grad - inner)).astype(jnp.bfloat16)
        query_grad = (
            jnp.einsum("hqk,khe->qhe", score_grad, key_rows, preferred_element_type=jnp.float32)
            * score_scale
        )
        key_total = (
            key_total
            + jnp.einsum("hqk,qhe->khe", score_grad, query_rows, preferred_element_type=jnp.float32)
            * score_scale
        )
        value_total = value_total + jnp.einsum(
            "hqk,qhe->khe",
            probabilities.astype(jnp.bfloat16),
            row_grad,
            preferred_element_type=jnp.float32,
        )
        return ((key_total, value_total), query_grad)

    empty_heads = jnp.zeros((seq_len, local_heads, HEAD_DIM), jnp.float32)
    (key_grad, value_grad), query_blocks = lax.scan(
        backward_block, (empty_heads, empty_heads), jnp.arange(block_count, dtype=jnp.int32)
    )
    query_grad = query_blocks.reshape(seq_len, local_heads, HEAD_DIM)
    mixed_grad = jnp.stack(
        [
            rotate_back(query_grad, cosine_table, sine_table).reshape(seq_len, head_cols),
            rotate_back(key_grad, cosine_table, sine_table).reshape(seq_len, head_cols),
            value_grad.reshape(seq_len, head_cols),
        ],
        axis=1,
    ).astype(jnp.bfloat16)
    bias_grad = jnp.sum(mixed_grad, axis=0, dtype=jnp.float32)
    query_weight_grad = jnp.einsum(
        "td,tjh->djh", rows_one, mixed_grad, preferred_element_type=jnp.float32
    )
    picked_rows = mixed_grad
    normed_one_grad = lax.psum_scatter(
        jnp.einsum("tjh,djh->td", picked_rows, w_query, preferred_element_type=jnp.float32).astype(
            jnp.bfloat16
        ),
        "row",
        scatter_dimension=0,
        tiled=True,
    ).astype(jnp.float32)
    input_grad = middle_grad + norm_back(normed_one_grad, plain_one, inverse_one, vectors[:, 0])
    norm_grads = jnp.stack(
        [
            jnp.sum(normed_one_grad * plain_one, axis=0),
            jnp.sum(normed_one_grad, axis=0),
            jnp.sum(normed_two_grad * plain_two, axis=0),
            jnp.sum(normed_two_grad, axis=0),
        ],
        axis=1,
    )
    placed = lax.dynamic_update_slice_in_dim(
        jnp.zeros((width, 3), jnp.float32), bias_grad.T, row_index * head_cols, 0
    )
    vector_grad = lax.psum(
        jnp.concatenate([norm_grads, placed], axis=1).astype(jnp.bfloat16), "row"
    )
    own_filled = lax.dynamic_slice_in_dim(filled, col_index * CAP, CAP, 0)
    own_source = lax.dynamic_slice_in_dim(source, col_index * CAP, CAP, 0)
    summed = (
        lax.psum(query_weight_grad.astype(jnp.bfloat16), "col").astype(jnp.float32),
        lax.psum(output_grad.astype(jnp.bfloat16), "col").astype(jnp.float32),
        lax.psum(gate_weight_grad.astype(jnp.bfloat16), "col").astype(jnp.float32),
        lax.psum(down_grad.astype(jnp.bfloat16), "col").astype(jnp.float32),
        lax.psum(vector_grad, "col").astype(jnp.float32),
    )
    owned_grads = tuple((own_blocks(whole_grad, own_source, block_rows) for whole_grad in summed))
    keep_rows = jnp.repeat(own_filled, block_rows)
    masters = (query_master, output_master, gate_master, down_master, vector_master)
    firsts = (query_first, output_first, gate_first, down_first, vector_first)
    seconds = (query_second, output_second, gate_second, down_second, vector_second)
    rates = step_rates()
    updated = [
        adam_step(
            masters[kind_index],
            firsts[kind_index],
            seconds[kind_index],
            owned_grads[kind_index],
            keep_rows,
            rates[kind_index],
        )
        for kind_index in range(5)
    ]
    return (
        layer_out[None],
        input_grad[None],
        updated[0][0],
        updated[0][1],
        updated[0][2],
        updated[1][0],
        updated[1][1],
        updated[1][2],
        updated[2][0],
        updated[2][1],
        updated[2][2],
        updated[3][0],
        updated[3][1],
        updated[3][2],
        updated[4][0],
        updated[4][1],
        updated[4][2],
    )


BF16 = jnp.bfloat16
F32 = jnp.float32


def smem():
    return pl.BlockSpec(memory_space=pltpu.SMEM)


def params(mib=16):
    return pltpu.CompilerParams(vmem_limit_bytes=mib * MIB)


def cost(flops, nbytes, powers=0):
    return pl.CostEstimate(flops=int(flops), bytes_accessed=int(nbytes), transcendentals=int(powers))


def lane_block(number):
    return pl.ds(pl.multiple_of(number * LANES, LANES), LANES)


def after(value, *others):
    return lax.optimization_barrier((value, *others))[0]


LIVE, PLACES, UNEVEN, TABLE = 10, 14, 18, 32


def plan_blocks(owners, places, columns, head_blocks):
    blocks = owners.shape[0]
    half = blocks // (columns // 2)

    def kernel(owner_ref, at_ref, table_ref, order_ref, sorted_ref, head_slot_ref, head_ref):
        held = [owner_ref[block] for block in range(blocks)]
        col, row = at_ref[0], at_ref[1]
        chip = lax.shift_right_logical(col, 1)
        core = jnp.bitwise_and(col, 1)

        def total(flags):
            return sum(flag.astype(jnp.int32) for flag in flags)

        def below(index):
            return total(owner < index for owner in held)

        for block in range(blocks):
            rank = total(held[other] == held[block] for other in range(block)) + jnp.int32(0)
            place = below(held[block]) + rank
            slot = held[block] * CAP + rank
            order_ref[place] = jnp.int32(block)
            sorted_ref[place] = slot
            head = block - row * head_blocks

            @pl.when((head >= 0) & (head < head_blocks))
            def mine(head=head, slot=slot, place=place):
                head_slot_ref[head] = slot
                head_ref[head] = place

        first = below(2 * chip)
        middle = below(2 * chip + 1)
        end = below(2 * chip + 2)
        own_first = below(col)
        own_count = below(col + 1) - own_first

        def chip_code(place):
            second = place >= middle
            rank = place - jnp.where(second, middle, first)
            code = jnp.where(second.astype(jnp.int32) == core, 0, 16) + rank
            return jnp.where((place >= first) & (place < end), code, 0)

        toward = 1 - 2 * core
        for index in range(2):
            offset = 2 * core + index
            table_ref[index] = chip_code(half * (chip + toward) + offset)
            table_ref[2 + index] = chip_code(half * (chip - toward) + offset)
            kept = half * chip + offset
            near, far = 32 + index, 48 + index
            table_ref[4 + index] = jnp.where(
                kept < first,
                jnp.where(core == 0, near, far),
                jnp.where(kept >= end, jnp.where(core == 0, far, near), chip_code(kept)),
            )
        for rank in range(CAP):
            live = rank < own_count
            place = own_first + jnp.minimum(rank, own_count - 1)
            there = lax.shift_right_logical(place, 2)
            side = there - chip
            other = lax.shift_right_logical(place - half * there, 1)
            near_side = 1 - 2 * other
            same = other == core
            source = jnp.where(
                side == 0,
                jnp.where(same, 0, 2),
                jnp.where(side == near_side, jnp.where(same, 1, 3), jnp.where(same, 4, 5)),
            )
            table_ref[6 + rank] = 16 * source + jnp.bitwise_and(place, 1)
            table_ref[LIVE + rank] = live.astype(jnp.int32)
            table_ref[PLACES + rank] = place
        widest = jnp.int32(0)
        for number in range(1, columns // 2):
            widest = jnp.maximum(widest, jnp.abs(below(2 * number) - half * number))
        table_ref[UNEVEN] = jnp.clip(widest - 2, 0, 2)
        table_ref[UNEVEN + 1] = chip_code(half * (chip - toward) + 1 + core)
        for index in range(UNEVEN + 2, TABLE):
            table_ref[index] = jnp.int32(0)

    def ints(size):
        return jax.ShapeDtypeStruct((size,), jnp.int32)

    return pl.pallas_call(
        kernel,
        in_specs=[smem(), smem()],
        out_specs=[smem()] * 5,
        out_shape=[ints(TABLE), ints(blocks), ints(blocks), ints(head_blocks), ints(head_blocks)],
        compiler_params=params(),
        name="plan_blocks",
    )(owners, places)


def pack_attention(slabs, output):
    kinds, rows, width = slabs.shape
    block = rows // CAP
    total = kinds * width + output.shape[1]

    def kernel(in_ref, output_ref, out_ref):
        for kind in range(kinds):
            out_ref[0, :, kind * width : (kind + 1) * width] = in_ref[kind].astype(BF16)
        out_ref[0, :, kinds * width :] = output_ref[...].astype(BF16)

    return pl.pallas_call(
        kernel,
        grid=(CAP,),
        in_specs=[
            pl.BlockSpec((kinds, block, width), lambda s: (0, s, 0)),
            pl.BlockSpec((block, output.shape[1]), lambda s: (s, 0)),
        ],
        out_specs=pl.BlockSpec((1, block, total), lambda s: (s, 0, 0)),
        out_shape=jax.ShapeDtypeStruct((CAP, block, total), BF16),
        compiler_params=params(58),
        cost_estimate=cost(0, 6 * rows * total),
        name="pack_attention",
    )(slabs, output)


def after(value, *others):
    return lax.optimization_barrier((value, *others))[0]


def gate_lines(values):
    rows, kinds, width = values.shape
    split = with_layout_constraint(
        values.reshape(rows, kinds, width // LANES, LANES), Layout(major_to_minor=(0, 2, 1, 3))
    )
    return jnp.transpose(split, (0, 2, 1, 3)).reshape(rows * kinds * width // LANES, LANES)


def gate_unlines(lines, shape):
    rows, kinds, width = shape
    split = jnp.transpose(lines.reshape(rows, width // LANES, kinds, LANES), (0, 2, 1, 3))
    return with_layout_constraint(split, Layout(major_to_minor=(0, 2, 1, 3))).reshape(shape)


def pack_flat(name, master):
    rows, width = master.shape
    block = rows // CAP

    def kernel(in_ref, out_ref):
        out_ref[0] = in_ref[...].astype(BF16)

    return pl.pallas_call(
        kernel,
        grid=(CAP,),
        in_specs=[pl.BlockSpec((block, width), lambda s: (s, 0))],
        out_specs=pl.BlockSpec((1, block, width), lambda s: (s, 0, 0)),
        out_shape=jax.ShapeDtypeStruct((CAP, block, width), BF16),
        compiler_params=params(),
        cost_estimate=cost(0, 6 * rows * width),
        name=name,
    )(master)


def pack_gate(lines, rows):
    block = rows // CAP
    tiles = lines.shape[0] // rows

    def kernel(in_ref, out_ref):
        for tile in range(tiles):
            out_ref[0, :, tile * LANES : (tile + 1) * LANES] = in_ref[
                pl.ds(tile, block, stride=tiles), :
            ].astype(BF16)

    return pl.pallas_call(
        kernel,
        grid=(CAP,),
        in_specs=[pl.BlockSpec((block * tiles, LANES), lambda s: (s, 0))],
        out_specs=pl.BlockSpec((1, block, tiles * LANES), lambda s: (s, 0, 0)),
        out_shape=jax.ShapeDtypeStruct((CAP, block, tiles * LANES), BF16),
        compiler_params=params(58),
        cost_estimate=cost(0, 6 * lines.size),
        name="pack_gate",
    )(lines)


def pick_blocks(codes, first, count, sources):
    shape = sources[0].shape[1:]

    def kernel(code_ref, *refs):
        ins, out, sems = refs[: len(sources)], refs[-2], refs[-1]
        for place in range(count):
            code = code_ref[first + place]
            index = jnp.bitwise_and(code, 15)
            origin = lax.shift_right_logical(code, 4)
            for number, source in enumerate(ins):

                @pl.when(origin == number)
                def start(source=source, index=index, place=place):
                    held = source.at[index if source.shape[0] > 1 else 0]
                    pltpu.make_async_copy(held, out.at[place], sems.at[place]).start()

        for place in range(count):
            pltpu.make_async_copy(ins[0].at[0], out.at[place], sems.at[place]).wait()

    moved = count * shape[0] * shape[1]
    return pl.pallas_call(
        kernel,
        in_specs=[smem()] + [pl.BlockSpec(memory_space=pl.ANY)] * len(sources),
        out_specs=pl.BlockSpec(memory_space=pltpu.VMEM),
        out_shape=jax.ShapeDtypeStruct((count, *shape), BF16),
        scratch_shapes=[pltpu.SemaphoreType.DMA((count,))],
        compiler_params=params(),
        cost_estimate=cost(0, 4 * moved),
        name="pick_blocks",
    )(codes, *sources)


def row_blocks(height, width, first=0):
    return pl.BlockSpec((height, width), lambda i: (i + first, 0))


def whole(height, width):
    return pl.BlockSpec((height, width), lambda i: (0, 0))


NORM_ROWS = 64


def statistics(values):
    center = jnp.mean(values, axis=-1, keepdims=True)
    spread = jnp.mean(values * values, axis=-1, keepdims=True) - center * center
    return center, lax.rsqrt(spread + NORM_EPSILON)


def order_grad(order, cotangent):
    rows, width = cotangent.shape

    def kernel(order_ref, in_ref, out_ref):
        for place in range(width // LANES):
            out_ref[:, place * LANES : (place + 1) * LANES] = in_ref[
                :, lane_block(order_ref[place])
            ].astype(BF16)

    return pl.pallas_call(
        kernel,
        grid=(rows // NORM_ROWS,),
        in_specs=[smem(), row_blocks(NORM_ROWS, width)],
        out_specs=row_blocks(NORM_ROWS, width),
        out_shape=jax.ShapeDtypeStruct((rows, width), BF16),
        compiler_params=params(),
        cost_estimate=cost(0, 6 * rows * width),
        name="order_grad",
    )(order, cotangent)


def norm_one(order, inputs):
    rows, width = inputs.shape

    def kernel(order_ref, in_ref, out_ref):
        center, inverse = statistics(in_ref[...])
        for place in range(width // LANES):
            span = slice(place * LANES, (place + 1) * LANES)
            plain = (in_ref[:, lane_block(order_ref[place])] - center) * inverse
            out_ref[:, span] = plain.astype(BF16)

    return pl.pallas_call(
        kernel,
        grid=(rows // NORM_ROWS,),
        in_specs=[smem(), row_blocks(NORM_ROWS, width)],
        out_specs=row_blocks(NORM_ROWS, width),
        out_shape=jax.ShapeDtypeStruct((rows, width), BF16),
        compiler_params=params(),
        cost_estimate=cost(0, 6 * rows * width),
        name="norm_one",
    )(order, inputs)


def scale_rows(plain, vectors):
    rows, width = plain.shape
    tile = 256

    def kernel(in_ref, vec_ref, out_ref):
        out_ref[...] = (in_ref[...].astype(F32) * vec_ref[0:1, :] + vec_ref[1:2, :]).astype(BF16)

    return pl.pallas_call(
        kernel,
        grid=(rows // tile,),
        in_specs=[row_blocks(tile, width), whole(8, width)],
        out_specs=row_blocks(tile, width),
        out_shape=jax.ShapeDtypeStruct((rows, width), BF16),
        compiler_params=params(),
        cost_estimate=cost(0, 4 * rows * width),
        name="scale_rows",
    )(plain, vectors)


def norm_two(order, inputs, partial, vectors):
    rows, width = inputs.shape
    own, from_x, from_y = partial

    def kernel(order_ref, in_ref, own_ref, x_ref, y_ref, vec_ref, mid_ref, out_ref):
        for place in range(width // LANES):
            span = slice(place * LANES, (place + 1) * LANES)
            mid_ref[:, span] = (
                in_ref[:, lane_block(order_ref[place])]
                + own_ref[:, span].astype(F32)
                + x_ref[:, span].astype(F32)
                + y_ref[:, span].astype(F32)
            )
        middle = mid_ref[...]
        center, inverse = statistics(middle)
        plain = (middle - center) * inverse
        out_ref[...] = (plain * vec_ref[2:3, :] + vec_ref[3:4, :]).astype(BF16)

    spec = row_blocks(NORM_ROWS, width)
    return pl.pallas_call(
        kernel,
        grid=(rows // NORM_ROWS,),
        in_specs=[smem(), spec, spec, spec, spec, whole(8, width)],
        out_specs=[spec, spec],
        out_shape=[
            jax.ShapeDtypeStruct((rows, width), F32),
            jax.ShapeDtypeStruct((rows, width), BF16),
        ],
        compiler_params=params(),
        cost_estimate=cost(0, 16 * rows * width),
        name="norm_two",
    )(order, inputs, own, from_x, from_y, vectors)


def finish_out(order, middle, partial):
    rows, width = middle.shape
    own, from_x, from_y = partial

    def kernel(order_ref, mid_ref, own_ref, x_ref, y_ref, out_ref):
        for place in range(width // LANES):
            span = slice(place * LANES, (place + 1) * LANES)
            out_ref[:, lane_block(order_ref[place])] = (
                mid_ref[:, span]
                + own_ref[:, span].astype(F32)
                + x_ref[:, span].astype(F32)
                + y_ref[:, span].astype(F32)
            )

    spec = row_blocks(NORM_ROWS, width)
    return pl.pallas_call(
        kernel,
        grid=(rows // NORM_ROWS,),
        in_specs=[smem(), spec, spec, spec, spec],
        out_specs=spec,
        out_shape=jax.ShapeDtypeStruct((rows, width), F32),
        compiler_params=params(),
        cost_estimate=cost(0, 14 * rows * width),
        name="finish_out",
    )(order, middle, own, from_x, from_y)


def norm_pull(upstream, plain, inverse, gain):
    scaled = upstream * gain
    return inverse * (
        scaled
        - jnp.mean(scaled, axis=-1, keepdims=True)
        - plain * jnp.mean(scaled * plain, axis=-1, keepdims=True)
    )


def add_sums(sum_ref, upstream, plain):
    @pl.when(pl.program_id(0) == 0)
    def clear():
        sum_ref[...] = jnp.zeros_like(sum_ref)

    sum_ref[0:1, :] += jnp.sum(upstream * plain, axis=0, keepdims=True)
    sum_ref[1:2, :] += jnp.sum(upstream, axis=0, keepdims=True)


def norm_two_back(order, cotangent, middle, partial, vectors):
    rows, width = middle.shape
    own, from_x, from_y = partial

    def kernel(
        order_ref, cot_ref, mid_ref, own_ref, x_ref, y_ref, vec_ref, grad_ref, low_ref, sum_ref
    ):
        middle_rows = mid_ref[...]
        center, inverse = statistics(middle_rows)
        plain = (middle_rows - center) * inverse
        upstream = own_ref[...].astype(F32) + x_ref[...].astype(F32) + y_ref[...].astype(F32)
        add_sums(sum_ref, upstream, plain)
        grad_ref[...] = norm_pull(upstream, plain, inverse, vec_ref[2:3, :])
        for place in range(width // LANES):
            span = slice(place * LANES, (place + 1) * LANES)
            total = grad_ref[:, span] + cot_ref[:, lane_block(order_ref[place])]
            grad_ref[:, span] = total
            low_ref[:, span] = total.astype(BF16)

    spec = row_blocks(NORM_ROWS, width)
    return pl.pallas_call(
        kernel,
        grid=(rows // NORM_ROWS,),
        in_specs=[smem(), spec, spec, spec, spec, spec, whole(8, width)],
        out_specs=[spec, spec, whole(8, width)],
        out_shape=[
            jax.ShapeDtypeStruct((rows, width), F32),
            jax.ShapeDtypeStruct((rows, width), BF16),
            jax.ShapeDtypeStruct((8, width), F32),
        ],
        compiler_params=params(),
        cost_estimate=cost(0, 20 * rows * width),
        name="norm_two_back",
    )(order, cotangent, middle, own, from_x, from_y, vectors)


def norm_one_back(order, inputs, middle_grad, partial, vectors):
    rows, width = inputs.shape
    own, from_x, from_y = partial

    def kernel(
        order_ref,
        in_ref,
        mid_ref,
        own_ref,
        x_ref,
        y_ref,
        vec_ref,
        out_ref,
        sum_ref,
        plain_ref,
        pull_ref,
    ):
        center, inverse = statistics(in_ref[...])
        for place in range(width // LANES):
            span = slice(place * LANES, (place + 1) * LANES)
            plain_ref[:, span] = (in_ref[:, lane_block(order_ref[place])] - center) * inverse
        plain = plain_ref[...]
        upstream = own_ref[...].astype(F32) + x_ref[...].astype(F32) + y_ref[...].astype(F32)
        add_sums(sum_ref, upstream, plain)
        pull_ref[...] = norm_pull(upstream, plain, inverse, vec_ref[0:1, :])
        for place in range(width // LANES):
            span = slice(place * LANES, (place + 1) * LANES)
            out_ref[:, lane_block(order_ref[place])] = mid_ref[:, span] + pull_ref[:, span]

    spec = row_blocks(NORM_ROWS, width)
    return pl.pallas_call(
        kernel,
        grid=(rows // NORM_ROWS,),
        in_specs=[smem(), spec, spec, spec, spec, spec, whole(8, width)],
        out_specs=[spec, whole(8, width)],
        out_shape=[
            jax.ShapeDtypeStruct((rows, width), F32),
            jax.ShapeDtypeStruct((8, width), F32),
        ],
        scratch_shapes=[pltpu.VMEM((NORM_ROWS, width), F32), pltpu.VMEM((NORM_ROWS, width), F32)],
        compiler_params=params(),
        cost_estimate=cost(0, 18 * rows * width),
        name="norm_one_back",
    )(order, inputs, middle_grad, own, from_x, from_y, vectors)


def spread_vectors(sorted_slots, head_slots, gathered):
    places = sorted_slots.shape[0]
    heads = head_slots.shape[0]

    def kernel(sorted_ref, head_ref, in_ref, vec_ref, bias_ref):
        for place in range(places):
            vec_ref[:, place * LANES : (place + 1) * LANES] = in_ref[sorted_ref[place]].astype(F32)
        for place in range(heads):
            bias_ref[:, place * LANES : (place + 1) * LANES] = in_ref[head_ref[place]].astype(F32)

    return pl.pallas_call(
        kernel,
        in_specs=[smem(), smem(), pl.BlockSpec(memory_space=pltpu.VMEM)],
        out_shape=[
            jax.ShapeDtypeStruct((16, places * LANES), F32),
            jax.ShapeDtypeStruct((16, heads * LANES), F32),
        ],
        compiler_params=params(),
        name="spread_vectors",
    )(sorted_slots, head_slots, gathered)


def place_vector_grads(head_places, sums_one, sums_two, bias_sums):
    heads = head_places.shape[0]

    def kernel(head_ref, one_ref, two_ref, bias_ref, out_ref):
        out_ref[0:2, :] = one_ref[0:2, :]
        out_ref[2:4, :] = two_ref[0:2, :]
        out_ref[4:8, :] = jnp.zeros((4, out_ref.shape[1]), F32)
        for place in range(heads):
            for kind in range(3):
                first = (kind * heads + place) * LANES
                out_ref[4 + kind : 5 + kind, lane_block(head_ref[place])] = bias_ref[
                    0:1, first : first + LANES
                ]

    return pl.pallas_call(
        kernel,
        in_specs=[smem()] + [pl.BlockSpec(memory_space=pltpu.VMEM)] * 3,
        out_shape=jax.ShapeDtypeStruct(sums_one.shape, F32),
        compiler_params=params(),
        name="place_vector_grads",
    )(head_places, sums_one, sums_two, bias_sums)


def adam_vector(keep, states, gradient, rate):
    kinds, rows = states[0].shape
    block = rows // CAP

    def kernel(keep_ref, m_ref, f_ref, s_ref, g_ref, mo_ref, fo_ref, so_ref):
        for slot in range(CAP):
            span = slice(slot * block, (slot + 1) * block)
            grad = g_ref[:, lane_block(keep_ref[PLACES + slot])][:kinds]
            mo_ref[:, span], fo_ref[:, span], so_ref[:, span] = adam_update(
                m_ref[:, span], f_ref[:, span], s_ref[:, span], grad, keep_ref[LIVE + slot] > 0, rate
            )

    return pl.pallas_call(
        kernel,
        in_specs=[smem()] + [pl.BlockSpec(memory_space=pltpu.VMEM)] * 4,
        out_shape=[jax.ShapeDtypeStruct(states[0].shape, F32)] * 3,
        compiler_params=params(),
        name="adam_vector",
    )(keep, *states, gradient)


def lane_tables(seq_len):
    half = ROT // 2
    frequency = (ROTARY_BASE ** (-2.0 * np.arange(half, dtype=np.float32) / ROT)).astype(np.float32)
    angles = np.arange(seq_len, dtype=np.float32)[:, None] * frequency[None, :]
    cosine = np.cos(angles).astype(np.float32)
    sine = np.sin(angles).astype(np.float32)
    rest = HEAD_DIM - ROT
    ones = np.ones((seq_len, rest), np.float32)
    none = np.zeros((seq_len, rest), np.float32)
    blank = np.zeros((seq_len, half), np.float32)
    keep = np.concatenate([cosine, cosine, ones], axis=1)
    lower = np.concatenate([-sine, blank, none], axis=1)
    upper = np.concatenate([blank, sine, none], axis=1)
    return tuple(jnp.asarray(np.concatenate([table, table], axis=1)) for table in (keep, lower, upper))


def turn(values, keep, lower, upper):
    half = ROT // 2
    return (
        values * keep
        + pltpu.roll(values, LANES - half, 1) * lower
        + pltpu.roll(values, half, 1) * upper
    )


def head_mask(rows, head):
    lanes = lax.broadcasted_iota(jnp.int32, (rows, LANES), 1)
    return (lanes // HEAD_DIM) == head


def dot_nt(left, right):
    return lax.dot_general(left, right, (((1,), (1,)), ((), ())), preferred_element_type=F32)


def dot_nn(left, right):
    return lax.dot_general(left, right, (((1,), (0,)), ((), ())), preferred_element_type=F32)


def fill_masks(starts_ref, mask_ref, region):
    for part in range(2):
        keys = part * region + lax.broadcasted_iota(jnp.int32, (region, region), 0)
        queries = part * region + lax.broadcasted_iota(jnp.int32, (region, region), 1)
        visible = keys <= queries
        for image in range(starts_ref.shape[1]):
            first = starts_ref[0, image]
            visible = visible | (
                (keys >= first)
                & (keys < first + IMG)
                & (queries >= first)
                & (queries < first + IMG)
            )
        mask_ref[part] = jnp.where(visible, 0.0, MASKED_SCORE)


def tile_scores(key_rows, query_tile, mask_ref, part, first, tile, region):
    scores = dot_nt(key_rows, query_tile)
    mask = mask_ref[part, :, first : first + tile]
    if part == 0:
        return scores + mask
    return jnp.concatenate([scores[:region], scores[region:] + mask], axis=0)


def attend(row, starts, mixed, bias, tables):
    seq_len = mixed.shape[0]
    width = mixed.shape[1] // 3
    pairs = width // LANES
    tile = seq_len // 4
    region = seq_len // 2
    scale = 1.0 / math.sqrt(HEAD_DIM)

    def kernel(
        row_ref,
        starts_ref,
        q_ref,
        k_ref,
        v_ref,
        qb_ref,
        kb_ref,
        vb_ref,
        keep_ref,
        lower_ref,
        upper_ref,
        out_ref,
        qo_ref,
        ko_ref,
        vo_ref,
        log_ref,
        mask_ref,
    ):
        @pl.when(pl.program_id(0) == 0)
        def masks():
            fill_masks(starts_ref, mask_ref, region)

        for number in range(4):
            place = slice(number * tile, (number + 1) * tile)
            origin = pl.ds(pl.multiple_of(jnp.bitwise_xor(row_ref[0], number) * tile, tile), tile)
            turns = (keep_ref[place, :], lower_ref[place, :], upper_ref[place, :])
            turned = turn(q_ref[origin, :] + qb_ref[4:5, :], *turns)
            qo_ref[place, :] = (turned.astype(BF16).astype(F32) * scale).astype(BF16)
            ko_ref[place, :] = turn(k_ref[origin, :] + kb_ref[5:6, :], *turns).astype(BF16)
            vo_ref[place, :] = (v_ref[origin, :] + vb_ref[6:7, :]).astype(BF16)
        value_columns = jnp.transpose(vo_ref[...])
        for number in range(4):
            part = number // 2
            seen = region * (part + 1)
            first = (number % 2) * tile
            outs = []
            for head in range(2):
                query_tile = jnp.where(
                    head_mask(tile, head),
                    qo_ref[number * tile : (number + 1) * tile, :],
                    jnp.zeros((), BF16),
                )
                scores = tile_scores(
                    ko_ref[:seen, :], query_tile, mask_ref, part, first, tile, region
                )
                peak = jnp.max(scores, axis=0, keepdims=True)
                powers = jnp.exp(scores - peak)
                total = jnp.sum(powers, axis=0, keepdims=True)
                log_ref[0, head : head + 1, number * tile : (number + 1) * tile] = peak + jnp.log(
                    total
                )
                mixed_values = dot_nn(
                    value_columns[head * HEAD_DIM : (head + 1) * HEAD_DIM, :seen],
                    powers.astype(BF16),
                )
                outs.append(mixed_values / total)
            place = pl.ds(pl.multiple_of(jnp.bitwise_xor(row_ref[0], number) * tile, tile), tile)
            out_ref[place, :] = jnp.transpose(jnp.concatenate(outs, axis=0)).astype(BF16)

    def columns(kind):
        return pl.BlockSpec((seq_len, LANES), lambda h: (0, kind * pairs + h))

    bias_block = pl.BlockSpec((8, LANES), lambda h: (0, h))
    table = pl.BlockSpec((seq_len, LANES), lambda h: (0, 0))
    low = jax.ShapeDtypeStruct((seq_len, width), BF16)
    return pl.pallas_call(
        kernel,
        grid=(pairs,),
        in_specs=[smem(), smem()]
        + [columns(0), columns(1), columns(2)]
        + [bias_block] * 3
        + [table] * 3,
        out_specs=[columns(0)] * 4 + [pl.BlockSpec((1, 8, seq_len), lambda h: (h, 0, 0))],
        out_shape=[low] * 4 + [jax.ShapeDtypeStruct((pairs, 8, seq_len), F32)],
        scratch_shapes=[pltpu.VMEM((2, region, region), F32)],
        compiler_params=params(40),
        cost_estimate=cost(
            3 * seq_len * seq_len * width * 4, 20 * seq_len * width, seq_len * seq_len * 2 * pairs
        ),
        name="attend",
    )(row, starts, mixed, mixed, mixed, bias, bias, bias, *tables)


def attend_back(row, starts, queries, keys, values, logs, outputs, grads, tables):
    seq_len, width = queries.shape
    pairs = width // LANES
    tile = seq_len // 4
    region = seq_len // 2
    scale = 1.0 / math.sqrt(HEAD_DIM)

    def kernel(
        row_ref,
        starts_ref,
        q_ref,
        k_ref,
        v_ref,
        log_ref,
        o_ref,
        g_ref,
        keep_ref,
        lower_ref,
        upper_ref,
        out_ref,
        sum_ref,
        mask_ref,
        dq_ref,
        dk_ref,
        dv_ref,
        low_ref,
        bias_ref,
    ):
        @pl.when((pl.program_id(0) == 0) & (pl.program_id(1) == 0))
        def masks():
            fill_masks(starts_ref, mask_ref, region)

        @pl.when(pl.program_id(1) == 0)
        def work():
            dk_ref[...] = jnp.zeros_like(dk_ref)
            dv_ref[...] = jnp.zeros_like(dv_ref)
            key_columns = jnp.transpose(k_ref[...])
            for number in range(4):
                part = number // 2
                seen = region * (part + 1)
                first = (number % 2) * tile
                span = slice(number * tile, (number + 1) * tile)
                origin = pl.ds(
                    pl.multiple_of(jnp.bitwise_xor(row_ref[0], number) * tile, tile), tile
                )
                grad_tile = g_ref[origin, :]
                products = jnp.transpose(grad_tile.astype(F32) * o_ref[origin, :].astype(F32))
                query_grads = []
                for head in range(2):
                    mine = head_mask(tile, head)
                    query_tile = jnp.where(mine, q_ref[span, :], jnp.zeros((), BF16))
                    head_grad = jnp.where(mine, grad_tile, jnp.zeros((), BF16))
                    inner = jnp.sum(
                        products[head * HEAD_DIM : (head + 1) * HEAD_DIM], axis=0, keepdims=True
                    )
                    scores = tile_scores(
                        k_ref[:seen, :], query_tile, mask_ref, part, first, tile, region
                    )
                    weights = jnp.exp(scores - log_ref[0, head : head + 1, span])
                    pulls = dot_nt(v_ref[:seen, :], head_grad)
                    score_grad = (weights * (pulls - inner)).astype(BF16)
                    dv_ref[:seen, :] += dot_nn(weights.astype(BF16), head_grad)
                    dk_ref[:seen, :] += dot_nn(score_grad, query_tile)
                    query_grads.append(
                        dot_nn(
                            key_columns[head * HEAD_DIM : (head + 1) * HEAD_DIM, :seen], score_grad
                        )
                    )
                dq_ref[span, :] = jnp.transpose(jnp.concatenate(query_grads, axis=0)) * scale
            bias_ref[...] = jnp.zeros_like(bias_ref)
            for number in range(4):
                span = slice(number * tile, (number + 1) * tile)
                origin = pl.ds(
                    pl.multiple_of(jnp.bitwise_xor(row_ref[0], number) * tile, tile), tile
                )
                turns = (keep_ref[span, :], -lower_ref[span, :], -upper_ref[span, :])
                parts = (
                    turn(dq_ref[span, :], *turns),
                    turn(dk_ref[span, :], *turns),
                    dv_ref[span, :],
                )
                for kind in range(3):
                    low = parts[kind].astype(BF16)
                    low_ref[kind, origin, :] = low
                    bias_ref[kind, 0:1, :] += jnp.sum(low.astype(F32), axis=0, keepdims=True)

        out_ref[...] = low_ref[pl.program_id(1)]
        sum_ref[...] = bias_ref[pl.program_id(1)]

    columns = pl.BlockSpec((seq_len, LANES), lambda h, j: (0, h))
    table = pl.BlockSpec((seq_len, LANES), lambda h, j: (0, 0))
    return pl.pallas_call(
        kernel,
        grid=(pairs, 3),
        in_specs=[smem(), smem()]
        + [columns] * 3
        + [pl.BlockSpec((1, 8, seq_len), lambda h, j: (h, 0, 0))]
        + [columns] * 2
        + [table] * 3,
        out_specs=[
            pl.BlockSpec((seq_len, LANES), lambda h, j: (0, j * pairs + h)),
            pl.BlockSpec((8, LANES), lambda h, j: (0, j * pairs + h)),
        ],
        out_shape=[
            jax.ShapeDtypeStruct((seq_len, 3 * width), BF16),
            jax.ShapeDtypeStruct((8, 3 * width), F32),
        ],
        scratch_shapes=[
            pltpu.VMEM((2, region, region), F32),
            pltpu.VMEM((seq_len, LANES), F32),
            pltpu.VMEM((seq_len, LANES), F32),
            pltpu.VMEM((seq_len, LANES), F32),
            pltpu.VMEM((3, seq_len, LANES), BF16),
            pltpu.VMEM((3, 8, LANES), F32),
        ],
        compiler_params=params(48),
        cost_estimate=cost(
            8 * seq_len * seq_len * width * 4, 20 * seq_len * width, seq_len * seq_len * 2 * pairs
        ),
        name="attend_back",
    )(row, starts, queries, keys, values, logs, outputs, grads, *tables)


def gate_up(rows_two, w_gate):
    tokens, width = rows_two.shape
    tiles = w_gate.shape[1] // (2 * LANES)

    def kernel(in_ref, w_ref, gate_ref, up_ref, hidden_ref):
        both = dot_nn(in_ref[...], w_ref[...])
        gate, up = both[:, :LANES], both[:, LANES:]
        gate_ref[...] = gate.astype(BF16)
        up_ref[...] = up.astype(BF16)
        hidden_ref[...] = (gate * jax.nn.sigmoid(gate) * up).astype(BF16)

    out = pl.BlockSpec((tokens, LANES), lambda i: (0, i))
    return pl.pallas_call(
        kernel,
        grid=(tiles,),
        in_specs=[whole(tokens, width), pl.BlockSpec((width, 2 * LANES), lambda i: (0, i))],
        out_specs=[out] * 3,
        out_shape=[jax.ShapeDtypeStruct((tokens, tiles * LANES), BF16)] * 3,
        compiler_params=params(40),
        cost_estimate=cost(
            2 * tokens * w_gate.size,
            2 * (rows_two.size + w_gate.size) + 6 * tokens * tiles * LANES,
            tokens * tiles * LANES,
        ),
        name="gate_up",
    )(rows_two, w_gate)


def gate_up_back(rows_grad, w_down, gate, up):
    tokens, width = rows_grad.shape
    hidden = w_down.shape[1]
    tile = 256

    def kernel(in_ref, w_ref, gate_ref, up_ref, out_ref):
        pulled = dot_nn(in_ref[...], w_ref[...])
        for number in range(hidden // LANES):
            span = slice(number * LANES, (number + 1) * LANES)
            grad = pulled[:, span]
            gate_part = gate_ref[:, span].astype(F32)
            up_part = up_ref[:, span].astype(F32)
            squash = jax.nn.sigmoid(gate_part)
            first = 2 * number * LANES
            out_ref[:, first : first + LANES] = (
                grad * up_part * squash * (1.0 + gate_part * (1.0 - squash))
            ).astype(BF16)
            out_ref[:, first + LANES : first + 2 * LANES] = (grad * gate_part * squash).astype(BF16)

    return pl.pallas_call(
        kernel,
        grid=(tokens // tile,),
        in_specs=[
            row_blocks(tile, width),
            whole(width, hidden),
            row_blocks(tile, hidden),
            row_blocks(tile, hidden),
        ],
        out_specs=row_blocks(tile, 2 * hidden),
        out_shape=jax.ShapeDtypeStruct((tokens, 2 * hidden), BF16),
        compiler_params=params(40),
        cost_estimate=cost(
            2 * tokens * w_down.size,
            2 * (rows_grad.size + w_down.size) + 8 * tokens * hidden,
            tokens * hidden,
        ),
        name="gate_up_back",
    )(rows_grad, w_down, gate, up)


def adam_update(master, first, second, gradient, keep, rate):
    correction = 1.0 - MOMENT_DECAY**STEP
    new_first = MOMENT_DECAY * first + (1.0 - MOMENT_DECAY) * gradient
    new_second = MOMENT_DECAY * second + (1.0 - MOMENT_DECAY) * gradient * gradient
    direction = new_first / correction / (jnp.sqrt(new_second / correction) + ADAM_EPSILON)
    new_master = master - rate * (direction + WEIGHT_DECAY * master)
    return (
        jnp.where(keep, new_master, master),
        jnp.where(keep, new_first, first),
        jnp.where(keep, new_second, second),
    )


def adam_call(name, keep, states, gradient, rate, grid, state_spec, grad_spec, pieces):
    def kernel(keep_ref, m_ref, f_ref, s_ref, g_ref, mo_ref, fo_ref, so_ref):
        live = keep_ref[LIVE + pl.program_id(0)] > 0
        for state_at, grad_at in pieces:
            results = adam_update(
                m_ref[state_at],
                f_ref[state_at],
                s_ref[state_at],
                g_ref[grad_at].astype(F32),
                live,
                rate,
            )
            mo_ref[state_at], fo_ref[state_at], so_ref[state_at] = results

    return pl.pallas_call(
        kernel,
        grid=grid,
        in_specs=[smem()] + [state_spec] * 3 + [grad_spec],
        out_specs=[state_spec] * 3,
        out_shape=[jax.ShapeDtypeStruct(states[0].shape, F32)] * 3,
        compiler_params=params(58),
        cost_estimate=cost(12 * states[0].size, 26 * states[0].size, states[0].size),
        name=name,
    )(keep, *states, gradient)


def adam_query(keep, states, gradient, rate):
    kinds, rows, width = states[0].shape
    block = rows // CAP
    return adam_call(
        "adam_query",
        keep,
        states,
        gradient,
        rate,
        (CAP,),
        pl.BlockSpec((kinds, block, width), lambda s: (0, s, 0)),
        pl.BlockSpec((1, block, kinds * width), lambda s: (s, 0, 0)),
        [
            ((kind,), (0, slice(None), slice(kind * width, (kind + 1) * width)))
            for kind in range(kinds)
        ],
    )


def adam_flat(name, keep, states, gradient, rate):
    rows, width = states[0].shape
    block = rows // CAP
    return adam_call(
        name,
        keep,
        states,
        gradient,
        rate,
        (CAP,),
        pl.BlockSpec((block, width), lambda s: (s, 0)),
        pl.BlockSpec((1, block, width), lambda s: (s, 0, 0)),
        [((slice(None), slice(None)), (0,))],
    )


def adam_gate(keep, states, gradient, rate):
    block, width = gradient.shape[1:]
    tiles = width // LANES
    pieces = [
        (
            (pl.ds(tile, block, stride=tiles), slice(None)),
            (0, slice(None), slice(tile * LANES, (tile + 1) * LANES)),
        )
        for tile in range(tiles)
    ]
    return adam_call(
        "adam_gate",
        keep,
        states,
        gradient,
        rate,
        (CAP,),
        pl.BlockSpec((block * tiles, LANES), lambda s: (s, 0)),
        pl.BlockSpec((1, block, width), lambda s: (s, 0, 0)),
        pieces,
    )


def matmul(left, right, left_dim, right_dim, dtype):
    return lax.dot_general(
        left, right, (((left_dim,), (right_dim,)), ((), ())), preferred_element_type=F32
    ).astype(dtype)


def flips(axis, reach):
    return [(index, index ^ reach) for index in range(lax.axis_size(axis))]


def x_pairs():
    return flips("row", 1)


def y_pairs():
    return flips("row", 2)


def share_rows(own):
    half = own.shape[0] // 2
    by_x = lax.ppermute(own, "row", x_pairs())
    by_y = lax.ppermute(own, "row", y_pairs())
    top = lax.ppermute(by_x[:half], "row", y_pairs())
    bottom = lax.ppermute(by_y[half:], "row", x_pairs())
    return jnp.concatenate([own, by_x, by_y, top, bottom], axis=0), by_x, by_y


def fold_rows(sums, top, bottom):
    half, width = top.shape

    def kernel(one_ref, two_ref, top_ref, bottom_ref, x_ref, y_ref):
        first = pl.program_id(0) == 0
        one, two = one_ref[...].astype(F32), two_ref[...].astype(F32)
        x_ref[...] = jnp.where(first, one + top_ref[...].astype(F32), one).astype(BF16)
        y_ref[...] = jnp.where(first, two, two + bottom_ref[...].astype(F32)).astype(BF16)

    out = jax.ShapeDtypeStruct((2 * half, width), BF16)
    return pl.pallas_call(
        kernel,
        grid=(2,),
        in_specs=[
            row_blocks(half, width, 2),
            row_blocks(half, width, 4),
            whole(half, width),
            whole(half, width),
        ],
        out_specs=[row_blocks(half, width)] * 2,
        out_shape=[out, out],
        compiler_params=params(),
        cost_estimate=cost(0, 10 * half * width),
        name="fold_rows",
    )(sums, sums, top, bottom)


def scatter_rows(sums, *others):
    rows = sums.shape[0] // 4
    half = rows // 2
    top = lax.ppermute(sums[3 * rows : 3 * rows + half], "row", y_pairs())
    bottom = lax.ppermute(sums[3 * rows + half :], "row", x_pairs())
    if others:
        top = after(top, *others)
    to_x, to_y = fold_rows(sums, top, bottom)
    return (
        (sums, lax.ppermute(to_x, "row", x_pairs()), lax.ppermute(to_y, "row", y_pairs())),
        to_x,
        to_y,
    )


def chip_moves(columns, moves):
    chips = columns // 2
    return [
        (2 * chip + core, 2 * (chip + moves[core]) + core)
        for chip in range(chips)
        for core in range(2)
        if 0 <= chip + moves[core] < chips
    ]


def swap_cores(values, columns):
    return lax.ppermute(values, "col", [(index, index ^ 1) for index in range(columns)])


def both_cores(values, columns):
    return values, swap_cores(values, columns)


def local_line(
    inputs,
    cotangent,
    image_starts,
    owners,
    query_master,
    query_first,
    query_second,
    output_master,
    output_first,
    output_second,
    gate_master,
    gate_first,
    gate_second,
    down_master,
    down_first,
    down_second,
    vector_master,
    vector_first,
    vector_second,
):
    columns = lax.axis_size("col")
    col_index = lax.axis_index("col")
    row_index = lax.axis_index("row")
    blocks = owners.shape[0]
    block_rows = D // blocks
    head_blocks = query_master.shape[2] // LANES
    codes, order, sorted_slots, head_slots, head_places = plan_blocks(
        owners, jnp.stack([col_index, row_index]), columns, head_blocks
    )
    uneven = codes[UNEVEN]

    inward = chip_moves(columns, (1, -1))
    outward = chip_moves(columns, (-1, 1))

    def spread_out(own, send_codes, keep_codes):
        partner = swap_cores(own, columns)
        sent = pick_blocks(send_codes, 0, 2, [own, partner])
        near = lax.ppermute(sent, "col", inward)

        def near_only():
            return pick_blocks(keep_codes, 4, 2, [own, partner, near])

        def farther(first, count):
            more = pick_blocks(codes, first, count, [own, partner])
            return pick_blocks(
                keep_codes, 4, 2, [own, partner, near, lax.ppermute(more, "col", outward)]
            )

        kept = lax.switch(
            uneven, [near_only, lambda: farther(UNEVEN + 1, 1), lambda: farther(2, 2)]
        )
        return sent, kept.reshape(2 * block_rows, own.shape[2])

    def gather(part):
        return lax.all_gather(part, "col", axis=0, tiled=True)

    def sum_up(gradient):
        own = lax.psum_scatter(gradient, "col", scatter_dimension=0, tiled=True)
        return own.reshape(2, block_rows, own.shape[1])

    def start_home(own):
        return own, lax.ppermute(own, "col", outward)

    def finish_home(own, near, codes):
        held = [own, near, swap_cores(own, columns), swap_cores(near, columns)]

        def near_only():
            return pick_blocks(codes, 6, CAP, held)

        def farther(more):
            far = lax.ppermute(more, "col", inward)
            return pick_blocks(codes, 6, CAP, held + [far, swap_cores(far, columns)])

        def one_farther():
            return farther(lax.dynamic_slice_in_dim(own, 1 - col_index % 2, 1, 0))

        return lax.switch(uneven, [near_only, one_farther, lambda: farther(own)])

    local_in = inputs[0]
    upstream = cotangent[0]
    row = row_index.reshape(1)
    tables = lane_tables(inputs.shape[1] * 4)
    rates = step_rates()

    query_slabs = [
        jnp.transpose(part, (1, 0, 2)) for part in (query_master, query_first, query_second)
    ]
    query_width = 3 * query_slabs[0].shape[2]
    sent_attention, attention_part = spread_out(
        pack_attention(query_slabs[0], output_master), codes, codes
    )
    plain_one = norm_one(after(order, sent_attention), local_in)
    rows_plain, *plain_parts = share_rows(plain_one)
    w_attention = gather(attention_part)
    w_query, w_output = w_attention[:, :query_width], w_attention[:, query_width:]
    vector_rows = jnp.pad(vector_master.T, ((0, 9), (0, 0))).astype(BF16)
    vector_blocks = jnp.transpose(vector_rows.reshape(16, CAP, block_rows), (1, 0, 2))
    vectors, bias = spread_vectors(
        sorted_slots, head_slots, gather(after(vector_blocks, attention_part, *plain_parts))
    )
    gate_states = [gate_lines(part) for part in (gate_master, gate_first, gate_second)]
    rows_grad = share_rows(order_grad(after(order, rows_plain), upstream))[0]
    rows_one = scale_rows(rows_plain, vectors)
    unused, gate_part = spread_out(
        pack_gate(gate_states[0], gate_master.shape[0]),
        after(codes, vectors),
        after(codes, rows_grad, rows_one),
    )
    w_gate = gather(gate_part)
    mixed = matmul(rows_one, w_query, 1, 0, F32)
    unused, down_part = spread_out(
        pack_flat("pack_down", down_master), after(codes, gate_part), after(codes, mixed)
    )
    w_down = gather(down_part)
    attended, queries, keys, values, logs = attend(
        after(row, down_part), image_starts, mixed, bias, tables
    )
    middle, normed_two = norm_two(
        order, local_in, scatter_rows(matmul(attended, w_output, 1, 1, BF16))[0], vectors
    )
    rows_two = share_rows(normed_two)[0]
    gate, up, hidden = gate_up(rows_two, w_gate)

    down_sums = matmul(rows_grad, hidden, 0, 0, BF16)
    down_own = sum_up(down_sums)
    gate_up_grad = gate_up_back(rows_grad, w_down, after(gate, down_sums), up)
    pulled_two = matmul(gate_up_grad, w_gate, 1, 1, BF16)
    gate_sums = matmul(rows_two, after(gate_up_grad, pulled_two), 0, 0, BF16)
    gate_own = sum_up(gate_sums)
    out_sums = matmul(after(hidden, gate_sums), w_down, 1, 1, BF16)
    middle_grad, low_middle, sums_two = norm_two_back(
        order, upstream, middle, scatter_rows(pulled_two)[0], after(vectors, gate_sums, out_sums)
    )
    rows_mid = share_rows(low_middle)[0]
    down_home = start_home(after(down_own, low_middle))
    attended_grad = matmul(rows_mid, w_output, 1, 0, BF16)
    output_sums = matmul(rows_mid, after(attended, attended_grad), 0, 0, BF16)
    output_own = sum_up(output_sums)
    out_partial, *out_parts = scatter_rows(after(out_sums, rows_mid), output_sums)
    mixed_grad, bias_sums = attend_back(
        after(row, *out_parts),
        image_starts,
        queries,
        keys,
        values,
        logs,
        attended,
        attended_grad,
        tables,
    )
    layer_out = finish_out(order, after(middle, mixed_grad), out_partial)
    pulled_one = matmul(after(mixed_grad, layer_out), w_query, 1, 1, BF16)
    query_sums = matmul(rows_one, after(mixed_grad, pulled_one, down_own), 0, 0, BF16)
    query_own = sum_up(query_sums)
    gate_home = start_home(after(gate_own, query_sums))
    new_down = adam_flat(
        "adam_down",
        codes,
        (down_master, down_first, down_second),
        finish_home(*down_home, after(codes, query_sums)),
        rates[3],
    )
    input_grad, sums_one = norm_one_back(
        order,
        local_in,
        middle_grad,
        scatter_rows(pulled_one)[0],
        after(vectors, new_down[0]),
    )
    vector_sums = place_vector_grads(head_places, sums_one, sums_two, bias_sums)
    for axis, reach in (("row", 1), ("row", 2), ("col", 1), ("col", 2), ("col", 4)):
        vector_sums = vector_sums + lax.ppermute(vector_sums, axis, flips(axis, reach))
    new_gate = [
        gate_unlines(part, gate_master.shape)
        for part in adam_gate(
            codes,
            gate_states,
            finish_home(gate_home[0], after(gate_home[1], input_grad), codes),
            rates[2],
        )
    ]
    output_home = start_home(after(output_own, input_grad))
    new_output = adam_flat(
        "adam_output",
        codes,
        (output_master, output_first, output_second),
        finish_home(output_home[0], after(output_home[1], new_gate[0]), codes),
        rates[1],
    )
    new_vector = [
        part.T
        for part in adam_vector(
            codes,
            [part.T for part in (vector_master, vector_first, vector_second)],
            vector_sums,
            rates[4],
        )
    ]
    query_own = after(query_own, new_output[0], new_vector[0])
    new_query = [
        jnp.transpose(part, (1, 0, 2))
        for part in adam_query(
            codes, query_slabs, finish_home(*start_home(query_own), codes), rates[0]
        )
    ]
    return (
        layer_out[None],
        input_grad[None],
        *new_query,
        *new_output,
        *new_gate,
        *new_down,
        *new_vector,
    )


def solution(mesh):
    one_hop_line = mesh.shape["row"] == 4 and mesh.shape["col"] == 8
    return jax.shard_map(
        local_line if one_hop_line else local,
        mesh=mesh,
        in_specs=(
            P("col", "row", None),
            P("col", "row", None),
            P("col", None),
            P(),
            P("col", None, "row"),
            P("col", None, "row"),
            P("col", None, "row"),
            P("col", "row"),
            P("col", "row"),
            P("col", "row"),
            P("col", None, "row"),
            P("col", None, "row"),
            P("col", None, "row"),
            P("col", "row"),
            P("col", "row"),
            P("col", "row"),
            P("col", None),
            P("col", None),
            P("col", None),
        ),
        out_specs=(
            P("col", "row", None),
            P("col", "row", None),
            P("col", None, "row"),
            P("col", None, "row"),
            P("col", None, "row"),
            P("col", "row"),
            P("col", "row"),
            P("col", "row"),
            P("col", None, "row"),
            P("col", None, "row"),
            P("col", None, "row"),
            P("col", "row"),
            P("col", "row"),
            P("col", "row"),
            P("col", None),
            P("col", None),
            P("col", None),
        ),
        check_vma=False,
    )
```
